32 devices in a mesh: group: 4 (over y, core), shard: 8 (over z, x).
Axes of the slice: x: 2, y: 2, z: 4, core: 2. Of those that a mesh axis runs over, the one named last changes fastest.
Arguments:
- tokens: bfloat16 [4096, 2048], P(('group', 'shard')), may hold values from -6 to 6
- lengths: int32 [32, 4], P(('group', 'shard')), may hold values from 1 to 96, as said below
- cotangent: bfloat16 [4096, 2048], P(('group', 'shard')), may hold values from -6 to 6
- norm1_gain: bfloat16 [2048], P('shard'), may hold values from 0.099609375 to 1.8984375
- gate_in: bfloat16 [2048, 2560], P('shard'), may hold values from -0.125 to 0.125
- linear_in: bfloat16 [2048, 2560], P('shard'), may hold values from -0.125 to 0.125
- conv_kernel: bfloat16 [4, 2560], P(None, 'shard'), may hold values from -3 to 3
- conv_bias: bfloat16 [2560], P('shard'), may hold values from -3 to 3
- rate_weight: bfloat16 [2560, 160], P('shard'), may hold values from -0.5 to 0.5
- rate_bias: bfloat16 [2560], P('shard'), may hold values from -4 to 4
- input_weight: bfloat16 [2560, 160], P('shard'), may hold values from -0.5 to 0.5
- input_bias: bfloat16 [2560], P('shard'), may hold values from -4 to 4
- decay_param: bfloat16 [2560], P('shard'), may hold values from 4 to 8
- out_proj: bfloat16 [2560, 2048], P('shard'), may hold values from -0.25 to 0.25
- norm2_gain: bfloat16 [2048], P('shard'), may hold values from 0.099609375 to 1.8984375
- mlp_gate: bfloat16 [2048, 6144], P('shard'), may hold values from -0.125 to 0.125
- mlp_up: bfloat16 [2048, 6144], P('shard'), may hold values from -0.125 to 0.125
- mlp_down: bfloat16 [6144, 2048], P('shard'), may hold values from -0.109375 to 0.109375
Outputs:
- mixed: bfloat16 [4096, 2048], P(('group', 'shard'))
- grad_tokens: bfloat16 [4096, 2048], P(('group', 'shard'))
- grad_norm1_gain: float32 [2048], P('shard')
- grad_gate_in: float32 [2048, 2560], P('shard')
- grad_linear_in: float32 [2048, 2560], P('shard')
- grad_conv_kernel: float32 [4, 2560], P(None, 'shard')
- grad_conv_bias: float32 [2560], P('shard')
- grad_rate_weight: float32 [2560, 160], P('shard')
- grad_rate_bias: float32 [2560], P('shard')
- grad_input_weight: float32 [2560, 160], P('shard')
- grad_input_bias: float32 [2560], P('shard')
- grad_decay: float32 [2560], P('shard')
- grad_out_proj: float32 [2560, 2048], P('shard')
- grad_norm2_gain: float32 [2048], P('shard')
- grad_mlp_gate: float32 [2048, 6144], P('shard')
- grad_mlp_up: float32 [2048, 6144], P('shard')
- grad_mlp_down: float32 [6144, 2048], P('shard')
The draws below stay inside these ranges and needn't reach their ends.
Inputs may be any that keep to these rules, and one draw needn't show every extreme that they name: Each row belongs to one device; its first 3 entries are the lengths of that device's sequences in order, one of them exactly 96, and its last entry is its padding, 1 to 16 rows; every row sums to 128.
All inputs are finite; a program needn't handle non-finite values.
Results may differ from the reference program's by a relative error of at most 0.018.
Values may be sent and summed in bfloat16 or wider, within the bound.
A program may use at most 448 MiB of HBM per device.

```python
import jax
import jax.numpy as jnp
from jax import lax

D = 2048
R = 2560
F = 6144
BLOCK = 160
CAP = 128
MOST = 96
TOKENS = 4096
N_GROUP = 4
N_SHARD = 8


def device_lengths(key):
    first_key, second_key, third_key = jax.random.split(key, 3)
    padding = jax.random.randint(first_key, (), 1, CAP // 8 + 1).astype(jnp.int32)
    remain = (CAP - MOST - padding).astype(jnp.int32)
    first_len = jax.random.randint(second_key, (), 1, remain).astype(jnp.int32)
    sequences = jnp.stack([jnp.int32(MOST), first_len, remain - first_len]).astype(jnp.int32)
    offset = jax.random.randint(third_key, (), 0, 3).astype(jnp.int32)
    sequences = jnp.roll(sequences, offset)
    return jnp.concatenate([sequences, padding[None]]).astype(jnp.int32)


def draw_lengths(key, part):
    row_keys = jax.random.split(jax.random.fold_in(key, 17), N_GROUP * N_SHARD)
    return jax.vmap(device_lengths)(row_keys).astype(jnp.int32)


def raised(result, key, source, target, blocks, factor):
    def block_of(axis_at):
        return (jnp.arange(result.shape[axis_at]) // (result.shape[axis_at] // blocks)).reshape((-1,) + (1,) * (result.ndim - 1 - axis_at))

    near = jax.random.permutation(key, blocks)[block_of(target)]
    far = (block_of(target) + blocks // 2) % blocks
    return jnp.where((block_of(source) == near) | (block_of(source) == far), factor * result, result)


def block_scale(own_key, dims, pieces, smallest, high):
    factor_of = 1.0
    for dim, shards_of in pieces:
        draws = jax.random.uniform(jax.random.fold_in(jax.random.fold_in(own_key, 6), dim), (shards_of,), jnp.float32, smallest / len(pieces), high / len(pieces))
        factor_of = factor_of * jnp.repeat(jnp.exp(draws), dims[dim] // shards_of).reshape((-1,) + (1,) * (len(dims) - 1 - dim))
    return factor_of


def scatter_about(rng, dims, scale, bound, shards=(), kind=jnp.bfloat16):
    loudness = block_scale(rng, dims, shards, -0.22, 0.18) if shards else 1.0
    values = jax.random.normal(rng, dims, jnp.float32) * scale * loudness
    return jnp.minimum(jnp.maximum(values, -bound), bound).astype(kind)


def noise_with(own_key, dims, spread, reach, cuts, heavy, kind=jnp.bfloat16):
    entries = spread * jax.random.normal(own_key, dims, jnp.float32)
    if cuts:
        entries = entries * block_scale(own_key, dims, cuts, -0.22, 0.18)
    return jnp.clip(raised(entries, jax.random.fold_in(own_key, 3), *heavy), -reach, reach).astype(kind)


def setup_inputs(seed: int = 0) -> dict:
    seeds = jax.random.split(jax.random.key(seed), 19)
    tokens = scatter_about(seeds[0], (TOKENS, D), 1.0, 6.0, ((0, 32),))
    lengths = draw_lengths(jax.random.fold_in(seeds[18], 71), 0)
    cotangent = noise_with(seeds[2], (TOKENS, D), 1.0, 6.0, ((0, 32),), (0, 1, 32, 2.75))
    norm1_gain = jnp.clip(1.0 + 0.18 * jax.random.normal(seeds[3], (D,), jnp.float32), 0.099609375, 1.8984375).astype(jnp.bfloat16)
    gate_in = scatter_about(seeds[4], (D, R), D ** -0.5, 0.125, ((0, 8),))
    linear_in = scatter_about(seeds[5], (D, R), D ** -0.5, 0.125, ((0, 8),))
    conv_kernel = scatter_about(seeds[6], (4, R), 4 ** -0.5, 3.0, ((1, 8),))
    conv_bias = scatter_about(seeds[7], (R,), 0.5, 3.0, ((0, 8),))
    rate_weight = scatter_about(seeds[8], (R, BLOCK), BLOCK ** -0.5, 0.5, ((0, 8),))
    rate_bias = scatter_about(seeds[9], (R,), 1.0, 4.0, ((0, 8),))
    input_weight = scatter_about(seeds[10], (R, BLOCK), BLOCK ** -0.5, 0.5, ((0, 8),))
    input_bias = scatter_about(seeds[11], (R,), 1.0, 4.0, ((0, 8),))
    decay_param = jnp.clip(4.0 + 4.0 * jax.random.uniform(seeds[12], (R,), jnp.float32) ** block_scale(seeds[12], (R,), ((0, 8),), -0.2, 0.2), 4.0, 8.0).astype(jnp.bfloat16)
    out_proj = scatter_about(seeds[13], (R, D), (R // 4) ** -0.5, 0.25, ((0, 8),))
    norm2_gain = jnp.clip(1.0 + 0.18 * jax.random.normal(seeds[14], (D,), jnp.float32), 0.099609375, 1.8984375).astype(jnp.bfloat16)
    mlp_gate = scatter_about(seeds[15], (D, F), D ** -0.5, 0.125, ((0, 8),))
    mlp_up = scatter_about(seeds[16], (D, F), D ** -0.5, 0.125, ((0, 8),))
    mlp_down = scatter_about(seeds[17], (F, D), (F // 2) ** -0.5, 0.109375, ((0, 8),))
    return {"tokens": tokens, "lengths": lengths, "cotangent": cotangent, "norm1_gain": norm1_gain, "gate_in": gate_in, "linear_in": linear_in, "conv_kernel": conv_kernel, "conv_bias": conv_bias, "rate_weight": rate_weight, "rate_bias": rate_bias, "input_weight": input_weight, "input_bias": input_bias, "decay_param": decay_param, "out_proj": out_proj, "norm2_gain": norm2_gain, "mlp_gate": mlp_gate, "mlp_up": mlp_up, "mlp_down": mlp_down}


@jax.custom_vjp
def low(v):
    return lax.optimization_barrier(v.astype(jnp.bfloat16)).astype(jnp.float32)

@jax.custom_vjp
def low_back(v):
    return v

def low_keep(v):
    return (low(v), None)

def low_pass(kept, grad):
    return (grad,)

def back_keep(v):
    return (v, None)

def back_low(kept, grad):
    return (low(grad),)
low.defvjp(low_keep, low_pass)
low_back.defvjp(back_keep, back_low)
RATE_SCALE = 8.0
EPSILON = 1e-06

def matmul(left, right):
    return jnp.dot(left, right, precision=lax.Precision.HIGHEST, preferred_element_type=jnp.float32)

def layout(counts, row_count):
    run_ends = jnp.cumsum(counts).astype(jnp.int32)
    positions = jnp.arange(row_count, dtype=jnp.int32)
    segment_ids = lax.optimization_barrier(jnp.sum((positions[:, None] >= run_ends[None, :-1]).astype(jnp.int32), axis=1)).astype(jnp.int32)
    live_rows = (positions < run_ends[-2]).astype(jnp.float32)
    return (segment_ids, live_rows)

def earlier_ids(segment_ids, offset):
    filler = jnp.full((offset,), -1, dtype=jnp.int32)
    return jnp.concatenate([filler, segment_ids[:-offset].astype(jnp.int32)]).astype(jnp.int32)

def normalize(values, gain_vec):
    scale = lax.rsqrt(lax.optimization_barrier(jnp.mean(values * values, axis=1, keepdims=True)) + EPSILON)
    return values * scale * gain_vec

def convolve(linear_out, kernel, shift_vec, segment_ids):
    summed = linear_out * kernel[0] + shift_vec
    for offset in range(1, kernel.shape[0]):
        shifted = jnp.concatenate([jnp.zeros((offset, linear_out.shape[1]), linear_out.dtype), linear_out[:-offset]], axis=0)
        same_seq = (earlier_ids(segment_ids, offset) == segment_ids).astype(linear_out.dtype)
        summed = summed + kernel[offset] * shifted * same_seq[:, None]
    return summed

def blockwise(values, weight):
    row_count = values.shape[0]
    size = weight.shape[1]
    heads = weight.shape[0] // size
    parts = values.reshape(row_count, heads, size)
    table = weight.reshape(heads, size, size)
    return jnp.einsum('thj,hjk->thk', parts, table, precision=lax.Precision.HIGHEST).reshape(row_count, heads * size)

def combine_pairs(earlier_pair, later_pair):
    return (earlier_pair[0] * later_pair[0], later_pair[0] * earlier_pair[1] + later_pair[1])

def recurrence(rate_pre, input_pre, inflow, decay_vec, segment_ids):
    rate_gate = jax.nn.sigmoid(rate_pre)
    opened = jax.nn.sigmoid(input_pre)
    log_keep = -RATE_SCALE * rate_gate * jax.nn.softplus(-decay_vec)
    factor = jnp.exp(log_keep)
    weight_in = jnp.sqrt(-jnp.expm1(2.0 * log_keep))
    same_run = (earlier_ids(segment_ids, 1) == segment_ids).astype(factor.dtype)
    carried, states = lax.associative_scan(combine_pairs, (factor * same_run[:, None], weight_in * opened * inflow), axis=0)
    return states

def block_forward(rows_in, counts, weights):
    gain_first, gate_w, linear_w, kernel, kernel_shift, rate_w, rate_shift, input_w, input_shift, decay_vec, out_w, gain_second, mlp_gate_w, mlp_up_w, mlp_down_w = weights
    segment_ids, live_rows = layout(counts, rows_in.shape[0])
    live_col = live_rows[:, None]
    masked_in = rows_in * live_col
    normed_low = low(normalize(masked_in, gain_first))
    gate_pre = low_back(matmul(normed_low, gate_w))
    linear_out = low_back(matmul(normed_low, linear_w))
    conv_out = convolve(linear_out, kernel, kernel_shift, segment_ids)
    conv_low = low(conv_out)
    rate_pre = low_back(blockwise(conv_low, rate_w) + rate_shift)
    input_pre = low_back(blockwise(conv_low, input_w) + input_shift)
    states = recurrence(rate_pre, input_pre, conv_out, decay_vec, segment_ids)
    merged_low = low(jax.nn.gelu(gate_pre) * states)
    middle = masked_in + low_back(matmul(merged_low, out_w))
    normed_two = low(normalize(middle, gain_second))
    gate_mlp = low_back(matmul(normed_two, mlp_gate_w))
    up_mlp = low_back(matmul(normed_two, mlp_up_w))
    hidden_low = low(jax.nn.gelu(gate_mlp) * up_mlp)
    return (middle + low_back(matmul(hidden_low, mlp_down_w))) * live_col

def reference(tokens, lengths, cotangent, norm1_gain, gate_in, linear_in, conv_kernel, conv_bias, rate_weight, rate_bias, input_weight, input_bias, decay_param, out_proj, norm2_gain, mlp_gate, mlp_up, mlp_down):
    params = tuple((entry.astype(jnp.float32) for entry in (norm1_gain, gate_in, linear_in, conv_kernel, conv_bias, rate_weight, rate_bias, input_weight, input_bias, decay_param, out_proj, norm2_gain, mlp_gate, mlp_up, mlp_down)))
    blocks = tokens.astype(jnp.float32).reshape(-1, CAP, D)
    seed_rows = cotangent.astype(jnp.float32).reshape(-1, CAP, D)

    def forward(inputs, weights):

        def single(entry_pair):
            return block_forward(entry_pair[0], entry_pair[1], weights)
        return lax.map(jax.checkpoint(single), (inputs, lengths))
    mixed_out, backward = jax.vjp(forward, blocks, params)
    grad_in, grad_list = backward(seed_rows)
    grad_first, grad_gate, grad_linear, grad_kernel, grad_kernel_shift, grad_rate, grad_rate_shift, grad_input, grad_input_shift, grad_decay, grad_out, grad_second, grad_mlp_gate, grad_mlp_up, grad_mlp_down = grad_list
    return (mixed_out.reshape(-1, D).astype(jnp.bfloat16), grad_in.reshape(-1, D).astype(jnp.bfloat16), grad_first, grad_gate, grad_linear, grad_kernel, grad_kernel_shift, grad_rate, grad_rate_shift, grad_input, grad_input_shift, grad_decay, grad_out, grad_second, grad_mlp_gate, grad_mlp_up, grad_mlp_down)
```

```python
from functools import partial

import jax
import jax.numpy as jnp
from jax import lax
from jax.experimental import pallas as pl
from jax.experimental.pallas import tpu as pltpu
from jax.sharding import PartitionSpec as P

FAST_MESH = (4, 8)
RATE_SCALE = 8.0
EPSILON = 1e-06
F32 = jnp.float32
BF16 = jnp.bfloat16
GELU_C = 0.7978845608028654
GELU_K = 0.044715


def positions_in_run(counts, row_count):
    first = counts[0]
    second = first + counts[1]
    third = second + counts[2]
    rows = lax.broadcasted_iota(jnp.int32, (row_count, 1), 0)
    start = jnp.where(rows >= first, first, 0)
    start = jnp.where(rows >= second, second, start)
    start = jnp.where(rows >= third, third, start)
    return rows - start, (rows < third).astype(F32)


def gelu_parts(x):
    t = jnp.tanh(GELU_C * (x + GELU_K * x * x * x))
    value = 0.5 * x * (1.0 + t)
    slope = 0.5 * (1.0 + t) + 0.5 * x * (1.0 - t * t) * GELU_C * (1.0 + 3.0 * GELU_K * x * x)
    return value, slope


def gelu_value(x):
    return 0.5 * x * (1.0 + jnp.tanh(GELU_C * (x + GELU_K * x * x * x)))


def sigmoid(x):
    return 0.5 * (1.0 + jnp.tanh(0.5 * x))


def one_less_exp(z):
    series = 1.0 - z * (1.0 / 7.0)
    for k in (6.0, 5.0, 4.0, 3.0, 2.0):
        series = 1.0 - z * (1.0 / k) * series
    return jnp.where(z < 0.35, z * series, 1.0 - jnp.exp(-z))


def softplus_neg(x):
    return jnp.maximum(-x, 0.0) + jnp.log1p(jnp.exp(-jnp.abs(x)))


def mm(a, b):
    return jnp.dot(a, b, preferred_element_type=F32)


def mm_nt(a, b):
    return lax.dot_general(a, b, (((1,), (1,)), ((), ())), preferred_element_type=F32)


def mm_tn(a, b):
    return lax.dot_general(a, b, (((0,), (0,)), ((), ())), preferred_element_type=F32)


def roll_rows(x, n):
    return pltpu.roll(x, n % x.shape[0], 0)


def conv_rows(linear, kernel, bias, masks):
    out = linear * kernel[0:1] + bias
    for k in range(1, 4):
        out = out + kernel[k : k + 1] * (roll_rows(linear, k) * masks[k - 1])
    return out


def decay_terms(rate_pre, decay):
    rate = sigmoid(rate_pre)
    keep = RATE_SCALE * rate * softplus_neg(decay)
    return rate, jnp.exp(-keep), jnp.sqrt(one_less_exp(2.0 * keep))


def mixer_forward_kernel(pos_ref, gate_ref, linear_ref, ck_ref, vec_ref, rw_ref, iw_ref,
                         merged_ref, rate_ref, input_ref, state_ref):
    pos = pos_ref[...]
    masks = [(pos >= k).astype(F32) for k in (1, 2, 3)]
    linear = linear_ref[...]
    conv = conv_rows(linear, ck_ref[...], vec_ref[0:1], masks)
    low = conv.astype(BF16)
    rate_pre = mm(low, rw_ref[...]) + vec_ref[1:2]
    input_pre = mm(low, iw_ref[...]) + vec_ref[2:3]
    _, a, weight_in = decay_terms(rate_pre, vec_ref[3:4])
    mult = a * masks[0]
    total = weight_in * sigmoid(input_pre) * conv
    step = 1
    rows = total.shape[0]
    while step < rows:
        total = total + mult * roll_rows(total, step)
        if 2 * step < rows:
            mult = mult * roll_rows(mult, step)
        step *= 2
    rate_ref[...] = rate_pre
    input_ref[...] = input_pre
    state_ref[...] = total
    merged_ref[...] = (gelu_value(gate_ref[...]) * total).astype(BF16)


def mixer_backward_kernel(pos_ref, gm_ref, gate_ref, linear_ref, rate_ref, input_ref, state_ref,
                          ck_ref, vec_ref, rw_ref, iw_ref,
                          gg_ref, gl_ref, small_ref, rate_out_ref, input_out_ref, tr_ref, ti_ref):
    @pl.when(pl.program_id(0) == 0)
    def _():
        small_ref[...] = jnp.zeros_like(small_ref)
        tr_ref[...] = jnp.zeros_like(tr_ref)
        ti_ref[...] = jnp.zeros_like(ti_ref)

    pos = pos_ref[...]
    rows = pos.shape[0]
    masks = [(pos >= k).astype(F32) for k in (1, 2, 3)]
    index = lax.broadcasted_iota(jnp.int32, pos.shape, 0)
    later = [
        jnp.where(index < rows - k, roll_rows(masks[k - 1], -k), 0.0) for k in (1, 2, 3)
    ]
    linear = linear_ref[...]
    kernel = ck_ref[...]
    conv = conv_rows(linear, kernel, vec_ref[0:1], masks)
    low = conv.astype(BF16)
    input_gate = sigmoid(input_ref[...])
    decay = vec_ref[3:4]
    rate, a, weight_in = decay_terms(rate_ref[...], decay)
    state = state_ref[...]
    g_merged = gm_ref[...]
    act, slope = gelu_parts(gate_ref[...])
    gg_ref[...] = (g_merged * state * slope).astype(BF16)
    lam = g_merged * act
    mult = roll_rows(a, -1) * later[0]
    step = 1
    while step < rows:
        lam = lam + mult * roll_rows(lam, -step)
        if 2 * step < rows:
            mult = mult * roll_rows(mult, -step)
        step *= 2
    g_a = lam * (roll_rows(state, 1) * masks[0])
    opened = input_gate * conv
    g_keep = g_a * a - lam * opened * (a * a) / weight_in
    slow = RATE_SCALE * rate
    g_rate = (g_keep * (-RATE_SCALE * softplus_neg(decay)) * (rate * (1.0 - rate))).astype(BF16)
    g_decay = g_keep * slow * sigmoid(-decay)
    flow = lam * weight_in
    g_inp = (flow * conv * (input_gate * (1.0 - input_gate))).astype(BF16)
    g_conv = flow * input_gate + mm_nt(g_rate, rw_ref[...]) + mm_nt(g_inp, iw_ref[...])
    g_linear = g_conv * kernel[0:1]
    sums = [jnp.sum(g_conv * linear, axis=0, keepdims=True)]
    for k in (1, 2, 3):
        g_linear = g_linear + kernel[k : k + 1] * (roll_rows(g_conv, -k) * later[k - 1])
        sums.append(jnp.sum(g_conv * (roll_rows(linear, k) * masks[k - 1]), axis=0, keepdims=True))
    gl_ref[...] = g_linear.astype(BF16)
    sums.append(jnp.sum(g_conv, axis=0, keepdims=True))
    sums.append(jnp.sum(g_rate.astype(F32), axis=0, keepdims=True))
    sums.append(jnp.sum(g_inp.astype(F32), axis=0, keepdims=True))
    sums.append(jnp.sum(g_decay, axis=0, keepdims=True))
    small_ref[...] += jnp.concatenate(sums, axis=0)
    tr_ref[...] += mm_tn(low, g_rate)
    ti_ref[...] += mm_tn(low, g_inp)

    @pl.when(pl.program_id(0) == pl.num_programs(0) - 1)
    def _():
        size = rate_out_ref.shape[1]
        for h in range(rate_out_ref.shape[0] // size):
            part = slice(h * size, (h + 1) * size)
            rate_out_ref[part] = tr_ref[part, part].astype(BF16)
            input_out_ref[part] = ti_ref[part, part].astype(BF16)


def block_diagonal(weight):
    size = weight.shape[1]
    heads = weight.shape[0] // size
    parts = []
    for h in range(heads):
        parts.append(
            jnp.pad(weight[h * size : (h + 1) * size], ((0, 0), (h * size, (heads - 1 - h) * size)))
        )
    return jnp.concatenate(parts, axis=0)


def per_device_split(
    tokens, lengths, cotangent, norm1_gain, gate_in, linear_in, conv_kernel, conv_bias, rate_weight,
    rate_bias, input_weight, input_bias, decay_param, out_proj, norm2_gain, mlp_gate, mlp_up, mlp_down,
):
    rows, width = tokens.shape
    n_shard = lax.axis_size("shard")
    size = rate_weight.shape[1]
    chans = rate_weight.shape[0]
    total_rows = rows * n_shard

    def gather(x):
        return lax.all_gather(x, "shard", axis=0, tiled=True)

    def scatter(x):
        return lax.psum_scatter(x.astype(BF16), "shard", scatter_dimension=0, tiled=True).astype(F32)

    def columns(w):
        return lax.all_to_all(w, "shard", split_axis=1, concat_axis=0, tiled=True)

    pos, live = positions_in_run(lengths[0], rows)
    gains = lax.all_gather(jnp.stack([norm1_gain, norm2_gain]), "shard", axis=1, tiled=True).astype(F32)
    masked = tokens.astype(F32) * live
    scale1 = lax.rsqrt(jnp.mean(masked * masked, axis=1, keepdims=True) + EPSILON)
    normed = (masked * scale1 * gains[0:1]).astype(BF16)
    sent = jnp.concatenate([normed, jnp.broadcast_to(pos.astype(BF16), (rows, 128))], axis=1)
    got = gather(sent)
    normed_all = got[:, :width]
    pos_all = got[:, width : width + 1].astype(jnp.int32)
    gate_w, linear_w = columns(gate_in), columns(linear_in)
    mg_w, mu_w = columns(mlp_gate), columns(mlp_up)
    gate_pre = mm(normed_all, gate_w)
    linear_pre = mm(normed_all, linear_w)
    vec = jnp.stack([conv_bias, rate_bias, input_bias, decay_param]).astype(F32)
    ck = conv_kernel.astype(F32)
    rate_bd, input_bd = block_diagonal(rate_weight), block_diagonal(input_weight)
    row_spec = pl.BlockSpec((rows, chans), lambda i: (i, 0))
    pos_spec = pl.BlockSpec((rows, 1), lambda i: (i, 0))

    def whole(a):
        return pl.BlockSpec(a.shape, lambda i: (0,) * a.ndim)

    f_shape = jax.ShapeDtypeStruct((total_rows, chans), F32)
    b_shape = jax.ShapeDtypeStruct((total_rows, chans), BF16)
    merged, rate_pre, input_pre, state = pl.pallas_call(
        mixer_forward_kernel,
        grid=(n_shard,),
        in_specs=[pos_spec, row_spec, row_spec, whole(ck), whole(vec), whole(rate_bd), whole(input_bd)],
        out_specs=[row_spec] * 4,
        out_shape=[b_shape, f_shape, f_shape, f_shape],
        compiler_params=pltpu.CompilerParams(vmem_limit_bytes=32 * 2**20),
        name="mixer_forward",
    )(pos_all, gate_pre, linear_pre, ck, vec, rate_bd, input_bd)
    middle = masked + scatter(mm(merged, out_proj))
    scale2 = lax.rsqrt(jnp.mean(middle * middle, axis=1, keepdims=True) + EPSILON)
    normed_two = gather((middle * scale2 * gains[1:2]).astype(BF16))
    g_out = cotangent.astype(F32) * live
    g_low = gather(g_out.astype(BF16))
    gate_mlp = mm(normed_two, mg_w)
    up_mlp = mm(normed_two, mu_w)
    act, slope = gelu_parts(gate_mlp)
    hidden = (act * up_mlp).astype(BF16)
    mixed = ((middle + scatter(mm(hidden, mlp_down))) * live).astype(BF16)
    term_down = mm_tn(hidden, g_low).astype(BF16)
    g_hidden = mm_nt(g_low, mlp_down)
    g_gate_mlp = (g_hidden * up_mlp * slope).astype(BF16)
    g_up = (g_hidden * act).astype(BF16)
    term_mg = mm_tn(normed_two, g_gate_mlp).astype(BF16)
    term_mu = mm_tn(normed_two, g_up).astype(BF16)
    g_normed_two = scatter(mm_nt(g_gate_mlp, mg_w) + mm_nt(g_up, mu_w))
    e2 = g_normed_two * gains[1:2]
    g_middle = (
        g_out + scale2 * e2
        - middle * (scale2 * scale2 * scale2) * jnp.mean(middle * e2, axis=1, keepdims=True)
    )
    gain2_term = jnp.sum(g_normed_two * middle * scale2, axis=0)
    g_mix = gather(g_middle.astype(BF16))
    term_out = mm_tn(merged, g_mix).astype(BF16)
    g_merged = mm_nt(g_mix, out_proj)
    small_shape = jax.ShapeDtypeStruct((8, chans), F32)
    bd_shape = jax.ShapeDtypeStruct((chans, size), BF16)
    g_gate, g_linear, small, tr, ti = pl.pallas_call(
        mixer_backward_kernel,
        grid=(n_shard,),
        in_specs=[pos_spec] + [row_spec] * 6 + [whole(ck), whole(vec), whole(rate_bd), whole(input_bd)],
        out_specs=[row_spec] * 2 + [whole(small_shape), whole(bd_shape), whole(bd_shape)],
        out_shape=[b_shape, b_shape, small_shape, bd_shape, bd_shape],
        scratch_shapes=[pltpu.VMEM((chans, chans), F32)] * 2,
        compiler_params=pltpu.CompilerParams(vmem_limit_bytes=32 * 2**20),
        name="mixer_backward",
    )(pos_all, g_merged, gate_pre, linear_pre, rate_pre, input_pre, state, ck, vec, rate_bd, input_bd)
    term_gi = mm_tn(normed_all, g_gate).astype(BF16)
    term_li = mm_tn(normed_all, g_linear).astype(BF16)
    g_normed = scatter(mm_nt(g_gate, gate_w) + mm_nt(g_linear, linear_w))
    e1 = g_normed * gains[0:1]
    g_masked = (
        scale1 * e1
        - masked * (scale1 * scale1 * scale1) * jnp.mean(masked * e1, axis=1, keepdims=True)
    )
    gain1_term = jnp.sum(g_normed * masked * scale1, axis=0)
    grad_tokens = ((g_middle + g_masked) * live).astype(BF16)

    def back_columns(t):
        return lax.all_to_all(t, "shard", split_axis=0, concat_axis=1, tiled=True)

    gain_terms = lax.psum_scatter(
        jnp.stack([gain1_term, gain2_term]).astype(BF16), "shard", scatter_dimension=1, tiled=True
    )
    sums = lax.psum(
        (gain_terms, back_columns(term_gi), back_columns(term_li), small.astype(BF16), tr, ti, term_out,
         back_columns(term_mg), back_columns(term_mu), term_down), "group",
    )
    gain_s, gi_s, li_s, small_s, tr_s, ti_s, out_s, mg_s, mu_s, down_s = [s.astype(F32) for s in sums]
    return (
        mixed, grad_tokens, gain_s[0], gi_s, li_s, small_s[0:4], small_s[4], tr_s, small_s[5], ti_s,
        small_s[6], small_s[7], out_s, gain_s[1], mg_s, mu_s, down_s,
    )


def as_sent(shard):
    return jax.tree.map(lambda a: a.astype(jnp.bfloat16) if a.dtype == jnp.float32 else a, shard)


def layout(counts, row_count):
    first = counts[0]
    second = first + counts[1]
    run_ends = jnp.stack([first, second, second + counts[2], second + counts[2] + counts[3]])
    positions = jnp.arange(row_count, dtype=jnp.int32)
    segment_ids = jnp.sum((positions[:, None] >= run_ends[None, :-1]).astype(jnp.int32), axis=1)
    live_rows = (positions < run_ends[-2]).astype(jnp.float32)
    return (segment_ids, live_rows)


def earlier_ids(segment_ids, offset):
    filler = jnp.full((offset,), -1, dtype=jnp.int32)
    return jnp.concatenate([filler, segment_ids[:-offset]])


def normalize(values, gain_vec):
    scale = lax.rsqrt(jnp.mean(values * values, axis=1, keepdims=True) + EPSILON)
    return values * scale * gain_vec


def convolve(linear_out, kernel, shift_vec, segment_ids):
    summed = linear_out * kernel[0] + shift_vec
    for offset in range(1, kernel.shape[0]):
        shifted = jnp.concatenate(
            [jnp.zeros((offset, linear_out.shape[1]), linear_out.dtype), linear_out[:-offset]],
            axis=0,
        )
        same_seq = (earlier_ids(segment_ids, offset) == segment_ids).astype(linear_out.dtype)
        summed = summed + kernel[offset] * shifted * same_seq[:, None]
    return summed


def combine_pairs(earlier_pair, later_pair):
    return (earlier_pair[0] * later_pair[0], later_pair[0] * earlier_pair[1] + later_pair[1])


def recurrence(rate_pre, input_pre, inflow, decay_vec, segment_ids):
    rate_gate = jax.nn.sigmoid(rate_pre)
    opened = jax.nn.sigmoid(input_pre)
    log_keep = -RATE_SCALE * rate_gate * jax.nn.softplus(-decay_vec)
    factor = jnp.exp(log_keep)
    weight_in = jnp.sqrt(-jnp.expm1(2.0 * log_keep))
    same_run = (earlier_ids(segment_ids, 1) == segment_ids).astype(factor.dtype)
    carried, states = lax.associative_scan(
        combine_pairs, (factor * same_run[:, None], weight_in * opened * inflow), axis=0
    )
    return states


def gated_gelu(gate_vals, up_vals):
    return jax.nn.gelu(gate_vals) * up_vals


def product(left, right):
    return jnp.dot(left, right, preferred_element_type=jnp.float32)


def contract(left, right):
    return jnp.einsum("ti,tj->ij", left, right, preferred_element_type=jnp.float32)


def back_dot(grad_vals, weight):
    return jnp.einsum("tj,ij->ti", grad_vals, weight, preferred_element_type=jnp.float32)


def blocked(values, weight):
    row_count = values.shape[0]
    size = weight.shape[1]
    heads = weight.shape[0] // size
    return jnp.einsum(
        "thj,hjk->thk",
        values.reshape(row_count, heads, size),
        weight.reshape(heads, size, size),
        preferred_element_type=jnp.float32,
    ).reshape(row_count, heads * size)


def block_terms(values, grad_vals, size):
    row_count = values.shape[0]
    heads = values.shape[1] // size
    terms = jnp.einsum(
        "thj,thk->hjk",
        values.reshape(row_count, heads, size),
        grad_vals.reshape(row_count, heads, size),
        preferred_element_type=jnp.float32,
    )
    return terms.reshape(heads * size, size)


def block_back(grad_vals, weight):
    row_count = grad_vals.shape[0]
    size = weight.shape[1]
    heads = weight.shape[0] // size
    return jnp.einsum(
        "thk,hjk->thj",
        grad_vals.reshape(row_count, heads, size),
        weight.reshape(heads, size, size),
        preferred_element_type=jnp.float32,
    ).reshape(row_count, heads * size)


def per_device_general(
    tokens,
    lengths,
    cotangent,
    norm1_gain,
    gate_in,
    linear_in,
    conv_kernel,
    conv_bias,
    rate_weight,
    rate_bias,
    input_weight,
    input_bias,
    decay_param,
    out_proj,
    norm2_gain,
    mlp_gate,
    mlp_up,
    mlp_down,
):
    row_count = tokens.shape[0]
    segment_ids, live_rows = layout(lengths[0], row_count)
    live_col = live_rows[:, None]
    mixer_full = (
        lax.all_gather(norm1_gain, "shard", axis=0, tiled=True),
        lax.all_gather(gate_in, "shard", axis=0, tiled=True),
        lax.all_gather(linear_in, "shard", axis=0, tiled=True),
        lax.all_gather(conv_kernel, "shard", axis=1, tiled=True),
        lax.all_gather(conv_bias, "shard", axis=0, tiled=True),
        lax.all_gather(rate_weight, "shard", axis=0, tiled=True),
        lax.all_gather(rate_bias, "shard", axis=0, tiled=True),
        lax.all_gather(input_weight, "shard", axis=0, tiled=True),
        lax.all_gather(input_bias, "shard", axis=0, tiled=True),
        lax.all_gather(decay_param, "shard", axis=0, tiled=True),
        lax.all_gather(out_proj, "shard", axis=0, tiled=True),
    )
    gain_first = mixer_full[0].astype(jnp.float32)
    kernel_full = mixer_full[3].astype(jnp.float32)
    kernel_shift = mixer_full[4].astype(jnp.float32)
    rate_shift = mixer_full[6].astype(jnp.float32)
    input_shift = mixer_full[8].astype(jnp.float32)
    decay_full = mixer_full[9].astype(jnp.float32)
    block_size = mixer_full[5].shape[1]
    masked_in = tokens.astype(jnp.float32) * live_col
    normed_low = normalize(masked_in, gain_first).astype(jnp.bfloat16)
    gate_pre = product(normed_low, mixer_full[1])
    linear_out = product(normed_low, mixer_full[2])
    gate_act = jax.nn.gelu(gate_pre)
    conv_out = convolve(linear_out, kernel_full, kernel_shift, segment_ids)
    conv_low = conv_out.astype(jnp.bfloat16)
    rate_pre = blocked(conv_low, mixer_full[5]) + rate_shift
    input_pre = blocked(conv_low, mixer_full[7]) + input_shift
    states = recurrence(rate_pre, input_pre, conv_out, decay_full, segment_ids)
    merged_low = (gate_act * states).astype(jnp.bfloat16)
    middle = masked_in + product(merged_low, mixer_full[10])
    mlp_full = (
        lax.all_gather(norm2_gain, "shard", axis=0, tiled=True),
        lax.all_gather(mlp_gate, "shard", axis=0, tiled=True),
        lax.all_gather(mlp_up, "shard", axis=0, tiled=True),
        lax.all_gather(mlp_down, "shard", axis=0, tiled=True),
    )
    gain_second = mlp_full[0].astype(jnp.float32)
    normed_two = normalize(middle, gain_second).astype(jnp.bfloat16)
    gate_mlp = product(normed_two, mlp_full[1])
    up_mlp = product(normed_two, mlp_full[2])
    hidden_low = gated_gelu(gate_mlp, up_mlp).astype(jnp.bfloat16)
    mixed_out = ((middle + product(hidden_low, mlp_full[3])) * live_col).astype(jnp.bfloat16)
    grad_out = cotangent.astype(jnp.float32) * live_col
    grad_down = grad_out.astype(jnp.bfloat16)
    again_mlp = (
        lax.all_gather(mlp_gate, "shard", axis=0, tiled=True),
        lax.all_gather(mlp_up, "shard", axis=0, tiled=True),
        lax.all_gather(mlp_down, "shard", axis=0, tiled=True),
    )
    term_down = contract(hidden_low, grad_down)
    part_down = lax.psum_scatter(
        term_down.astype(jnp.bfloat16), "shard", scatter_dimension=0, tiled=True
    ).astype(jnp.float32)
    grad_hidden = back_dot(grad_down, again_mlp[2])
    unused_val, hidden_back = jax.vjp(gated_gelu, gate_mlp, up_mlp)
    grad_gate_mlp, grad_up_mlp = hidden_back(grad_hidden)
    gate_mlp_low = grad_gate_mlp.astype(jnp.bfloat16)
    up_mlp_low = grad_up_mlp.astype(jnp.bfloat16)
    term_gate_mlp = contract(normed_two, gate_mlp_low)
    term_up_mlp = contract(normed_two, up_mlp_low)
    grad_normed_two = back_dot(gate_mlp_low, again_mlp[0]) + back_dot(up_mlp_low, again_mlp[1])
    unused_two, second_back = jax.vjp(normalize, middle, gain_second)
    grad_middle_norm, term_gain_two = second_back(grad_normed_two)
    parts_mlp = (
        lax.psum_scatter(
            term_gain_two.astype(jnp.bfloat16), "shard", scatter_dimension=0, tiled=True
        ).astype(jnp.float32),
        lax.psum_scatter(
            term_gate_mlp.astype(jnp.bfloat16), "shard", scatter_dimension=0, tiled=True
        ).astype(jnp.float32),
        lax.psum_scatter(
            term_up_mlp.astype(jnp.bfloat16), "shard", scatter_dimension=0, tiled=True
        ).astype(jnp.float32),
    )
    grad_middle = grad_out + grad_middle_norm
    grad_mix_low = grad_middle.astype(jnp.bfloat16)
    again_mixer = (
        lax.all_gather(gate_in, "shard", axis=0, tiled=True),
        lax.all_gather(linear_in, "shard", axis=0, tiled=True),
        lax.all_gather(rate_weight, "shard", axis=0, tiled=True),
        lax.all_gather(input_weight, "shard", axis=0, tiled=True),
        lax.all_gather(out_proj, "shard", axis=0, tiled=True),
    )
    term_out = contract(merged_low, grad_mix_low)
    grad_merged = back_dot(grad_mix_low, again_mixer[4])
    grad_states = grad_merged * gate_act
    unused_three, gelu_back = jax.vjp(jax.nn.gelu, gate_pre)
    gate_low = gelu_back(grad_merged * states)[0].astype(jnp.bfloat16)
    unused_four, scan_back = jax.vjp(
        partial(recurrence, segment_ids=segment_ids), rate_pre, input_pre, conv_out, decay_full
    )
    grad_rate, grad_input, grad_flow, term_decay = scan_back(grad_states)
    rate_low = grad_rate.astype(jnp.bfloat16)
    input_low = grad_input.astype(jnp.bfloat16)
    term_rate = block_terms(conv_low, rate_low, block_size)
    term_input = block_terms(conv_low, input_low, block_size)
    term_rate_shift = jnp.sum(rate_low.astype(jnp.float32), axis=0)
    term_input_shift = jnp.sum(input_low.astype(jnp.float32), axis=0)
    grad_conv = (
        grad_flow + block_back(rate_low, again_mixer[2]) + block_back(input_low, again_mixer[3])
    )
    unused_five, conv_back = jax.vjp(
        partial(convolve, segment_ids=segment_ids), linear_out, kernel_full, kernel_shift
    )
    grad_linear, term_kernel, term_kernel_shift = conv_back(grad_conv)
    linear_low = grad_linear.astype(jnp.bfloat16)
    term_gate_in = contract(normed_low, gate_low)
    term_linear = contract(normed_low, linear_low)
    grad_normed = back_dot(gate_low, again_mixer[0]) + back_dot(linear_low, again_mixer[1])
    unused_six, first_back = jax.vjp(normalize, masked_in, gain_first)
    grad_masked, term_gain_one = first_back(grad_normed)
    grad_tokens = ((grad_middle + grad_masked) * live_col).astype(jnp.bfloat16)
    small_terms = (
        term_gain_one,
        term_kernel,
        term_kernel_shift,
        term_rate,
        term_rate_shift,
        term_input,
        term_input_shift,
        term_decay,
    )
    placed = tuple((term for term in small_terms))
    mixer_terms = (
        placed[0],
        term_gate_in,
        term_linear,
        placed[1],
        placed[2],
        placed[3],
        placed[4],
        placed[5],
        placed[6],
        placed[7],
        term_out,
    )
    parts_mixer = (
        lax.psum_scatter(
            mixer_terms[0].astype(jnp.bfloat16), "shard", scatter_dimension=0, tiled=True
        ).astype(jnp.float32),
        lax.psum_scatter(
            mixer_terms[1].astype(jnp.bfloat16), "shard", scatter_dimension=0, tiled=True
        ).astype(jnp.float32),
        lax.psum_scatter(
            mixer_terms[2].astype(jnp.bfloat16), "shard", scatter_dimension=0, tiled=True
        ).astype(jnp.float32),
        lax.psum_scatter(
            mixer_terms[3].astype(jnp.bfloat16), "shard", scatter_dimension=1, tiled=True
        ).astype(jnp.float32),
        lax.psum_scatter(
            mixer_terms[4].astype(jnp.bfloat16), "shard", scatter_dimension=0, tiled=True
        ).astype(jnp.float32),
        lax.psum_scatter(
            mixer_terms[5].astype(jnp.bfloat16), "shard", scatter_dimension=0, tiled=True
        ).astype(jnp.float32),
        lax.psum_scatter(
            mixer_terms[6].astype(jnp.bfloat16), "shard", scatter_dimension=0, tiled=True
        ).astype(jnp.float32),
        lax.psum_scatter(
            mixer_terms[7].astype(jnp.bfloat16), "shard", scatter_dimension=0, tiled=True
        ).astype(jnp.float32),
        lax.psum_scatter(
            mixer_terms[8].astype(jnp.bfloat16), "shard", scatter_dimension=0, tiled=True
        ).astype(jnp.float32),
        lax.psum_scatter(
            mixer_terms[9].astype(jnp.bfloat16), "shard", scatter_dimension=0, tiled=True
        ).astype(jnp.float32),
        lax.psum_scatter(
            mixer_terms[10].astype(jnp.bfloat16), "shard", scatter_dimension=0, tiled=True
        ).astype(jnp.float32),
    )
    shard_parts = tuple(parts_mixer) + (parts_mlp[0], parts_mlp[1], parts_mlp[2], part_down)
    totals = jax.tree.map(
        lambda part: part.astype(jnp.float32), lax.psum(as_sent(shard_parts), "group")
    )
    return (mixed_out, grad_tokens) + tuple(totals)


def solution(mesh):
    placed = (
        P(("group", "shard"), None),
        P(("group", "shard"), None),
        P(("group", "shard"), None),
        P("shard"),
        P("shard", None),
        P("shard", None),
        P(None, "shard"),
        P("shard"),
        P("shard", None),
        P("shard"),
        P("shard", None),
        P("shard"),
        P("shard"),
        P("shard", None),
        P("shard"),
        P("shard", None),
        P("shard", None),
        P("shard", None),
    )
    split_fits = FAST_MESH == tuple(mesh.shape[axis] for axis in ("group", "shard"))
    return jax.shard_map(
        per_device_split if split_fits else per_device_general,
        mesh=mesh,
        in_specs=placed,
        out_specs=(
            P(("group", "shard"), None),
            P(("group", "shard"), None),
            P("shard"),
            P("shard", None),
            P("shard", None),
            P(None, "shard"),
            P("shard"),
            P("shard", None),
            P("shard"),
            P("shard", None),
            P("shard"),
            P("shard"),
            P("shard", None),
            P("shard"),
            P("shard", None),
            P("shard", None),
            P("shard", None),
        ),
        check_vma=False,
    )
```

```python
from functools import partial

import jax
import jax.numpy as jnp
from jax import lax
from jax.experimental import pallas as pl
from jax.experimental.pallas import tpu as pltpu
from jax.sharding import PartitionSpec as P

FAST_MESH = (4, 8)
RATE_SCALE = 8.0
EPSILON = 1e-06
F32 = jnp.float32
BF16 = jnp.bfloat16
GELU_C = 0.7978845608028654
GELU_K = 0.044715
CAP = 128


def positions_in_run(counts, row_count):
    first = counts[0]
    second = first + counts[1]
    third = second + counts[2]
    rows = lax.broadcasted_iota(jnp.int32, (row_count, 1), 0)
    start = jnp.where(rows >= first, first, 0)
    start = jnp.where(rows >= second, second, start)
    start = jnp.where(rows >= third, third, start)
    return rows - start, (rows < third).astype(F32)


def gelu_parts(x):
    t = jnp.tanh(GELU_C * (x + GELU_K * x * x * x))
    value = 0.5 * x * (1.0 + t)
    slope = 0.5 * (1.0 + t) + 0.5 * x * (1.0 - t * t) * GELU_C * (1.0 + 3.0 * GELU_K * x * x)
    return value, slope


def gelu_value(x):
    return 0.5 * x * (1.0 + jnp.tanh(GELU_C * (x + GELU_K * x * x * x)))


def sigmoid(x):
    return 0.5 * (1.0 + jnp.tanh(0.5 * x))


def one_less_exp(z):
    series = 1.0 - z * (1.0 / 7.0)
    for k in (6.0, 5.0, 4.0, 3.0, 2.0):
        series = 1.0 - z * (1.0 / k) * series
    return jnp.where(z < 0.35, z * series, 1.0 - jnp.exp(-z))


def softplus_neg(x):
    return jnp.maximum(-x, 0.0) + jnp.log1p(jnp.exp(-jnp.abs(x)))


def mm(a, b):
    return jnp.dot(a, b, preferred_element_type=F32)


def mm_nt(a, b):
    return lax.dot_general(a, b, (((1,), (1,)), ((), ())), preferred_element_type=F32)


def mm_tn(a, b):
    return lax.dot_general(a, b, (((0,), (0,)), ((), ())), preferred_element_type=F32)


def roll_rows(x, n):
    return pltpu.roll(x, n % x.shape[0], 0)


def conv_rows(linear, kernel, bias, masks):
    out = linear * kernel[0:1] + bias
    for k in range(1, 4):
        out = out + kernel[k : k + 1] * (roll_rows(linear, k) * masks[k - 1])
    return out


def decay_terms(rate_pre, decay):
    rate = sigmoid(rate_pre)
    keep = RATE_SCALE * rate * softplus_neg(decay)
    return rate, jnp.exp(-keep), jnp.sqrt(one_less_exp(2.0 * keep))


MESH_ID = pl.DeviceIdType.MESH
VMEM_LIMIT = 62 * 2**20
N_Z, N_X = 4, 2


def place():
    shard = lax.axis_index("shard")
    return lax.axis_index("group"), shard, shard // N_X, shard % N_X


def greet(peers):
    bar = pltpu.get_barrier_semaphore()
    count = 0
    for device, there in peers:
        if there is True:
            pl.semaphore_signal(bar, inc=1, device_id=device, device_id_type=MESH_ID)
            count = count + 1
        else:
            @pl.when(there)
            def _(device=device):
                pl.semaphore_signal(bar, inc=1, device_id=device, device_id_type=MESH_ID)
            count = count + there.astype(jnp.int32)
    pl.semaphore_wait(bar, count)


def line_peers():
    group, shard, z, x = place()
    return [
        ((group, shard + N_X), z < N_Z - 1),
        ((group, shard - N_X), z > 0),
        ((group, z * N_X + 1 - x), True),
    ]


class Gather:
    CHUNKS = 2

    @classmethod
    def scratch(cls):
        return [pltpu.SemaphoreType.DMA((3, N_Z, cls.CHUNKS)), pltpu.SemaphoreType.DMA((N_Z * N_X, cls.CHUNKS))]

    def __init__(self, buf, sems):
        self.buf, (self.send, self.recv) = buf, sems
        self.group, self.shard, self.z, self.x = place()
        self.rows = buf.shape[1] // self.CHUNKS

    def copy(self, origin, column, c, way):
        slot = origin * N_X + column
        z = (self.z + 1, self.z - 1, self.z)[way]
        x = 1 - self.x if way == 2 else self.x
        piece = self.buf.at[slot, pl.ds(c * self.rows, self.rows)]
        return pltpu.make_async_remote_copy(
            src_ref=piece, dst_ref=piece, send_sem=self.send.at[way, origin, c],
            recv_sem=self.recv.at[slot, c], device_id=(self.group, z * N_X + x), device_id_type=MESH_ID,
        )

    def start(self):
        for c in range(self.CHUNKS):
            self.forward(self.z, c, True, True)

    def forward(self, origin, c, up, down):
        if up:
            @pl.when(self.z < N_Z - 1)
            def _():
                self.copy(origin, self.x, c, 0).start()
        if down:
            @pl.when(self.z > 0)
            def _():
                self.copy(origin, self.x, c, 1).start()
        self.copy(origin, self.x, c, 2).start()

    def step(self, k):
        for c in range(self.CHUNKS):
            @pl.when(self.z >= k)
            def _(c=c):
                self.copy(self.z - k, self.x, c, 2).wait_recv()
                self.forward(self.z - k, c, True, False)

            @pl.when(self.z + k < N_Z)
            def _(c=c):
                self.copy(self.z + k, self.x, c, 2).wait_recv()
                self.forward(self.z + k, c, False, True)

    def wait_across(self, origin):
        for c in range(self.CHUNKS):
            self.copy(origin, 1 - self.x, c, 2).wait_recv()

    def finish(self):
        for c in range(self.CHUNKS):
            for origin in range(N_Z):
                @pl.when((self.z < N_Z - 1) & (origin <= self.z))
                def _():
                    self.copy(origin, self.x, c, 0).wait_send()

                @pl.when((self.z > 0) & (origin >= self.z))
                def _():
                    self.copy(origin, self.x, c, 1).wait_send()
                self.copy(origin, self.x, c, 2).wait_send()


class Scatter:
    CHUNKS = 2

    @classmethod
    def scratch(cls, rows, width):
        dma = pltpu.SemaphoreType.DMA
        return [
            pltpu.VMEM((N_Z, rows, width), BF16),
            pltpu.VMEM((N_Z + 1, rows, width), BF16),
            pltpu.VMEM((N_Z, rows, width), BF16),
            dma((2, N_Z, cls.CHUNKS)), dma((N_Z, cls.CHUNKS)), dma((N_Z + 1, cls.CHUNKS)),
        ]

    def __init__(self, parts, scratch):
        self.parts = parts
        self.across, self.along, self.held, self.send, self.recv_x, self.recv_z = scratch
        self.group, self.shard, self.z, self.x = place()
        self.rows = parts.shape[1] // self.CHUNKS

    def dest(self, i):
        low = jnp.minimum(self.z, N_Z - 1 - self.z)
        value = (N_Z - 1, N_Z - 2, jnp.where(low == 0, 1, 0), low)[i]
        return jnp.where(self.z >= N_Z // 2, N_Z - 1 - value, value)

    def span(self, c):
        return pl.ds(c * self.rows, self.rows)

    def copy_x(self, dest, c):
        return pltpu.make_async_remote_copy(
            src_ref=self.parts.at[dest * N_X + 1 - self.x, self.span(c)],
            dst_ref=self.across.at[dest, self.span(c)],
            send_sem=self.send.at[0, dest, c], recv_sem=self.recv_x.at[dest, c],
            device_id=(self.group, self.z * N_X + 1 - self.x), device_id_type=MESH_ID,
        )

    def copy_z(self, dest, slot, c, step):
        return pltpu.make_async_remote_copy(
            src_ref=self.held.at[dest, self.span(c)], dst_ref=self.along.at[slot, self.span(c)],
            send_sem=self.send.at[1, dest, c], recv_sem=self.recv_z.at[slot, c],
            device_id=(self.group, (self.z + step) * N_X + self.x), device_id_type=MESH_ID,
        )

    def start(self, i):
        for c in range(self.CHUNKS):
            self.copy_x(self.dest(i), c).start()

    def arrived(self, slot, c):
        self.copy_z(0, slot, c, 0).wait_recv()
        return self.along[slot, self.span(c)].astype(F32)

    def step(self, i):
        dest = self.dest(i)
        for c in range(self.CHUNKS):
            self.copy_x(dest, c).wait_recv()
            own = dest * N_X + self.x
            self.held[dest, self.span(c)] = (
                self.parts[own, self.span(c)].astype(F32) + self.across[dest, self.span(c)].astype(F32)
            ).astype(BF16)

            @pl.when(((dest > self.z) & (self.z > 0)) | ((dest < self.z) & (self.z < N_Z - 1)))
            def _(c=c):
                self.held[dest, self.span(c)] = (
                    self.parts[own, self.span(c)].astype(F32) + self.across[dest, self.span(c)].astype(F32)
                    + self.arrived(dest, c)
                ).astype(BF16)

            @pl.when(dest > self.z)
            def _(c=c):
                self.copy_z(dest, dest, c, 1).start()

            @pl.when(dest < self.z)
            def _(c=c):
                self.copy_z(dest, jnp.where(dest == self.z - 1, N_Z, dest), c, -1).start()

    def last(self, out):
        for c in range(self.CHUNKS):
            self.copy_x(self.z, c).wait_recv()
            out[self.span(c)] = self.parts[self.shard, self.span(c)].astype(F32) + self.across[self.z, self.span(c)].astype(F32)

            @pl.when(self.z > 0)
            def _(c=c):
                out[self.span(c)] += self.arrived(self.z, c)

            @pl.when(self.z < N_Z - 1)
            def _(c=c):
                out[self.span(c)] += self.arrived(N_Z, c)

    def finish(self):
        for c in range(self.CHUNKS):
            for dest in range(N_Z):
                self.copy_x(dest, c).wait_send()

                @pl.when(dest != self.z)
                def _():
                    self.copy_z(dest, 0, c, 0).wait_send()


class Exchange:
    @classmethod
    def scratch(cls, shards, sources):
        dma = pltpu.SemaphoreType.DMA
        return [dma((sources, shards)), dma((sources, shards)), dma((3, shards)), dma((3, shards))]

    def __init__(self, sources, full, spans, sems):
        self.sources, self.full, self.spans = sources, full, spans
        self.send_first, self.recv_first, self.send, self.recv = sems
        self.group, self.shard, _, _ = place()
        self.shards = full.shape[0]
        self.core_mate, self.y_mate = mates()

    def first(self, j, to, origin):
        return pltpu.make_async_remote_copy(
            src_ref=self.sources[j](to), dst_ref=self.full.at[origin, self.group, :, self.spans[j]],
            send_sem=self.send_first.at[j, to], recv_sem=self.recv_first.at[j, origin],
            device_id=(self.group, to), device_id_type=MESH_ID,
        )

    def own(self, j):
        return pltpu.make_async_copy(
            self.sources[j](self.shard), self.full.at[self.shard, self.group, :, self.spans[j]],
            self.recv_first.at[j, self.shard],
        )

    def pass_on(self, origin, quarter, mate, way):
        piece = self.full.at[origin, quarter]
        return pltpu.make_async_remote_copy(
            src_ref=piece, dst_ref=piece, send_sem=self.send.at[way, origin], recv_sem=self.recv.at[way, origin],
            device_id=(mate, self.shard), device_id_type=MESH_ID,
        )

    def start(self):
        for j in range(len(self.sources)):
            self.own(j).start()

        @pl.loop(1, self.shards)
        def _(i):
            to = (self.shard + i) % self.shards
            for j in range(len(self.sources)):
                self.first(j, to, self.shard).start()

    def spread(self):
        for j in range(len(self.sources)):
            self.own(j).wait()
        self.pass_on(self.shard, self.group, self.core_mate, 0).start()
        self.pass_on(self.shard, self.group, self.y_mate, 1).start()

        @pl.loop(1, self.shards)
        def _(i):
            origin = (self.shard + self.shards - i) % self.shards
            for j in range(len(self.sources)):
                self.first(j, origin, origin).wait_recv()
            self.pass_on(origin, self.group, self.core_mate, 0).start()
            self.pass_on(origin, self.group, self.y_mate, 1).start()

    def relay(self):
        @pl.loop(0, self.shards)
        def _(i):
            origin = (self.shard + self.shards - i) % self.shards
            self.pass_on(origin, self.y_mate, self.core_mate, 1).wait_recv()
            self.pass_on(origin, self.y_mate, self.core_mate, 2).start()

    def arrive(self):
        @pl.loop(0, self.shards)
        def _(origin):
            self.pass_on(origin, self.group, self.core_mate, 0).wait_recv()
            self.pass_on(origin, self.group, self.core_mate, 2).wait_recv()

    def finish(self):
        @pl.loop(1, self.shards)
        def _(i):
            to = (self.shard + i) % self.shards
            for j in range(len(self.sources)):
                self.first(j, to, self.shard).wait_send()

        @pl.loop(0, self.shards)
        def _(origin):
            for way in range(3):
                self.pass_on(origin, self.group, self.core_mate, way).wait_send()


def mates():
    group = lax.axis_index("group")
    return group + 1 - 2 * (group % 2), group + 2 - 4 * (group // 2)


def all_peers():
    group, shard, _, _ = place()
    core_mate, y_mate = mates()
    others = [((group, (shard + i) % (N_Z * N_X)), True) for i in range(1, N_Z * N_X)]
    return others + [((core_mate, shard), True), ((y_mate, shard), True)]


def mixer_forward(linear, gate, pos, vec, gates):
    masks = [(pos >= k).astype(F32) for k in (1, 2, 3)]
    conv = conv_rows(linear, vec[0:4], vec[4:5], masks)
    width = linear.shape[1]
    both = mm(conv.astype(BF16), gates)
    rate_pre = both[:, :width] + vec[5:6]
    input_pre = both[:, width:] + vec[6:7]
    _, a, weight_in = decay_terms(rate_pre, vec[7:8])
    mult = a * masks[0]
    total = weight_in * sigmoid(input_pre) * conv
    step = 1
    while step < CAP:
        total = total + mult * roll_rows(total, step)
        if 2 * step < CAP:
            mult = mult * roll_rows(mult, step)
        step *= 2
    return rate_pre, input_pre, total, (gelu_value(gate) * total).astype(BF16)


def rms_scale(values):
    return lax.rsqrt(jnp.mean(values * values, axis=1, keepdims=True) + EPSILON)


def forward_kernel(
    lengths_ref, tokens_ref, gains_ref, vec_ref, gates_ref, out_proj_ref, gate_in_ref, linear_in_ref, mlp_gate_ref, mlp_up_ref,
    gather_out, weights_out, mlp_out, gains_out, saved_out, merged_out, middle_ref, normed_two_ref,
    buf, weights, quarter, raw, masked, saved, merged, parts,
    gather_a, gather_b, ex_a, ex_b, ex_c, ex_d, mx_a, mx_b, mx_c, mx_d, *rest,
):
    scatter_scratch, (gain_send, gain_recv, raw_sem, out_sem, pair_sem) = rest[:-5], rest[-5:]
    group, shard, z, x = place()
    shards = N_Z * N_X
    rows, width = tokens_ref.shape
    quarter_rows = raw.shape[1]
    chans = linear_in_ref.shape[1] // shards
    padded = vec_ref.shape[1]
    fetch = [
        pltpu.make_async_copy(ref.at[pl.ds(group * quarter_rows, quarter_rows)], raw.at[i], raw_sem.at[i])
        for i, ref in enumerate((gate_in_ref, linear_in_ref))
    ]
    for copy in fetch:
        copy.start()
    greet(all_peers())

    def gain_copy(to, origin):
        return pltpu.make_async_remote_copy(
            src_ref=gains_ref, dst_ref=gains_out.at[origin], send_sem=gain_send.at[to], recv_sem=gain_recv.at[origin],
            device_id=(group, to), device_id_type=MESH_ID,
        )

    for i in range(1, shards):
        gain_copy((shard + i) % shards, shard).start()
    gains_out[shard] = gains_ref[...]
    inside = lax.broadcasted_iota(jnp.int32, (quarter_rows, padded), 1) < chans
    for i, copy in enumerate(fetch):
        copy.wait()
        for to in range(shards):
            piece = raw[i, :, to * chans : (to + 1) * chans].astype(F32)
            piece = jnp.concatenate([piece, jnp.zeros((quarter_rows, padded - chans), F32)], axis=1)
            quarter[to, :, i * padded : (i + 1) * padded] = piece.astype(BF16)
    exchange = Exchange([lambda to: quarter.at[to]], weights, [slice(None)], (ex_a, ex_b, ex_c, ex_d))
    exchange.start()
    hidden = mlp_up_ref.shape[1] // shards

    def part_of(ref):
        return lambda to: ref.at[pl.ds(group * quarter_rows, quarter_rows), pl.ds(to * hidden, hidden)]

    mlp_exchange = Exchange(
        [part_of(mlp_gate_ref), part_of(mlp_up_ref)], mlp_out, [slice(0, hidden), slice(hidden, 2 * hidden)], (mx_a, mx_b, mx_c, mx_d)
    )
    pos, live = positions_in_run([lengths_ref[0, i] for i in range(3)], rows)
    masked[...] = tokens_ref[...].astype(F32) * live
    for i in range(1, shards):
        gain_copy(shard, (shard + i) % shards).wait_recv()
    gains = jnp.concatenate([gains_out[i] for i in range(shards)], axis=1)
    gather = Gather(buf, (gather_a, gather_b))
    buf[shard, :, :width] = (masked[...] * rms_scale(masked[...]) * gains[0:1]).astype(BF16)
    buf[shard, :, width:] = jnp.broadcast_to(pos.astype(F32).astype(BF16), (rows, buf.shape[2] - width))
    gather.start()
    gather.step(1)
    exchange.spread()
    gather.step(2)
    exchange.relay()
    mlp_exchange.start()
    exchange.arrive()
    scatter = Scatter(parts, scatter_scratch)

    def pair_copies(origin):
        return [
            pltpu.make_async_copy(saved.at[origin], saved_out.at[origin], pair_sem.at[0, origin]),
            pltpu.make_async_copy(merged.at[origin], merged_out.at[origin], pair_sem.at[1, origin]),
        ]

    @pl.loop(0, N_Z)
    def _(i):
        @pl.when(i == 1)
        def _():
            gather.step(3)

        origin = nearest(z, i)
        gather.wait_across(origin)
        pair = pl.ds(origin * N_X, N_X)
        both = buf[pair].reshape(N_X * rows, buf.shape[2])
        pre = mm(both[:, :width], weights[...].reshape(width, 2 * padded))
        gate, linear = pre[:, :padded], pre[:, padded:]
        where = both[:, width : width + 1].astype(F32)
        rate_pre, input_pre, state, merge = mixer_forward(linear, gate, where, vec_ref[...], gates_ref[...])
        for j, value in enumerate((gate, linear, rate_pre, input_pre, state)):
            saved[origin, j] = value
        merged[origin] = merge
        for copy in pair_copies(origin):
            copy.start()
        parts[pair] = mm(merge[:, :chans], out_proj_ref[...]).astype(BF16).reshape(N_X, rows, width)

    outs = [
        pltpu.make_async_copy(buf, gather_out, out_sem.at[0]),
        pltpu.make_async_copy(weights, weights_out, out_sem.at[1]),
    ]
    for copy in outs:
        copy.start()
    for i in range(N_Z):
        scatter.start(i)
    mlp_exchange.spread()
    scatter.step(0)
    mlp_exchange.relay()
    scatter.step(1)
    scatter.step(2)
    scatter.last(middle_ref)
    middle_ref[...] += masked[...]
    normed_two_ref[...] = (middle_ref[...] * rms_scale(middle_ref[...]) * gains[1:2]).astype(BF16)
    for i in range(1, shards):
        gain_copy((shard + i) % shards, shard).wait_send()
    gather.finish()
    exchange.finish()
    mlp_exchange.arrive()
    mlp_exchange.finish()
    scatter.finish()
    for copy in outs:
        copy.wait()

    @pl.loop(0, N_Z)
    def _(origin):
        for copy in pair_copies(origin):
            copy.wait()


def nearest(z, i):
    low = jnp.minimum(z, N_Z - 1 - z)
    value = jnp.where(low == 0, i, jnp.where(i == 0, 1, jnp.where(i == 1, 0, i)))
    return jnp.where(z >= N_Z // 2, N_Z - 1 - value, value)


def any_spec():
    return pl.BlockSpec(memory_space=pl.ANY)


def vmem_spec():
    return pl.BlockSpec(memory_space=pltpu.VMEM)


def forward_call(lengths, tokens, gains, vec, gates, out_proj, gate_in, linear_in, mlp_gate, mlp_up):
    rows, width = tokens.shape
    shards, groups = lax.axis_size("shard"), lax.axis_size("group")
    padded = vec.shape[1]
    quarter_rows = gate_in.shape[0] // groups
    hidden = mlp_up.shape[1] // shards
    dma = pltpu.SemaphoreType.DMA
    shape = jax.ShapeDtypeStruct
    out_shape = [
        shape((shards, rows, width + 128), BF16),
        shape((shards, groups, quarter_rows, 2 * padded), BF16),
        shape((shards, groups, quarter_rows, 2 * hidden), BF16),
        shape((shards,) + gains.shape, F32),
        shape((N_Z, 5, N_X * rows, padded), F32),
        shape((N_Z, N_X * rows, padded), BF16),
        shape((rows, width), F32),
        shape((rows, width), BF16),
    ]
    return pl.pallas_call(
        forward_kernel,
        out_shape=out_shape,
        in_specs=[pl.BlockSpec(memory_space=pltpu.SMEM)] + [vmem_spec()] * 5 + [any_spec()] * 4,
        out_specs=[any_spec()] * 3 + [vmem_spec()] + [any_spec()] * 2 + [vmem_spec()] * 2,
        scratch_shapes=[
            pltpu.VMEM((shards, rows, width + 128), BF16),
            pltpu.VMEM((shards, groups, quarter_rows, 2 * padded), BF16),
            pltpu.VMEM((shards, quarter_rows, 2 * padded), BF16),
            pltpu.VMEM((2, quarter_rows, gate_in.shape[1]), BF16),
            pltpu.VMEM((rows, width), F32),
            pltpu.VMEM((N_Z, 5, N_X * rows, padded), F32),
            pltpu.VMEM((N_Z, N_X * rows, padded), BF16),
            pltpu.VMEM((shards, rows, width), BF16),
        ]
        + Gather.scratch()
        + Exchange.scratch(shards, 1)
        + Exchange.scratch(shards, 2)
        + Scatter.scratch(rows, width)
        + [dma((shards,)), dma((shards,)), dma((2,)), dma((2,)), dma((2, N_Z))],
        compiler_params=pltpu.CompilerParams(collective_id=1, has_side_effects=True, vmem_limit_bytes=VMEM_LIMIT),
        name="mixer_forward",
    )(lengths, tokens, gains, vec, gates, out_proj, gate_in, linear_in, mlp_gate, mlp_up)


def mixer_backward_kernel(pos_ref, gm_ref, gate_ref, linear_ref, rate_ref, input_ref, state_ref,
                          ck_ref, vec_ref, rw_ref, iw_ref,
                          gg_ref, gl_ref, small_ref, rate_out_ref, input_out_ref, tr_ref, ti_ref):
    @pl.when(pl.program_id(0) == 0)
    def _():
        small_ref[...] = jnp.zeros_like(small_ref)
        tr_ref[...] = jnp.zeros_like(tr_ref)
        ti_ref[...] = jnp.zeros_like(ti_ref)

    pos = pos_ref[...]
    rows = pos.shape[0]
    masks = [(pos >= k).astype(F32) for k in (1, 2, 3)]
    index = lax.broadcasted_iota(jnp.int32, pos.shape, 0)
    later = [
        jnp.where(index < rows - k, roll_rows(masks[k - 1], -k), 0.0) for k in (1, 2, 3)
    ]
    linear = linear_ref[...]
    kernel = ck_ref[...]
    conv = conv_rows(linear, kernel, vec_ref[0:1], masks)
    low = conv.astype(BF16)
    input_gate = sigmoid(input_ref[...])
    decay = vec_ref[3:4]
    rate, a, weight_in = decay_terms(rate_ref[...], decay)
    state = state_ref[...]
    g_merged = gm_ref[...]
    act, slope = gelu_parts(gate_ref[...])
    gg_ref[...] = (g_merged * state * slope).astype(BF16)
    lam = g_merged * act
    mult = roll_rows(a, -1) * later[0]
    step = 1
    while step < rows:
        lam = lam + mult * roll_rows(lam, -step)
        if 2 * step < rows:
            mult = mult * roll_rows(mult, -step)
        step *= 2
    g_a = lam * (roll_rows(state, 1) * masks[0])
    opened = input_gate * conv
    g_keep = g_a * a - lam * opened * (a * a) / weight_in
    slow = RATE_SCALE * rate
    g_rate = (g_keep * (-RATE_SCALE * softplus_neg(decay)) * (rate * (1.0 - rate))).astype(BF16)
    g_decay = g_keep * slow * sigmoid(-decay)
    flow = lam * weight_in
    g_inp = (flow * conv * (input_gate * (1.0 - input_gate))).astype(BF16)
    g_conv = flow * input_gate + mm_nt(g_rate, rw_ref[...]) + mm_nt(g_inp, iw_ref[...])
    g_linear = g_conv * kernel[0:1]
    sums = [jnp.sum(g_conv * linear, axis=0, keepdims=True)]
    for k in (1, 2, 3):
        g_linear = g_linear + kernel[k : k + 1] * (roll_rows(g_conv, -k) * later[k - 1])
        sums.append(jnp.sum(g_conv * (roll_rows(linear, k) * masks[k - 1]), axis=0, keepdims=True))
    gl_ref[...] = g_linear.astype(BF16)
    sums.append(jnp.sum(g_conv, axis=0, keepdims=True))
    sums.append(jnp.sum(g_rate.astype(F32), axis=0, keepdims=True))
    sums.append(jnp.sum(g_inp.astype(F32), axis=0, keepdims=True))
    sums.append(jnp.sum(g_decay, axis=0, keepdims=True))
    small_ref[...] += jnp.concatenate(sums, axis=0)
    tr_ref[...] += mm_tn(low, g_rate)
    ti_ref[...] += mm_tn(low, g_inp)

    @pl.when(pl.program_id(0) == pl.num_programs(0) - 1)
    def _():
        size = rate_out_ref.shape[1]
        for h in range(rate_out_ref.shape[0] // size):
            part = slice(h * size, (h + 1) * size)
            rate_out_ref[part] = tr_ref[part, part].astype(BF16)
            input_out_ref[part] = ti_ref[part, part].astype(BF16)


def block_diagonal(weight):
    size = weight.shape[1]
    heads = weight.shape[0] // size
    parts = []
    for h in range(heads):
        parts.append(
            jnp.pad(weight[h * size : (h + 1) * size], ((0, 0), (h * size, (heads - 1 - h) * size)))
        )
    return jnp.concatenate(parts, axis=0)


def per_device_split(
    tokens, lengths, cotangent, norm1_gain, gate_in, linear_in, conv_kernel, conv_bias, rate_weight,
    rate_bias, input_weight, input_bias, decay_param, out_proj, norm2_gain, mlp_gate, mlp_up, mlp_down,
):
    rows, width = tokens.shape
    n_shard = lax.axis_size("shard")
    size = rate_weight.shape[1]
    chans = rate_weight.shape[0]
    total_rows = rows * n_shard

    def gather(x):
        return lax.all_gather(x, "shard", axis=0, tiled=True)

    def scatter(x):
        return lax.psum_scatter(x.astype(BF16), "shard", scatter_dimension=0, tiled=True).astype(F32)

    def columns(w):
        return lax.all_to_all(w, "shard", split_axis=1, concat_axis=0, tiled=True)

    pos, live = positions_in_run(lengths[0], rows)
    padded = -(-chans // 128) * 128
    masked = tokens.astype(F32) * live
    scale1 = lax.rsqrt(jnp.mean(masked * masked, axis=1, keepdims=True) + EPSILON)
    own_gains = jnp.pad(jnp.stack([norm1_gain, norm2_gain]).astype(F32), ((0, 6), (0, 0)))
    rate_bd, input_bd = block_diagonal(rate_weight), block_diagonal(input_weight)
    fill = ((0, padded - chans), (0, padded - chans))
    gates = jnp.concatenate([jnp.pad(rate_bd, fill), jnp.pad(input_bd, fill)], axis=1)
    vec = jnp.concatenate([conv_kernel, jnp.stack([conv_bias, rate_bias, input_bias, decay_param])]).astype(F32)
    vec8 = jnp.pad(vec, ((0, 0), (0, padded - chans)))
    got, gl_w, mlp_w, gains, saved, merged, middle, normed_two_own = forward_call(
        lengths, tokens, own_gains, vec8, gates, out_proj, gate_in, linear_in, mlp_gate, mlp_up
    )
    gains = gains.transpose(1, 0, 2).reshape(8, width)
    got = got.reshape(total_rows, -1)
    normed_all = got[:, :width]
    pos_all = got[:, width : width + 1].astype(jnp.int32)
    gl_w = gl_w.reshape(width, -1)
    gate_w, linear_w = gl_w[:, :chans], gl_w[:, padded : padded + chans]
    mlp_w = mlp_w.reshape(width, -1)
    mg_w, mu_w = mlp_w[:, : mlp_w.shape[1] // 2], mlp_w[:, mlp_w.shape[1] // 2 :]
    gate_pre, linear_pre, rate_pre, input_pre, state = [
        saved[:, j].reshape(total_rows, padded)[:, :chans] for j in range(5)
    ]
    merged = merged.reshape(total_rows, padded)[:, :chans]
    vec, ck = vec[4:], vec[:4]
    row_spec = pl.BlockSpec((rows, chans), lambda i: (i, 0))
    pos_spec = pl.BlockSpec((rows, 1), lambda i: (i, 0))

    def whole(a):
        return pl.BlockSpec(a.shape, lambda i: (0,) * a.ndim)

    b_shape = jax.ShapeDtypeStruct((total_rows, chans), BF16)
    scale2 = lax.rsqrt(jnp.mean(middle * middle, axis=1, keepdims=True) + EPSILON)
    normed_two = gather(normed_two_own)
    g_out = cotangent.astype(F32) * live
    g_low = gather(g_out.astype(BF16))
    gate_mlp = mm(normed_two, mg_w)
    up_mlp = mm(normed_two, mu_w)
    act, slope = gelu_parts(gate_mlp)
    hidden = (act * up_mlp).astype(BF16)
    mixed = ((middle + scatter(mm(hidden, mlp_down))) * live).astype(BF16)
    term_down = mm_tn(hidden, g_low).astype(BF16)
    g_hidden = mm_nt(g_low, mlp_down)
    g_gate_mlp = (g_hidden * up_mlp * slope).astype(BF16)
    g_up = (g_hidden * act).astype(BF16)
    term_mg = mm_tn(normed_two, g_gate_mlp).astype(BF16)
    term_mu = mm_tn(normed_two, g_up).astype(BF16)
    g_normed_two = scatter(mm_nt(g_gate_mlp, mg_w) + mm_nt(g_up, mu_w))
    e2 = g_normed_two * gains[1:2]
    g_middle = (
        g_out + scale2 * e2
        - middle * (scale2 * scale2 * scale2) * jnp.mean(middle * e2, axis=1, keepdims=True)
    )
    gain2_term = jnp.sum(g_normed_two * middle * scale2, axis=0)
    g_mix = gather(g_middle.astype(BF16))
    term_out = mm_tn(merged, g_mix).astype(BF16)
    g_merged = mm_nt(g_mix, out_proj)
    small_shape = jax.ShapeDtypeStruct((8, chans), F32)
    bd_shape = jax.ShapeDtypeStruct((chans, size), BF16)
    g_gate, g_linear, small, tr, ti = pl.pallas_call(
        mixer_backward_kernel,
        grid=(n_shard,),
        in_specs=[pos_spec] + [row_spec] * 6 + [whole(ck), whole(vec), whole(rate_bd), whole(input_bd)],
        out_specs=[row_spec] * 2 + [whole(small_shape), whole(bd_shape), whole(bd_shape)],
        out_shape=[b_shape, b_shape, small_shape, bd_shape, bd_shape],
        scratch_shapes=[pltpu.VMEM((chans, chans), F32)] * 2,
        compiler_params=pltpu.CompilerParams(vmem_limit_bytes=32 * 2**20),
        name="mixer_backward",
    )(pos_all, g_merged, gate_pre, linear_pre, rate_pre, input_pre, state, ck, vec, rate_bd, input_bd)
    term_gi = mm_tn(normed_all, g_gate).astype(BF16)
    term_li = mm_tn(normed_all, g_linear).astype(BF16)
    g_normed = scatter(mm_nt(g_gate, gate_w) + mm_nt(g_linear, linear_w))
    e1 = g_normed * gains[0:1]
    g_masked = (
        scale1 * e1
        - masked * (scale1 * scale1 * scale1) * jnp.mean(masked * e1, axis=1, keepdims=True)
    )
    gain1_term = jnp.sum(g_normed * masked * scale1, axis=0)
    grad_tokens = ((g_middle + g_masked) * live).astype(BF16)

    def back_columns(t):
        return lax.all_to_all(t, "shard", split_axis=0, concat_axis=1, tiled=True)

    gain_terms = lax.psum_scatter(
        jnp.stack([gain1_term, gain2_term]).astype(BF16), "shard", scatter_dimension=1, tiled=True
    )
    sums = lax.psum(
        (gain_terms, back_columns(term_gi), back_columns(term_li), small.astype(BF16), tr, ti, term_out,
         back_columns(term_mg), back_columns(term_mu), term_down), "group",
    )
    gain_s, gi_s, li_s, small_s, tr_s, ti_s, out_s, mg_s, mu_s, down_s = [s.astype(F32) for s in sums]
    return (
        mixed, grad_tokens, gain_s[0], gi_s, li_s, small_s[0:4], small_s[4], tr_s, small_s[5], ti_s,
        small_s[6], small_s[7], out_s, gain_s[1], mg_s, mu_s, down_s,
    )


def as_sent(shard):
    return jax.tree.map(lambda a: a.astype(jnp.bfloat16) if a.dtype == jnp.float32 else a, shard)


def layout(counts, row_count):
    first = counts[0]
    second = first + counts[1]
    run_ends = jnp.stack([first, second, second + counts[2], second + counts[2] + counts[3]])
    positions = jnp.arange(row_count, dtype=jnp.int32)
    segment_ids = jnp.sum((positions[:, None] >= run_ends[None, :-1]).astype(jnp.int32), axis=1)
    live_rows = (positions < run_ends[-2]).astype(jnp.float32)
    return (segment_ids, live_rows)


def earlier_ids(segment_ids, offset):
    filler = jnp.full((offset,), -1, dtype=jnp.int32)
    return jnp.concatenate([filler, segment_ids[:-offset]])


def normalize(values, gain_vec):
    scale = lax.rsqrt(jnp.mean(values * values, axis=1, keepdims=True) + EPSILON)
    return values * scale * gain_vec


def convolve(linear_out, kernel, shift_vec, segment_ids):
    summed = linear_out * kernel[0] + shift_vec
    for offset in range(1, kernel.shape[0]):
        shifted = jnp.concatenate(
            [jnp.zeros((offset, linear_out.shape[1]), linear_out.dtype), linear_out[:-offset]],
            axis=0,
        )
        same_seq = (earlier_ids(segment_ids, offset) == segment_ids).astype(linear_out.dtype)
        summed = summed + kernel[offset] * shifted * same_seq[:, None]
    return summed


def combine_pairs(earlier_pair, later_pair):
    return (earlier_pair[0] * later_pair[0], later_pair[0] * earlier_pair[1] + later_pair[1])


def recurrence(rate_pre, input_pre, inflow, decay_vec, segment_ids):
    rate_gate = jax.nn.sigmoid(rate_pre)
    opened = jax.nn.sigmoid(input_pre)
    log_keep = -RATE_SCALE * rate_gate * jax.nn.softplus(-decay_vec)
    factor = jnp.exp(log_keep)
    weight_in = jnp.sqrt(-jnp.expm1(2.0 * log_keep))
    same_run = (earlier_ids(segment_ids, 1) == segment_ids).astype(factor.dtype)
    carried, states = lax.associative_scan(
        combine_pairs, (factor * same_run[:, None], weight_in * opened * inflow), axis=0
    )
    return states


def gated_gelu(gate_vals, up_vals):
    return jax.nn.gelu(gate_vals) * up_vals


def product(left, right):
    return jnp.dot(left, right, preferred_element_type=jnp.float32)


def contract(left, right):
    return jnp.einsum("ti,tj->ij", left, right, preferred_element_type=jnp.float32)


def back_dot(grad_vals, weight):
    return jnp.einsum("tj,ij->ti", grad_vals, weight, preferred_element_type=jnp.float32)


def blocked(values, weight):
    row_count = values.shape[0]
    size = weight.shape[1]
    heads = weight.shape[0] // size
    return jnp.einsum(
        "thj,hjk->thk",
        values.reshape(row_count, heads, size),
        weight.reshape(heads, size, size),
        preferred_element_type=jnp.float32,
    ).reshape(row_count, heads * size)


def block_terms(values, grad_vals, size):
    row_count = values.shape[0]
    heads = values.shape[1] // size
    terms = jnp.einsum(
        "thj,thk->hjk",
        values.reshape(row_count, heads, size),
        grad_vals.reshape(row_count, heads, size),
        preferred_element_type=jnp.float32,
    )
    return terms.reshape(heads * size, size)


def block_back(grad_vals, weight):
    row_count = grad_vals.shape[0]
    size = weight.shape[1]
    heads = weight.shape[0] // size
    return jnp.einsum(
        "thk,hjk->thj",
        grad_vals.reshape(row_count, heads, size),
        weight.reshape(heads, size, size),
        preferred_element_type=jnp.float32,
    ).reshape(row_count, heads * size)


def per_device_general(
    tokens,
    lengths,
    cotangent,
    norm1_gain,
    gate_in,
    linear_in,
    conv_kernel,
    conv_bias,
    rate_weight,
    rate_bias,
    input_weight,
    input_bias,
    decay_param,
    out_proj,
    norm2_gain,
    mlp_gate,
    mlp_up,
    mlp_down,
):
    row_count = tokens.shape[0]
    segment_ids, live_rows = layout(lengths[0], row_count)
    live_col = live_rows[:, None]
    mixer_full = (
        lax.all_gather(norm1_gain, "shard", axis=0, tiled=True),
        lax.all_gather(gate_in, "shard", axis=0, tiled=True),
        lax.all_gather(linear_in, "shard", axis=0, tiled=True),
        lax.all_gather(conv_kernel, "shard", axis=1, tiled=True),
        lax.all_gather(conv_bias, "shard", axis=0, tiled=True),
        lax.all_gather(rate_weight, "shard", axis=0, tiled=True),
        lax.all_gather(rate_bias, "shard", axis=0, tiled=True),
        lax.all_gather(input_weight, "shard", axis=0, tiled=True),
        lax.all_gather(input_bias, "shard", axis=0, tiled=True),
        lax.all_gather(decay_param, "shard", axis=0, tiled=True),
        lax.all_gather(out_proj, "shard", axis=0, tiled=True),
    )
    gain_first = mixer_full[0].astype(jnp.float32)
    kernel_full = mixer_full[3].astype(jnp.float32)
    kernel_shift = mixer_full[4].astype(jnp.float32)
    rate_shift = mixer_full[6].astype(jnp.float32)
    input_shift = mixer_full[8].astype(jnp.float32)
    decay_full = mixer_full[9].astype(jnp.float32)
    block_size = mixer_full[5].shape[1]
    masked_in = tokens.astype(jnp.float32) * live_col
    normed_low = normalize(masked_in, gain_first).astype(jnp.bfloat16)
    gate_pre = product(normed_low, mixer_full[1])
    linear_out = product(normed_low, mixer_full[2])
    gate_act = jax.nn.gelu(gate_pre)
    conv_out = convolve(linear_out, kernel_full, kernel_shift, segment_ids)
    conv_low = conv_out.astype(jnp.bfloat16)
    rate_pre = blocked(conv_low, mixer_full[5]) + rate_shift
    input_pre = blocked(conv_low, mixer_full[7]) + input_shift
    states = recurrence(rate_pre, input_pre, conv_out, decay_full, segment_ids)
    merged_low = (gate_act * states).astype(jnp.bfloat16)
    middle = masked_in + product(merged_low, mixer_full[10])
    mlp_full = (
        lax.all_gather(norm2_gain, "shard", axis=0, tiled=True),
        lax.all_gather(mlp_gate, "shard", axis=0, tiled=True),
        lax.all_gather(mlp_up, "shard", axis=0, tiled=True),
        lax.all_gather(mlp_down, "shard", axis=0, tiled=True),
    )
    gain_second = mlp_full[0].astype(jnp.float32)
    normed_two = normalize(middle, gain_second).astype(jnp.bfloat16)
    gate_mlp = product(normed_two, mlp_full[1])
    up_mlp = product(normed_two, mlp_full[2])
    hidden_low = gated_gelu(gate_mlp, up_mlp).astype(jnp.bfloat16)
    mixed_out = ((middle + product(hidden_low, mlp_full[3])) * live_col).astype(jnp.bfloat16)
    grad_out = cotangent.astype(jnp.float32) * live_col
    grad_down = grad_out.astype(jnp.bfloat16)
    again_mlp = (
        lax.all_gather(mlp_gate, "shard", axis=0, tiled=True),
        lax.all_gather(mlp_up, "shard", axis=0, tiled=True),
        lax.all_gather(mlp_down, "shard", axis=0, tiled=True),
    )
    term_down = contract(hidden_low, grad_down)
    part_down = lax.psum_scatter(
        term_down.astype(jnp.bfloat16), "shard", scatter_dimension=0, tiled=True
    ).astype(jnp.float32)
    grad_hidden = back_dot(grad_down, again_mlp[2])
    unused_val, hidden_back = jax.vjp(gated_gelu, gate_mlp, up_mlp)
    grad_gate_mlp, grad_up_mlp = hidden_back(grad_hidden)
    gate_mlp_low = grad_gate_mlp.astype(jnp.bfloat16)
    up_mlp_low = grad_up_mlp.astype(jnp.bfloat16)
    term_gate_mlp = contract(normed_two, gate_mlp_low)
    term_up_mlp = contract(normed_two, up_mlp_low)
    grad_normed_two = back_dot(gate_mlp_low, again_mlp[0]) + back_dot(up_mlp_low, again_mlp[1])
    unused_two, second_back = jax.vjp(normalize, middle, gain_second)
    grad_middle_norm, term_gain_two = second_back(grad_normed_two)
    parts_mlp = (
        lax.psum_scatter(
            term_gain_two.astype(jnp.bfloat16), "shard", scatter_dimension=0, tiled=True
        ).astype(jnp.float32),
        lax.psum_scatter(
            term_gate_mlp.astype(jnp.bfloat16), "shard", scatter_dimension=0, tiled=True
        ).astype(jnp.float32),
        lax.psum_scatter(
            term_up_mlp.astype(jnp.bfloat16), "shard", scatter_dimension=0, tiled=True
        ).astype(jnp.float32),
    )
    grad_middle = grad_out + grad_middle_norm
    grad_mix_low = grad_middle.astype(jnp.bfloat16)
    again_mixer = (
        lax.all_gather(gate_in, "shard", axis=0, tiled=True),
        lax.all_gather(linear_in, "shard", axis=0, tiled=True),
        lax.all_gather(rate_weight, "shard", axis=0, tiled=True),
        lax.all_gather(input_weight, "shard", axis=0, tiled=True),
        lax.all_gather(out_proj, "shard", axis=0, tiled=True),
    )
    term_out = contract(merged_low, grad_mix_low)
    grad_merged = back_dot(grad_mix_low, again_mixer[4])
    grad_states = grad_merged * gate_act
    unused_three, gelu_back = jax.vjp(jax.nn.gelu, gate_pre)
    gate_low = gelu_back(grad_merged * states)[0].astype(jnp.bfloat16)
    unused_four, scan_back = jax.vjp(
        partial(recurrence, segment_ids=segment_ids), rate_pre, input_pre, conv_out, decay_full
    )
    grad_rate, grad_input, grad_flow, term_decay = scan_back(grad_states)
    rate_low = grad_rate.astype(jnp.bfloat16)
    input_low = grad_input.astype(jnp.bfloat16)
    term_rate = block_terms(conv_low, rate_low, block_size)
    term_input = block_terms(conv_low, input_low, block_size)
    term_rate_shift = jnp.sum(rate_low.astype(jnp.float32), axis=0)
    term_input_shift = jnp.sum(input_low.astype(jnp.float32), axis=0)
    grad_conv = (
        grad_flow + block_back(rate_low, again_mixer[2]) + block_back(input_low, again_mixer[3])
    )
    unused_five, conv_back = jax.vjp(
        partial(convolve, segment_ids=segment_ids), linear_out, kernel_full, kernel_shift
    )
    grad_linear, term_kernel, term_kernel_shift = conv_back(grad_conv)
    linear_low = grad_linear.astype(jnp.bfloat16)
    term_gate_in = contract(normed_low, gate_low)
    term_linear = contract(normed_low, linear_low)
    grad_normed = back_dot(gate_low, again_mixer[0]) + back_dot(linear_low, again_mixer[1])
    unused_six, first_back = jax.vjp(normalize, masked_in, gain_first)
    grad_masked, term_gain_one = first_back(grad_normed)
    grad_tokens = ((grad_middle + grad_masked) * live_col).astype(jnp.bfloat16)
    small_terms = (
        term_gain_one,
        term_kernel,
        term_kernel_shift,
        term_rate,
        term_rate_shift,
        term_input,
        term_input_shift,
        term_decay,
    )
    placed = tuple((term for term in small_terms))
    mixer_terms = (
        placed[0],
        term_gate_in,
        term_linear,
        placed[1],
        placed[2],
        placed[3],
        placed[4],
        placed[5],
        placed[6],
        placed[7],
        term_out,
    )
    parts_mixer = (
        lax.psum_scatter(
            mixer_terms[0].astype(jnp.bfloat16), "shard", scatter_dimension=0, tiled=True
        ).astype(jnp.float32),
        lax.psum_scatter(
            mixer_terms[1].astype(jnp.bfloat16), "shard", scatter_dimension=0, tiled=True
        ).astype(jnp.float32),
        lax.psum_scatter(
            mixer_terms[2].astype(jnp.bfloat16), "shard", scatter_dimension=0, tiled=True
        ).astype(jnp.float32),
        lax.psum_scatter(
            mixer_terms[3].astype(jnp.bfloat16), "shard", scatter_dimension=1, tiled=True
        ).astype(jnp.float32),
        lax.psum_scatter(
            mixer_terms[4].astype(jnp.bfloat16), "shard", scatter_dimension=0, tiled=True
        ).astype(jnp.float32),
        lax.psum_scatter(
            mixer_terms[5].astype(jnp.bfloat16), "shard", scatter_dimension=0, tiled=True
        ).astype(jnp.float32),
        lax.psum_scatter(
            mixer_terms[6].astype(jnp.bfloat16), "shard", scatter_dimension=0, tiled=True
        ).astype(jnp.float32),
        lax.psum_scatter(
            mixer_terms[7].astype(jnp.bfloat16), "shard", scatter_dimension=0, tiled=True
        ).astype(jnp.float32),
        lax.psum_scatter(
            mixer_terms[8].astype(jnp.bfloat16), "shard", scatter_dimension=0, tiled=True
        ).astype(jnp.float32),
        lax.psum_scatter(
            mixer_terms[9].astype(jnp.bfloat16), "shard", scatter_dimension=0, tiled=True
        ).astype(jnp.float32),
        lax.psum_scatter(
            mixer_terms[10].astype(jnp.bfloat16), "shard", scatter_dimension=0, tiled=True
        ).astype(jnp.float32),
    )
    shard_parts = tuple(parts_mixer) + (parts_mlp[0], parts_mlp[1], parts_mlp[2], part_down)
    totals = jax.tree.map(
        lambda part: part.astype(jnp.float32), lax.psum(as_sent(shard_parts), "group")
    )
    return (mixed_out, grad_tokens) + tuple(totals)


def solution(mesh):
    placed = (
        P(("group", "shard"), None),
        P(("group", "shard"), None),
        P(("group", "shard"), None),
        P("shard"),
        P("shard", None),
        P("shard", None),
        P(None, "shard"),
        P("shard"),
        P("shard", None),
        P("shard"),
        P("shard", None),
        P("shard"),
        P("shard"),
        P("shard", None),
        P("shard"),
        P("shard", None),
        P("shard", None),
        P("shard", None),
    )
    split_fits = FAST_MESH == tuple(mesh.shape[axis] for axis in ("group", "shard"))
    return jax.shard_map(
        per_device_split if split_fits else per_device_general,
        mesh=mesh,
        in_specs=placed,
        out_specs=(
            P(("group", "shard"), None),
            P(("group", "shard"), None),
            P("shard"),
            P("shard", None),
            P("shard", None),
            P(None, "shard"),
            P("shard"),
            P("shard", None),
            P("shard"),
            P("shard", None),
            P("shard"),
            P("shard"),
            P("shard", None),
            P("shard"),
            P("shard", None),
            P("shard", None),
            P("shard", None),
        ),
        check_vma=False,
    )
```

```python
from functools import partial

import jax
import jax.numpy as jnp
from jax import lax
from jax.experimental import pallas as pl
from jax.experimental.pallas import tpu as pltpu
from jax.sharding import PartitionSpec as P

FAST_MESH = (4, 8)
RATE_SCALE = 8.0
EPSILON = 1e-06
F32 = jnp.float32
BF16 = jnp.bfloat16
GELU_C = 0.7978845608028654
GELU_K = 0.044715
CAP = 128


def positions_in_run(counts, row_count):
    first = counts[0]
    second = first + counts[1]
    third = second + counts[2]
    rows = lax.broadcasted_iota(jnp.int32, (row_count, 1), 0)
    start = jnp.where(rows >= first, first, 0)
    start = jnp.where(rows >= second, second, start)
    start = jnp.where(rows >= third, third, start)
    return rows - start, (rows < third).astype(F32)


def gelu_parts(x):
    t = jnp.tanh(GELU_C * (x + GELU_K * x * x * x))
    value = 0.5 * x * (1.0 + t)
    slope = 0.5 * (1.0 + t) + 0.5 * x * (1.0 - t * t) * GELU_C * (1.0 + 3.0 * GELU_K * x * x)
    return value, slope


def gelu_value(x):
    return 0.5 * x * (1.0 + jnp.tanh(GELU_C * (x + GELU_K * x * x * x)))


def sigmoid(x):
    return 0.5 * (1.0 + jnp.tanh(0.5 * x))


def one_less_exp(z):
    series = 1.0 - z * (1.0 / 7.0)
    for k in (6.0, 5.0, 4.0, 3.0, 2.0):
        series = 1.0 - z * (1.0 / k) * series
    return jnp.where(z < 0.35, z * series, 1.0 - jnp.exp(-z))


def softplus_neg(x):
    return jnp.maximum(-x, 0.0) + jnp.log1p(jnp.exp(-jnp.abs(x)))


def mm(a, b):
    return jnp.dot(a, b, preferred_element_type=F32)


def mm_nt(a, b):
    return lax.dot_general(a, b, (((1,), (1,)), ((), ())), preferred_element_type=F32)


def mm_tn(a, b):
    return lax.dot_general(a, b, (((0,), (0,)), ((), ())), preferred_element_type=F32)


def roll_rows(x, n):
    return pltpu.roll(x, n % x.shape[0], 0)


def conv_rows(linear, kernel, bias, masks):
    out = linear * kernel[0:1] + bias
    for k in range(1, 4):
        out = out + kernel[k : k + 1] * (roll_rows(linear, k) * masks[k - 1])
    return out


def decay_terms(rate_pre, decay):
    rate = sigmoid(rate_pre)
    keep = RATE_SCALE * rate * softplus_neg(decay)
    return rate, jnp.exp(-keep), jnp.sqrt(one_less_exp(2.0 * keep))


MESH_ID = pl.DeviceIdType.MESH
VMEM_LIMIT = 62 * 2**20
N_Z, N_X = 4, 2


def place():
    shard = lax.axis_index("shard")
    return lax.axis_index("group"), shard, shard // N_X, shard % N_X


def greet(peers):
    bar = pltpu.get_barrier_semaphore()
    count = 0
    for device, there in peers:
        if there is True:
            pl.semaphore_signal(bar, inc=1, device_id=device, device_id_type=MESH_ID)
            count = count + 1
        else:
            @pl.when(there)
            def _(device=device):
                pl.semaphore_signal(bar, inc=1, device_id=device, device_id_type=MESH_ID)
            count = count + there.astype(jnp.int32)
    pl.semaphore_wait(bar, count)


def line_peers():
    group, shard, z, x = place()
    return [
        ((group, shard + N_X), z < N_Z - 1),
        ((group, shard - N_X), z > 0),
        ((group, z * N_X + 1 - x), True),
    ]


class Gather:
    CHUNKS = 2

    @classmethod
    def scratch(cls):
        return [pltpu.SemaphoreType.DMA((3, N_Z, cls.CHUNKS)), pltpu.SemaphoreType.DMA((N_Z * N_X, cls.CHUNKS))]

    def __init__(self, buf, sems):
        self.buf, (self.send, self.recv) = buf, sems
        self.group, self.shard, self.z, self.x = place()
        self.rows = buf.shape[1] // self.CHUNKS

    def copy(self, origin, column, c, way):
        slot = origin * N_X + column
        z = (self.z + 1, self.z - 1, self.z)[way]
        x = 1 - self.x if way == 2 else self.x
        piece = self.buf.at[slot, pl.ds(c * self.rows, self.rows)]
        return pltpu.make_async_remote_copy(
            src_ref=piece, dst_ref=piece, send_sem=self.send.at[way, origin, c],
            recv_sem=self.recv.at[slot, c], device_id=(self.group, z * N_X + x), device_id_type=MESH_ID,
        )

    def start(self):
        for c in range(self.CHUNKS):
            self.forward(self.z, c, True, True)

    def forward(self, origin, c, up, down):
        if up:
            @pl.when(self.z < N_Z - 1)
            def _():
                self.copy(origin, self.x, c, 0).start()
        if down:
            @pl.when(self.z > 0)
            def _():
                self.copy(origin, self.x, c, 1).start()
        self.copy(origin, self.x, c, 2).start()

    def step(self, k):
        for c in range(self.CHUNKS):
            @pl.when(self.z >= k)
            def _(c=c):
                self.copy(self.z - k, self.x, c, 2).wait_recv()
                self.forward(self.z - k, c, True, False)

            @pl.when(self.z + k < N_Z)
            def _(c=c):
                self.copy(self.z + k, self.x, c, 2).wait_recv()
                self.forward(self.z + k, c, False, True)

    def wait_across(self, origin):
        for c in range(self.CHUNKS):
            self.copy(origin, 1 - self.x, c, 2).wait_recv()

    def finish(self):
        for c in range(self.CHUNKS):
            for origin in range(N_Z):
                @pl.when((self.z < N_Z - 1) & (origin <= self.z))
                def _():
                    self.copy(origin, self.x, c, 0).wait_send()

                @pl.when((self.z > 0) & (origin >= self.z))
                def _():
                    self.copy(origin, self.x, c, 1).wait_send()
                self.copy(origin, self.x, c, 2).wait_send()


class Scatter:
    CHUNKS = 2

    @classmethod
    def scratch(cls, rows, width):
        dma = pltpu.SemaphoreType.DMA
        return [
            pltpu.VMEM((N_Z, rows, width), BF16),
            pltpu.VMEM((N_Z + 1, rows, width), BF16),
            pltpu.VMEM((N_Z, rows, width), BF16),
            dma((2, N_Z, cls.CHUNKS)), dma((N_Z, cls.CHUNKS)), dma((N_Z + 1, cls.CHUNKS)),
        ]

    def __init__(self, parts, scratch):
        self.parts = parts
        self.across, self.along, self.held, self.send, self.recv_x, self.recv_z = scratch
        self.group, self.shard, self.z, self.x = place()
        self.rows = parts.shape[1] // self.CHUNKS

    def dest(self, i):
        low = jnp.minimum(self.z, N_Z - 1 - self.z)
        value = (N_Z - 1, N_Z - 2, jnp.where(low == 0, 1, 0), low)[i]
        return jnp.where(self.z >= N_Z // 2, N_Z - 1 - value, value)

    def span(self, c):
        return pl.ds(c * self.rows, self.rows)

    def copy_x(self, dest, c):
        return pltpu.make_async_remote_copy(
            src_ref=self.parts.at[dest * N_X + 1 - self.x, self.span(c)],
            dst_ref=self.across.at[dest, self.span(c)],
            send_sem=self.send.at[0, dest, c], recv_sem=self.recv_x.at[dest, c],
            device_id=(self.group, self.z * N_X + 1 - self.x), device_id_type=MESH_ID,
        )

    def copy_z(self, dest, slot, c, step):
        return pltpu.make_async_remote_copy(
            src_ref=self.held.at[dest, self.span(c)], dst_ref=self.along.at[slot, self.span(c)],
            send_sem=self.send.at[1, dest, c], recv_sem=self.recv_z.at[slot, c],
            device_id=(self.group, (self.z + step) * N_X + self.x), device_id_type=MESH_ID,
        )

    def start(self, i):
        for c in range(self.CHUNKS):
            self.copy_x(self.dest(i), c).start()

    def arrived(self, slot, c):
        self.copy_z(0, slot, c, 0).wait_recv()
        return self.along[slot, self.span(c)].astype(F32)

    def step(self, i):
        dest = self.dest(i)
        for c in range(self.CHUNKS):
            self.copy_x(dest, c).wait_recv()
            own = dest * N_X + self.x
            self.held[dest, self.span(c)] = (
                self.parts[own, self.span(c)].astype(F32) + self.across[dest, self.span(c)].astype(F32)
            ).astype(BF16)

            @pl.when(((dest > self.z) & (self.z > 0)) | ((dest < self.z) & (self.z < N_Z - 1)))
            def _(c=c):
                self.held[dest, self.span(c)] = (
                    self.parts[own, self.span(c)].astype(F32) + self.across[dest, self.span(c)].astype(F32)
                    + self.arrived(dest, c)
                ).astype(BF16)

            @pl.when(dest > self.z)
            def _(c=c):
                self.copy_z(dest, dest, c, 1).start()

            @pl.when(dest < self.z)
            def _(c=c):
                self.copy_z(dest, jnp.where(dest == self.z - 1, N_Z, dest), c, -1).start()

    def last(self, out):
        for c in range(self.CHUNKS):
            self.copy_x(self.z, c).wait_recv()
            out[self.span(c)] = self.parts[self.shard, self.span(c)].astype(F32) + self.across[self.z, self.span(c)].astype(F32)

            @pl.when(self.z > 0)
            def _(c=c):
                out[self.span(c)] += self.arrived(self.z, c)

            @pl.when(self.z < N_Z - 1)
            def _(c=c):
                out[self.span(c)] += self.arrived(N_Z, c)

    def finish(self):
        for c in range(self.CHUNKS):
            for dest in range(N_Z):
                self.copy_x(dest, c).wait_send()

                @pl.when(dest != self.z)
                def _():
                    self.copy_z(dest, 0, c, 0).wait_send()


class Exchange:
    @classmethod
    def scratch(cls, blocks, count):
        dma = pltpu.SemaphoreType.DMA
        return [dma((count, blocks)), dma((count, blocks)), dma((3, count, blocks)), dma((3, count, blocks))]

    def __init__(self, sources, views, blocks, sems):
        self.sources, self.views, self.blocks = sources, views, blocks
        self.send_first, self.recv_first, self.send, self.recv = sems
        self.group, self.shard, _, _ = place()
        self.home = self.shard if blocks > 1 else 0
        self.core_mate, self.y_mate = mates()
        self.count = len(sources)

    def first(self, j, to, origin):
        return pltpu.make_async_remote_copy(
            src_ref=self.sources[j](to), dst_ref=self.views[j](origin, self.group),
            send_sem=self.send_first.at[j, to], recv_sem=self.recv_first.at[j, origin],
            device_id=(self.group, to), device_id_type=MESH_ID,
        )

    def own(self, j):
        return pltpu.make_async_copy(
            self.sources[j](self.home), self.views[j](self.home, self.group), self.recv_first.at[j, self.home]
        )

    def pass_on(self, j, origin, quarter, mate, way):
        piece = self.views[j](origin, quarter)
        return pltpu.make_async_remote_copy(
            src_ref=piece, dst_ref=piece, send_sem=self.send.at[way, j, origin], recv_sem=self.recv.at[way, j, origin],
            device_id=(mate, self.shard), device_id_type=MESH_ID,
        )

    def others(self, body):
        if self.blocks > 1:
            pl.loop(1, self.blocks)(lambda i: body((self.home + i) % self.blocks))

    def start(self):
        for j in range(self.count):
            self.own(j).start()

        def send(to):
            for j in range(self.count):
                self.first(j, to, self.home).start()

        self.others(send)

    def both(self, j, origin):
        self.pass_on(j, origin, self.group, self.y_mate, 1).start()
        self.pass_on(j, origin, self.group, self.core_mate, 0).start()

    def spread(self):
        for j in range(self.count):
            self.own(j).wait()
            self.both(j, self.home)

        def forward(origin):
            for j in range(self.count):
                self.first(j, origin, origin).wait_recv()
                self.both(j, origin)

        self.others(forward)

    def each(self, body):
        for j in range(self.count):
            body(j, self.home)

        def rest(origin):
            for j in range(self.count):
                body(j, origin)

        self.others(rest)

    def relay(self):
        def forward(j, origin):
            self.pass_on(j, origin, self.y_mate, self.core_mate, 1).wait_recv()
            self.pass_on(j, origin, self.y_mate, self.core_mate, 2).start()

        self.each(forward)

    def arrive(self):
        def wait(j, origin):
            self.pass_on(j, origin, self.group, self.core_mate, 0).wait_recv()
            self.pass_on(j, origin, self.group, self.core_mate, 2).wait_recv()

        self.each(wait)

    def finish(self):
        def sent(to):
            for j in range(self.count):
                self.first(j, to, self.home).wait_send()

        def passed(j, origin):
            for way in range(3):
                self.pass_on(j, origin, self.group, self.core_mate, way).wait_send()

        self.others(sent)
        self.each(passed)


def mates():
    group = lax.axis_index("group")
    return group + 1 - 2 * (group % 2), group + 2 - 4 * (group // 2)


def all_peers():
    group, shard, _, _ = place()
    core_mate, y_mate = mates()
    others = [((group, (shard + i) % (N_Z * N_X)), True) for i in range(1, N_Z * N_X)]
    return others + [((core_mate, shard), True), ((y_mate, shard), True)]


def mixer_forward(linear, gate, pos, vec, gates):
    masks = [(pos >= k).astype(F32) for k in (1, 2, 3)]
    conv = conv_rows(linear, vec[0:4], vec[4:5], masks)
    width = linear.shape[1]
    both = mm(conv.astype(BF16), gates)
    rate_pre = both[:, :width] + vec[5:6]
    input_pre = both[:, width:] + vec[6:7]
    _, a, weight_in = decay_terms(rate_pre, vec[7:8])
    mult = a * masks[0]
    total = weight_in * sigmoid(input_pre) * conv
    step = 1
    while step < CAP:
        total = total + mult * roll_rows(total, step)
        if 2 * step < CAP:
            mult = mult * roll_rows(mult, step)
        step *= 2
    return rate_pre, input_pre, total, (gelu_value(gate) * total).astype(BF16)


def rms_scale(values):
    return lax.rsqrt(jnp.mean(values * values, axis=1, keepdims=True) + EPSILON)


def forward_kernel(
    lengths_ref, tokens_ref, gains_ref, vec_ref, gates_ref, out_proj_ref, gate_in_ref, linear_in_ref, mlp_gate_ref, mlp_up_ref,
    gather_out, weights_out, mlp_out, gains_out, saved_out, merged_out, middle_ref, normed_two_ref,
    buf, weights, quarter, raw, masked, saved, merged, parts,
    gather_a, gather_b, ex_a, ex_b, ex_c, ex_d, mx_a, mx_b, mx_c, mx_d, *rest,
):
    scatter_scratch, (gain_send, gain_recv, raw_sem, out_sem, pair_sem) = rest[:-5], rest[-5:]
    group, shard, z, x = place()
    shards = N_Z * N_X
    rows, width = tokens_ref.shape
    quarter_rows = raw.shape[1]
    chans = linear_in_ref.shape[1] // shards
    padded = vec_ref.shape[1]
    fetch = [
        pltpu.make_async_copy(ref.at[pl.ds(group * quarter_rows, quarter_rows)], raw.at[i], raw_sem.at[i])
        for i, ref in enumerate((gate_in_ref, linear_in_ref))
    ]
    for copy in fetch:
        copy.start()
    greet(all_peers())

    def gain_copy(to, origin):
        return pltpu.make_async_remote_copy(
            src_ref=gains_ref, dst_ref=gains_out.at[origin], send_sem=gain_send.at[to], recv_sem=gain_recv.at[origin],
            device_id=(group, to), device_id_type=MESH_ID,
        )

    for i in range(1, shards):
        gain_copy((shard + i) % shards, shard).start()
    gains_out[shard] = gains_ref[...]
    inside = lax.broadcasted_iota(jnp.int32, (quarter_rows, padded), 1) < chans
    for i, copy in enumerate(fetch):
        copy.wait()
        for to in range(shards):
            piece = raw[i, :, to * chans : (to + 1) * chans].astype(F32)
            piece = jnp.concatenate([piece, jnp.zeros((quarter_rows, padded - chans), F32)], axis=1)
            quarter[to, :, i * padded : (i + 1) * padded] = piece.astype(BF16)
    exchange = Exchange(
        [lambda to: quarter.at[to]], [lambda origin, q: weights.at[origin, q]], shards, (ex_a, ex_b, ex_c, ex_d)
    )
    exchange.start()
    hidden = mlp_up_ref.shape[1] // shards

    def part_of(ref):
        return lambda to: ref.at[pl.ds(group * quarter_rows, quarter_rows), pl.ds(to * hidden, hidden)]

    mlp_exchange = Exchange(
        [part_of(mlp_gate_ref), part_of(mlp_up_ref)],
        [lambda origin, q: mlp_out.at[origin, q, :, 0:hidden], lambda origin, q: mlp_out.at[origin, q, :, hidden : 2 * hidden]],
        shards, (mx_a, mx_b, mx_c, mx_d),
    )
    pos, live = positions_in_run([lengths_ref[0, i] for i in range(3)], rows)
    masked[...] = tokens_ref[...].astype(F32) * live
    for i in range(1, shards):
        gain_copy(shard, (shard + i) % shards).wait_recv()
    gains = jnp.concatenate([gains_out[i] for i in range(shards)], axis=1)
    gather = Gather(buf, (gather_a, gather_b))
    buf[shard, :, :width] = (masked[...] * rms_scale(masked[...]) * gains[0:1]).astype(BF16)
    buf[shard, :, width:] = jnp.broadcast_to(pos.astype(F32).astype(BF16), (rows, buf.shape[2] - width))
    gather.start()
    gather.step(1)
    exchange.spread()
    gather.step(2)
    exchange.relay()
    mlp_exchange.start()
    exchange.arrive()
    scatter = Scatter(parts, scatter_scratch)

    def pair_copies(origin):
        return [
            pltpu.make_async_copy(saved.at[origin], saved_out.at[origin], pair_sem.at[0, origin]),
            pltpu.make_async_copy(merged.at[origin], merged_out.at[origin], pair_sem.at[1, origin]),
        ]

    @pl.loop(0, N_Z)
    def _(i):
        @pl.when(i == 1)
        def _():
            gather.step(3)

        origin = nearest(z, i)
        gather.wait_across(origin)
        pair = pl.ds(origin * N_X, N_X)
        both = buf[pair].reshape(N_X * rows, buf.shape[2])
        pre = mm(both[:, :width], weights[...].reshape(width, 2 * padded))
        gate, linear = pre[:, :padded], pre[:, padded:]
        where = both[:, width : width + 1].astype(F32)
        rate_pre, input_pre, state, merge = mixer_forward(linear, gate, where, vec_ref[...], gates_ref[...])
        for j, value in enumerate((gate, linear, rate_pre, input_pre, state)):
            saved[origin, j] = value
        merged[origin] = merge
        for copy in pair_copies(origin):
            copy.start()
        parts[pair] = mm(merge[:, :chans], out_proj_ref[...]).astype(BF16).reshape(N_X, rows, width)

    outs = [
        pltpu.make_async_copy(buf, gather_out, out_sem.at[0]),
        pltpu.make_async_copy(weights, weights_out, out_sem.at[1]),
    ]
    for copy in outs:
        copy.start()
    for i in range(N_Z):
        scatter.start(i)
    mlp_exchange.spread()
    scatter.step(0)
    mlp_exchange.relay()
    scatter.step(1)
    scatter.step(2)
    scatter.last(middle_ref)
    middle_ref[...] += masked[...]
    normed_two_ref[...] = (middle_ref[...] * rms_scale(middle_ref[...]) * gains[1:2]).astype(BF16)
    for i in range(1, shards):
        gain_copy((shard + i) % shards, shard).wait_send()
    gather.finish()
    exchange.finish()
    mlp_exchange.arrive()
    mlp_exchange.finish()
    scatter.finish()
    for copy in outs:
        copy.wait()

    @pl.loop(0, N_Z)
    def _(origin):
        for copy in pair_copies(origin):
            copy.wait()


def nearest(z, i):
    low = jnp.minimum(z, N_Z - 1 - z)
    value = jnp.where(low == 0, i, jnp.where(i == 0, 1, jnp.where(i == 1, 0, i)))
    return jnp.where(z >= N_Z // 2, N_Z - 1 - value, value)


def any_spec():
    return pl.BlockSpec(memory_space=pl.ANY)


def vmem_spec():
    return pl.BlockSpec(memory_space=pltpu.VMEM)


def forward_call(lengths, tokens, gains, vec, gates, out_proj, gate_in, linear_in, mlp_gate, mlp_up):
    rows, width = tokens.shape
    shards, groups = lax.axis_size("shard"), lax.axis_size("group")
    padded = vec.shape[1]
    quarter_rows = gate_in.shape[0] // groups
    hidden = mlp_up.shape[1] // shards
    dma = pltpu.SemaphoreType.DMA
    shape = jax.ShapeDtypeStruct
    out_shape = [
        shape((shards, rows, width + 128), BF16),
        shape((shards, groups, quarter_rows, 2 * padded), BF16),
        shape((shards, groups, quarter_rows, 2 * hidden), BF16),
        shape((shards,) + gains.shape, F32),
        shape((N_Z, 5, N_X * rows, padded), F32),
        shape((N_Z, N_X * rows, padded), BF16),
        shape((rows, width), F32),
        shape((rows, width), BF16),
    ]
    return pl.pallas_call(
        forward_kernel,
        out_shape=out_shape,
        in_specs=[pl.BlockSpec(memory_space=pltpu.SMEM)] + [vmem_spec()] * 5 + [any_spec()] * 4,
        out_specs=[any_spec()] * 3 + [vmem_spec()] + [any_spec()] * 2 + [vmem_spec()] * 2,
        scratch_shapes=[
            pltpu.VMEM((shards, rows, width + 128), BF16),
            pltpu.VMEM((shards, groups, quarter_rows, 2 * padded), BF16),
            pltpu.VMEM((shards, quarter_rows, 2 * padded), BF16),
            pltpu.VMEM((2, quarter_rows, gate_in.shape[1]), BF16),
            pltpu.VMEM((rows, width), F32),
            pltpu.VMEM((N_Z, 5, N_X * rows, padded), F32),
            pltpu.VMEM((N_Z, N_X * rows, padded), BF16),
            pltpu.VMEM((shards, rows, width), BF16),
        ]
        + Gather.scratch()
        + Exchange.scratch(shards, 1)
        + Exchange.scratch(shards, 2)
        + Scatter.scratch(rows, width)
        + [dma((shards,)), dma((shards,)), dma((2,)), dma((2,)), dma((2, N_Z))],
        compiler_params=pltpu.CompilerParams(collective_id=1, has_side_effects=True, vmem_limit_bytes=VMEM_LIMIT),
        name="mixer_forward",
    )(lengths, tokens, gains, vec, gates, out_proj, gate_in, linear_in, mlp_gate, mlp_up)


class CoreSum:
    @classmethod
    def scratch(cls, count):
        return [pltpu.SemaphoreType.DMA((count, 2))] * 2

    def __init__(self, terms, arrived, sums, sems):
        self.terms, self.arrived, self.sums = terms, arrived, sums
        self.send, self.recv = sems
        group, self.shard, _, _ = place()
        self.core, self.y = group % 2, group // 2
        self.core_mate, _ = mates()

    def copy(self, j, half):
        return pltpu.make_async_remote_copy(
            src_ref=self.terms[j].at[2 * half + 1 - self.core], dst_ref=self.arrived[j].at[half],
            send_sem=self.send.at[j, half], recv_sem=self.recv.at[j, half],
            device_id=(self.core_mate, self.shard), device_id_type=MESH_ID,
        )

    def start(self):
        for half in (1 - self.y, self.y):
            for j in range(len(self.terms)):
                self.copy(j, half).start()

    def add(self, half):
        for j in range(len(self.terms)):
            self.copy(j, half).wait_recv()
            own = self.sums[j](half)

            @pl.loop(0, self.arrived[j].shape[1])
            def _(i, j=j, own=own):
                own[i] = (own[i].astype(F32) + self.arrived[j][half, i].astype(F32)).astype(BF16)

    def finish(self):
        for half in (0, 1):
            for j in range(len(self.terms)):
                self.copy(j, half).wait_send()


class LineSum:
    @classmethod
    def scratch(cls, count):
        return [pltpu.SemaphoreType.DMA((count,))] * 2

    def __init__(self, halves, arrived, sums, sems):
        self.halves, self.arrived, self.sums = halves, arrived, sums
        self.send, self.recv = sems
        group, self.shard, _, _ = place()
        self.y = group // 2
        _, self.y_mate = mates()

    def copy(self, j):
        return pltpu.make_async_remote_copy(
            src_ref=self.halves[j].at[1 - self.y], dst_ref=self.arrived[j],
            send_sem=self.send.at[j], recv_sem=self.recv.at[j],
            device_id=(self.y_mate, self.shard), device_id_type=MESH_ID,
        )

    def start(self):
        for j in range(len(self.halves)):
            self.copy(j).start()

    def add(self):
        for j in range(len(self.halves)):
            self.copy(j).wait_recv()
            own = self.sums[j]

            @pl.loop(0, self.arrived[j].shape[0])
            def _(i, j=j, own=own):
                own[i] = (own[i].astype(F32) + self.arrived[j][i].astype(F32)).astype(BF16)

    def finish(self):
        for j in range(len(self.halves)):
            self.copy(j).wait_send()


def split_gains(ref, row, values):
    size = ref.shape[2]
    for i in range(ref.shape[0]):
        ref[i, row : row + 1] = values[:, i * size : (i + 1) * size]


def norm_backward(values, gain, grad):
    scale = rms_scale(values)
    e = grad * gain
    back = scale * e - values * (scale * scale * scale) * jnp.mean(values * e, axis=1, keepdims=True)
    return back, jnp.sum(grad * values * scale, axis=0, keepdims=True)


def mlp_kernel(
    lengths_ref, normed_ref, cotangent_ref, middle_ref, gains_ref, weights_ref, down_ref,
    mixed_out, half_gu_out, half_down_out, g_middle_ref, gain_ref,
    normed, g_low, weights, down, act, slope, hidden, grads, parts, term_gu, term_down, core_gu, core_down,
    a_send, a_recv, b_send, b_recv, core_send, core_recv, load_sem, part_sem, out_sem, *scatter_scratch,
):
    _, shard, z, x = place()
    group = lax.axis_index("group")
    core_mate, _ = mates()
    rows, width = normed_ref.shape
    size = hidden.shape[2]
    loads = [
        pltpu.make_async_copy(weights_ref, weights, load_sem.at[0]),
        pltpu.make_async_copy(down_ref, down, load_sem.at[1]),
    ]
    for copy in loads:
        copy.start()
    gather = Gather(normed, (a_send, a_recv))
    gather_g = Gather(g_low, (b_send, b_recv))
    scatter = Scatter(parts, scatter_scratch)
    core_sum = CoreSum(
        [term_gu, term_down], [core_gu, core_down],
        [lambda half: term_gu.at[2 * half + group % 2], lambda half: term_down.at[2 * half + group % 2]],
        (core_send, core_recv),
    )
    greet(line_peers() + [((core_mate, shard), True)])
    normed[shard] = normed_ref[...]
    gather.start()
    _, live = positions_in_run([lengths_ref[0, i] for i in range(3)], rows)
    g_low[shard] = (cotangent_ref[...].astype(F32) * live).astype(BF16)
    gather.step(1)
    gather.step(2)
    for copy in loads:
        copy.wait()

    def part_copy(origin):
        pair = pl.ds(origin * N_X, N_X)
        return pltpu.make_async_copy(parts.at[pair], mixed_out.at[pair], part_sem.at[origin])

    @pl.loop(0, N_Z)
    def _(i):
        @pl.when(i == 1)
        def _():
            gather.step(3)
            gather_g.start()

        origin = nearest(z, i)
        gather.wait_across(origin)
        pair = pl.ds(origin * N_X, N_X)
        both = mm(normed[pair].reshape(N_X * rows, width), weights[...].reshape(width, 2 * size))
        value, inclined = gelu_parts(both[:, :size])
        up = both[:, size:]
        act[origin] = value
        slope[origin] = up * inclined
        hidden[origin] = (value * up).astype(BF16)
        parts[pair] = mm(hidden[origin], down[...]).astype(BF16).reshape(N_X, rows, width)
        part_copy(origin).start()

    gather_g.step(1)
    gather_g.step(2)

    @pl.loop(0, N_Z)
    def _(i):
        @pl.when(i == 1)
        def _():
            gather_g.step(3)

        origin = nearest(z, i)
        gather_g.wait_across(origin)
        pair = pl.ds(origin * N_X, N_X)
        g_hidden = mm_nt(g_low[pair].reshape(N_X * rows, width), down[...])
        grads[origin, :, :size] = (g_hidden * slope[origin]).astype(BF16)
        grads[origin, :, size:] = (g_hidden * act[origin]).astype(BF16)
        part_copy(origin).wait()
        back = mm_nt(grads[origin], weights[...].reshape(width, 2 * size))
        parts[pair] = back.astype(BF16).reshape(N_X, rows, width)

    for i in range(N_Z):
        scatter.start(i)
    tile = normed.shape[2] // (N_Z * N_X)
    total = N_Z * N_X * rows

    @pl.loop(0, size // tile)
    def _(i):
        left = hidden[:, :, pl.ds(i * tile, tile)].reshape(total, tile)
        term = mm_tn(left, g_low[...].reshape(total, width)).astype(BF16)
        step = term_down.shape[2]
        for j in range(tile // step):
            chunk = i * (tile // step) + j
            term_down[chunk // term_down.shape[1], chunk % term_down.shape[1]] = term[j * step : (j + 1) * step]

    def gu_terms(first, last):
        @pl.loop(first, last)
        def _(i):
            left = normed[:, :, pl.ds(i * tile, tile)].reshape(total, tile)
            term = mm_tn(left, grads[...].reshape(total, 2 * size)).astype(BF16)
            term_gu[:, i] = term.reshape(term_gu.shape[0], term_gu.shape[2], 2 * size)

    scatter.step(0)
    gu_terms(0, N_Z)
    scatter.step(1)
    gu_terms(N_Z, 2 * N_Z)
    core_sum.start()
    scatter.step(2)
    outs = []
    y = group // 2
    for half in (1 - y, y):
        core_sum.add(half)
        for j, (term, out) in enumerate(((term_gu, half_gu_out), (term_down, half_down_out))):
            outs.append(pltpu.make_async_copy(term.at[2 * half + group % 2], out.at[half], out_sem.at[j, half]))
            outs[-1].start()
    scatter.last(g_middle_ref)
    gain = jnp.concatenate([gains_ref[i] for i in range(N_Z * N_X)], axis=1)[1:2]
    back, gain_term = norm_backward(middle_ref[...], gain, g_middle_ref[...])
    g_middle_ref[...] = g_low[shard].astype(F32) + back
    gain_ref[...] = jnp.zeros_like(gain_ref)
    split_gains(gain_ref, 1, gain_term)
    gather.finish()
    gather_g.finish()
    core_sum.finish()
    scatter.finish()
    for copy in outs:
        copy.wait()


def mlp_call(lengths, normed, cotangent, middle, gains, weights, down):
    rows, width = normed.shape
    shards, groups, quarter_rows, both = weights.shape
    size = down.shape[0]
    dma = pltpu.SemaphoreType.DMA
    shape = jax.ShapeDtypeStruct
    down_term = (size // groups // 64, 64, width)
    gu_term = (shards, quarter_rows, both)
    pairs = (N_Z, N_X * rows)
    return pl.pallas_call(
        mlp_kernel,
        out_shape=[
            shape((shards, rows, width), BF16),
            shape((2,) + gu_term, BF16),
            shape((2,) + down_term, BF16),
            shape((rows, width), F32),
            shape(gains.shape, F32),
        ],
        in_specs=[pl.BlockSpec(memory_space=pltpu.SMEM)] + [vmem_spec()] * 4 + [any_spec()] * 2,
        out_specs=[any_spec()] * 3 + [vmem_spec()] * 2,
        scratch_shapes=[
            pltpu.VMEM((shards, rows, width), BF16),
            pltpu.VMEM((shards, rows, width), BF16),
            pltpu.VMEM(weights.shape, BF16),
            pltpu.VMEM(down.shape, BF16),
            pltpu.VMEM(pairs + (size,), F32),
            pltpu.VMEM(pairs + (size,), F32),
            pltpu.VMEM(pairs + (size,), BF16),
            pltpu.VMEM(pairs + (both,), BF16),
            pltpu.VMEM((shards, rows, width), BF16),
            pltpu.VMEM((groups,) + gu_term, BF16),
            pltpu.VMEM((groups,) + down_term, BF16),
            pltpu.VMEM((2,) + gu_term, BF16),
            pltpu.VMEM((2,) + down_term, BF16),
        ]
        + Gather.scratch()
        + Gather.scratch()
        + CoreSum.scratch(2)
        + [dma((2,)), dma((N_Z,)), dma((2, 2))]
        + Scatter.scratch(rows, width),
        compiler_params=pltpu.CompilerParams(collective_id=2, has_side_effects=True, vmem_limit_bytes=VMEM_LIMIT),
        name="mlp",
    )(lengths, normed, cotangent, middle, gains, weights, down)


def mixer_backward(g_merged, saved, pos, vec, gates):
    gate, linear, rate_pre, input_pre, state = saved
    width = linear.shape[1]
    masks = [(pos >= k).astype(F32) for k in (1, 2, 3)]
    later = [roll_rows(jnp.broadcast_to(masks[k - 1], linear.shape), -k) for k in (1, 2, 3)]
    conv = conv_rows(linear, vec[0:4], vec[4:5], masks)
    input_gate = sigmoid(input_pre)
    decay = vec[7:8]
    rate, a, weight_in = decay_terms(rate_pre, decay)
    act, slope = gelu_parts(gate)
    g_gate = (g_merged * state * slope).astype(BF16)
    lam = g_merged * act
    mult = roll_rows(a, -1) * later[0]
    step = 1
    while step < CAP:
        lam = lam + mult * roll_rows(lam, -step)
        if 2 * step < CAP:
            mult = mult * roll_rows(mult, -step)
        step *= 2
    g_a = lam * (roll_rows(state, 1) * masks[0])
    g_keep = g_a * a - lam * (input_gate * conv) * (a * a) / weight_in
    g_rate = (g_keep * (-RATE_SCALE * softplus_neg(decay)) * (rate * (1.0 - rate))).astype(BF16)
    g_decay = g_keep * (RATE_SCALE * rate) * sigmoid(-decay)
    flow = lam * weight_in
    g_inp = (flow * conv * (input_gate * (1.0 - input_gate))).astype(BF16)
    g_conv = flow * input_gate + mm_nt(jnp.concatenate([g_rate, g_inp], axis=1), gates)
    g_linear = g_conv * vec[0:1]
    sums = [jnp.sum(g_conv * linear, axis=0, keepdims=True)]
    for k in (1, 2, 3):
        g_linear = g_linear + vec[k : k + 1] * (roll_rows(g_conv, -k) * later[k - 1])
        sums.append(jnp.sum(g_conv * (roll_rows(linear, k) * masks[k - 1]), axis=0, keepdims=True))
    for value in (g_conv, g_rate.astype(F32), g_inp.astype(F32), g_decay):
        sums.append(jnp.sum(value, axis=0, keepdims=True))
    return g_gate, g_linear.astype(BF16), jnp.concatenate(sums, axis=0), conv.astype(BF16), g_rate, g_inp


def backward_kernel(
    lengths_ref, tokens_ref, g_middle_ref, gains_ref, gain_in_ref, vec_ref, gates_ref, out_proj_ref,
    half_gu_ref, half_down_ref, weights_ref, saved_ref, merged_ref, gathered_ref,
    grad_gate_out, grad_up_out, grad_down_out, term_gl_out, term_out_out, grad_tokens_ref, gain_ref, small_ref, term_bd_ref,
    g_mix, normed, weights, saved, merged, grads, parts, term_gl, term_out, total_bd, g_normed,
    sum_gu, sum_down, line_gu, line_down,
    a_send, a_recv, line_send, line_recv, ex_a, ex_b, ex_c, ex_d, dn_a, dn_b, dn_c, dn_d, load_sem, out_sem, *scatter_scratch,
):
    group, shard, z, x = place()
    y = group // 2
    shards = N_Z * N_X
    rows, width = tokens_ref.shape
    padded = vec_ref.shape[1]
    total = shards * rows
    chans = out_proj_ref.shape[0]
    loads = [
        pltpu.make_async_copy(source, target, load_sem.at[i])
        for i, (source, target) in enumerate((
            (half_gu_ref.at[y], sum_gu), (half_down_ref.at[y], sum_down),
            (saved_ref, saved), (weights_ref, weights), (gathered_ref, normed), (merged_ref, merged),
        ))
    ]
    for copy in loads:
        copy.start()
    gather = Gather(g_mix, (a_send, a_recv))
    scatter = Scatter(parts, scatter_scratch)
    line_sum = LineSum([half_gu_ref, half_down_ref], [line_gu, line_down], [sum_gu, sum_down], (line_send, line_recv))
    half = sum_gu.shape[2] // 2
    quarter_rows = sum_gu.shape[1]

    def columns(ref):
        return lambda origin, quarter: ref.at[pl.ds(quarter * quarter_rows, quarter_rows), pl.ds(origin * half, half)]

    exchange = Exchange(
        [lambda to: sum_gu.at[to, :, 0:half], lambda to: sum_gu.at[to, :, half : 2 * half]],
        [columns(grad_gate_out), columns(grad_up_out)], shards, (ex_a, ex_b, ex_c, ex_d),
    )
    down_exchange = Exchange(
        [lambda to: sum_down], [lambda origin, quarter: grad_down_out.at[quarter]], 1, (dn_a, dn_b, dn_c, dn_d)
    )
    greet(all_peers())
    line_sum.start()
    g_mix[shard] = g_middle_ref[...].astype(BF16)
    gather.start()
    small_ref[...] = jnp.zeros_like(small_ref)
    total_bd[...] = jnp.zeros_like(total_bd)
    gather.step(1)
    gather.step(2)
    for copy in loads:
        copy.wait()

    @pl.loop(0, N_Z)
    def _(i):
        @pl.when(i == 1)
        def _():
            gather.step(3)

        origin = nearest(z, i)
        gather.wait_across(origin)
        pair = pl.ds(origin * N_X, N_X)
        g_merged = mm_nt(g_mix[pair].reshape(N_X * rows, width), out_proj_ref[...])
        g_merged = jnp.concatenate([g_merged, jnp.zeros((N_X * rows, padded - chans), F32)], axis=1)
        where = normed[pair, :, width:].reshape(N_X * rows, normed.shape[2] - width)[:, :1].astype(F32)
        g_gate, g_linear, sums, low, g_rate, g_inp = mixer_backward(
            g_merged, [saved[origin, j] for j in range(5)], where, vec_ref[...], gates_ref[...]
        )
        grads[origin, :, :padded] = g_gate
        grads[origin, :, padded:] = g_linear
        small_ref[...] += sums
        total_bd[0] += mm_tn(low, g_rate)
        total_bd[1] += mm_tn(low, g_inp)
        back = mm_nt(grads[origin], weights[...].reshape(width, 2 * padded))
        parts[pair] = back.astype(BF16).reshape(N_X, rows, width)

    for i in range(N_Z):
        scatter.start(i)
    line_sum.add()
    exchange.start()
    down_exchange.start()
    tile = width // shards

    @pl.loop(0, shards)
    def _(i):
        left = normed[:, :, pl.ds(i * tile, tile)].reshape(total, tile)
        term = mm_tn(left, grads[...].reshape(total, 2 * padded)).astype(BF16)
        term_gl[:, i] = term.reshape(term_gl.shape[0], term_gl.shape[2], 2 * padded)

    scatter.step(0)
    down_exchange.spread()
    exchange.spread()
    term = mm_tn(merged[...].reshape(total, padded), g_mix[...].reshape(total, width))
    term_out[...] = term[:chans].astype(BF16).reshape(term_out.shape)
    outs = [
        pltpu.make_async_copy(term_gl, term_gl_out, out_sem.at[0]),
        pltpu.make_async_copy(term_out, term_out_out, out_sem.at[1]),
    ]
    for copy in outs:
        copy.start()
    scatter.step(1)
    size = term_bd_ref.shape[1] // 2
    for h in range(chans // size):
        part = slice(h * size, (h + 1) * size)
        both = jnp.concatenate([total_bd[0, part, part], total_bd[1, part, part]], axis=1)
        term_bd_ref[part] = both.astype(BF16)
    scatter.step(2)
    down_exchange.relay()
    exchange.relay()
    scatter.last(g_normed)
    _, live = positions_in_run([lengths_ref[0, i] for i in range(3)], rows)
    masked = tokens_ref[...].astype(F32) * live
    gain = jnp.concatenate([gains_ref[i] for i in range(shards)], axis=1)[0:1]
    back, gain_term = norm_backward(masked, gain, g_normed[...])
    grad_tokens_ref[...] = ((g_middle_ref[...] + back) * live).astype(BF16)
    gain_ref[...] = gain_in_ref[...]
    split_gains(gain_ref, 0, gain_term)
    gather.finish()
    line_sum.finish()
    for one in (down_exchange, exchange):
        one.arrive()
        one.finish()
    scatter.finish()
    for copy in outs:
        copy.wait()


def block_diagonal(weight):
    size = weight.shape[1]
    heads = weight.shape[0] // size
    parts = []
    for h in range(heads):
        parts.append(
            jnp.pad(weight[h * size : (h + 1) * size], ((0, 0), (h * size, (heads - 1 - h) * size)))
        )
    return jnp.concatenate(parts, axis=0)


def backward_call(
    head, lengths, tokens, g_middle, gains, gain_terms, vec, gates, out_proj, half_gu, half_down, weights, saved, merged, gathered
):
    rows, width = tokens.shape
    shards, groups = N_Z * N_X, weights.shape[1]
    quarter_rows, both = half_gu.shape[2:]
    padded = vec.shape[1]
    chans = out_proj.shape[0]
    dma = pltpu.SemaphoreType.DMA
    shape = jax.ShapeDtypeStruct
    gl_term = (groups, shards, quarter_rows, 2 * padded)
    out_term = (groups, chans // groups // 16, 16, width)
    return pl.pallas_call(
        backward_kernel,
        out_shape=[
            shape((groups * quarter_rows, shards * both // 2), BF16),
            shape((groups * quarter_rows, shards * both // 2), BF16),
            shape((groups,) + half_down.shape[1:], BF16),
            shape(gl_term, BF16),
            shape(out_term, BF16),
            shape((rows, width), BF16),
            shape(gains.shape, F32),
            shape(vec.shape, F32),
            shape((chans, 2 * head), BF16),
        ],
        in_specs=[pl.BlockSpec(memory_space=pltpu.SMEM)] + [vmem_spec()] * 7 + [any_spec()] * 6,
        out_specs=[any_spec()] * 5 + [vmem_spec()] * 4,
        scratch_shapes=[
            pltpu.VMEM((shards, rows, width), BF16),
            pltpu.VMEM(gathered.shape, BF16),
            pltpu.VMEM(weights.shape, BF16),
            pltpu.VMEM(saved.shape, F32),
            pltpu.VMEM(merged.shape, BF16),
            pltpu.VMEM((N_Z, N_X * rows, 2 * padded), BF16),
            pltpu.VMEM((shards, rows, width), BF16),
            pltpu.VMEM(gl_term, BF16),
            pltpu.VMEM(out_term, BF16),
            pltpu.VMEM((2, padded, padded), F32),
            pltpu.VMEM((rows, width), F32),
        ]
        + [pltpu.VMEM(half.shape[1:], BF16) for half in (half_gu, half_down)] * 2
        + Gather.scratch()
        + LineSum.scratch(2)
        + Exchange.scratch(shards, 2)
        + Exchange.scratch(1, 1)
        + [dma((6,)), dma((2,))]
        + Scatter.scratch(rows, width),
        compiler_params=pltpu.CompilerParams(collective_id=3, has_side_effects=True, vmem_limit_bytes=VMEM_LIMIT),
        name="mixer_backward",
    )(lengths, tokens, g_middle, gains, gain_terms, vec, gates, out_proj, half_gu, half_down, weights, saved, merged, gathered)


def final_kernel(
    lengths_ref, middle_ref, small_ref, gain_ref, parts_ref, term_gl_ref, term_out_ref, term_bd_ref,
    gl_out, out_out, bd_out, mixed_ref, small_out_ref,
    sum_gl, sum_out, sum_bd, core_gl, core_out, core_bd, line_gl, line_out, line_bd, gains, packed, packs, result,
    core_send, core_recv, line_send, line_recv, ex_a, ex_b, ex_c, ex_d, sp_a, sp_b, sp_c, sp_d, sq_a, sq_b, sq_c, sq_d,
    gain_send, gain_recv, pack_send, pack_recv, load_sem, *scatter_scratch,
):
    group, shard, z, x = place()
    y, core = group // 2, group % 2
    shards = N_Z * N_X
    rows, width = middle_ref.shape
    core_mate, y_mate = mates()
    terms = [term_gl_ref, term_out_ref, term_bd_ref]
    sums = [sum_gl, sum_out, sum_bd]
    loads = [
        pltpu.make_async_copy(term.at[2 * half + core], total.at[half], load_sem.at[j, half])
        for j, (term, total) in enumerate(zip(terms, sums)) for half in (0, 1)
    ]
    for copy in loads:
        copy.start()
    core_sum = CoreSum(
        terms, [core_gl, core_out, core_bd], [lambda half, total=total: total.at[half] for total in sums], (core_send, core_recv)
    )
    line_sum = LineSum(sums, [line_gl, line_out, line_bd], [total.at[y] for total in sums], (line_send, line_recv))
    scatter = Scatter(parts_ref, scatter_scratch)
    exchanges = [
        Exchange(
            [lambda to: sum_gl.at[y, to]], [lambda origin, quarter: gl_out.at[origin, quarter]], shards, (ex_a, ex_b, ex_c, ex_d)
        ),
        Exchange([lambda to: sum_out.at[y]], [lambda origin, quarter: out_out.at[quarter]], 1, (sp_a, sp_b, sp_c, sp_d)),
        Exchange([lambda to: sum_bd.at[y]], [lambda origin, quarter: bd_out.at[quarter]], 1, (sq_a, sq_b, sq_c, sq_d)),
    ]

    def gain_copy(to, origin):
        return pltpu.make_async_remote_copy(
            src_ref=gain_ref.at[to], dst_ref=gains.at[origin], send_sem=gain_send.at[to], recv_sem=gain_recv.at[origin],
            device_id=(group, to), device_id_type=MESH_ID,
        )

    def pack_copy(i):
        return pltpu.make_async_remote_copy(
            src_ref=packed, dst_ref=packs.at[i], send_sem=pack_send.at[i], recv_sem=pack_recv.at[i],
            device_id=((core_mate, y_mate, 3 - group)[i], shard), device_id_type=MESH_ID,
        )

    greet(all_peers() + [((3 - group, shard), True)])
    core_sum.start()
    for i in range(1, shards):
        gain_copy((shard + i) % shards, shard).start()
    for i in range(N_Z):
        scatter.start(i)
    for copy in loads:
        copy.wait()
    core_sum.add(1 - y)
    line_sum.start()
    core_sum.add(y)
    total = gain_ref[shard]
    for i in range(1, shards):
        origin = (shard + i) % shards
        gain_copy(origin, origin).wait_recv()
        total = total + gains[origin]
    packed[0:8] = small_ref[...]
    packed[8:16] = jnp.concatenate([total, jnp.zeros((8, packed.shape[1] - total.shape[1]), F32)], axis=1)
    for i in range(3):
        pack_copy(i).start()
    scatter.step(0)
    scatter.step(1)
    line_sum.add()
    for one in exchanges:
        one.start()
    for one in exchanges[1:]:
        one.spread()
    scatter.step(2)
    exchanges[0].spread()
    scatter.last(result)
    _, live = positions_in_run([lengths_ref[0, i] for i in range(3)], rows)
    mixed_ref[...] = ((middle_ref[...] + result[...]) * live).astype(BF16)
    total = packed[...]
    for i in range(3):
        pack_copy(i).wait_recv()
        total = total + packs[i]
    small_out_ref[...] = total
    for one in exchanges[1:] + exchanges[:1]:
        one.relay()
    for i in range(1, shards):
        gain_copy((shard + i) % shards, shard).wait_send()
    for i in range(3):
        pack_copy(i).wait_send()
    core_sum.finish()
    line_sum.finish()
    scatter.finish()
    for one in exchanges:
        one.arrive()
        one.finish()


def final_call(lengths, middle, small, gain_terms, parts, term_gl, term_out, term_bd):
    rows, width = middle.shape
    shards = N_Z * N_X
    terms = (term_gl, term_out, term_bd)
    dma = pltpu.SemaphoreType.DMA
    shape = jax.ShapeDtypeStruct
    groups = term_gl.shape[0]
    packed = (16, small.shape[1])
    return pl.pallas_call(
        final_kernel,
        out_shape=[
            shape((shards, groups) + term_gl.shape[2:], BF16),
            shape(term_out.shape, BF16),
            shape(term_bd.shape, BF16),
            shape((rows, width), BF16),
            shape(packed, F32),
        ],
        in_specs=[pl.BlockSpec(memory_space=pltpu.SMEM)] + [vmem_spec()] * 4 + [any_spec()] * 3,
        out_specs=[any_spec()] * 3 + [vmem_spec()] * 2,
        scratch_shapes=[pltpu.VMEM((2,) + term.shape[1:], BF16) for term in terms] * 2
        + [pltpu.VMEM(term.shape[1:], BF16) for term in terms]
        + [
            pltpu.VMEM(gain_terms.shape, F32),
            pltpu.VMEM(packed, F32),
            pltpu.VMEM((3,) + packed, F32),
            pltpu.VMEM((rows, width), F32),
        ]
        + CoreSum.scratch(3)
        + LineSum.scratch(3)
        + Exchange.scratch(shards, 1)
        + Exchange.scratch(1, 1) * 2
        + [dma((shards,)), dma((shards,)), dma((3,)), dma((3,)), dma((3, 2))]
        + Scatter.scratch(rows, width),
        compiler_params=pltpu.CompilerParams(collective_id=4, has_side_effects=True, vmem_limit_bytes=VMEM_LIMIT),
        name="last_sums",
    )(lengths, middle, small, gain_terms, parts, term_gl, term_out, term_bd)


def per_device_split(
    tokens, lengths, cotangent, norm1_gain, gate_in, linear_in, conv_kernel, conv_bias, rate_weight,
    rate_bias, input_weight, input_bias, decay_param, out_proj, norm2_gain, mlp_gate, mlp_up, mlp_down,
):
    width = tokens.shape[1]
    chans, size = rate_weight.shape
    padded = -(-chans // 128) * 128
    own_gains = jnp.pad(jnp.stack([norm1_gain, norm2_gain]).astype(F32), ((0, 6), (0, 0)))
    fill = ((0, padded - chans), (0, padded - chans))
    gates = jnp.concatenate(
        [jnp.pad(block_diagonal(rate_weight), fill), jnp.pad(block_diagonal(input_weight), fill)], axis=1
    )
    vec = jnp.concatenate([conv_kernel, jnp.stack([conv_bias, rate_bias, input_bias, decay_param])]).astype(F32)
    vec = jnp.pad(vec, ((0, 0), (0, padded - chans)))
    gathered, weights, mlp_weights, gains, saved, merged, middle, normed_two = forward_call(
        lengths, tokens, own_gains, vec, gates, out_proj, gate_in, linear_in, mlp_gate, mlp_up
    )
    parts, half_gu, half_down, g_middle, gain_terms = mlp_call(
        lengths, normed_two, cotangent, middle, gains, mlp_weights, mlp_down
    )
    grad_gate, grad_up, grad_down, term_gl, term_out, grad_tokens, gain_terms, small, term_bd = backward_call(
        size, lengths, tokens, g_middle, gains, gain_terms, vec, gates, out_proj, half_gu, half_down, weights, saved, merged, gathered
    )
    groups = term_gl.shape[0]
    gl, grad_out, bd, mixed, small = final_call(
        lengths, middle, small, gain_terms, parts, term_gl, term_out, term_bd.reshape(groups, -1, 16, 2 * size)
    )
    gl = gl.transpose(1, 2, 0, 3).reshape(gate_in.shape[0], -1, 2 * padded)
    grad_gate_in = gl[:, :, :chans].astype(F32).reshape(gate_in.shape)
    grad_linear_in = gl[:, :, padded : padded + chans].astype(F32).reshape(gate_in.shape)
    bd = bd.reshape(chans, 2 * size).astype(F32)
    own = norm1_gain.shape[0]
    return (
        mixed, grad_tokens, small[8, :own], grad_gate_in, grad_linear_in, small[0:4, :chans], small[4, :chans], bd[:, :size],
        small[5, :chans], bd[:, size:], small[6, :chans], small[7, :chans], grad_out.reshape(out_proj.shape).astype(F32),
        small[9, :own], grad_gate.astype(F32), grad_up.astype(F32), grad_down.reshape(mlp_down.shape).astype(F32),
    )


def as_sent(shard):
    return jax.tree.map(lambda a: a.astype(jnp.bfloat16) if a.dtype == jnp.float32 else a, shard)


def layout(counts, row_count):
    first = counts[0]
    second = first + counts[1]
    run_ends = jnp.stack([first, second, second + counts[2], second + counts[2] + counts[3]])
    positions = jnp.arange(row_count, dtype=jnp.int32)
    segment_ids = jnp.sum((positions[:, None] >= run_ends[None, :-1]).astype(jnp.int32), axis=1)
    live_rows = (positions < run_ends[-2]).astype(jnp.float32)
    return (segment_ids, live_rows)


def earlier_ids(segment_ids, offset):
    filler = jnp.full((offset,), -1, dtype=jnp.int32)
    return jnp.concatenate([filler, segment_ids[:-offset]])


def normalize(values, gain_vec):
    scale = lax.rsqrt(jnp.mean(values * values, axis=1, keepdims=True) + EPSILON)
    return values * scale * gain_vec


def convolve(linear_out, kernel, shift_vec, segment_ids):
    summed = linear_out * kernel[0] + shift_vec
    for offset in range(1, kernel.shape[0]):
        shifted = jnp.concatenate(
            [jnp.zeros((offset, linear_out.shape[1]), linear_out.dtype), linear_out[:-offset]],
            axis=0,
        )
        same_seq = (earlier_ids(segment_ids, offset) == segment_ids).astype(linear_out.dtype)
        summed = summed + kernel[offset] * shifted * same_seq[:, None]
    return summed


def combine_pairs(earlier_pair, later_pair):
    return (earlier_pair[0] * later_pair[0], later_pair[0] * earlier_pair[1] + later_pair[1])


def recurrence(rate_pre, input_pre, inflow, decay_vec, segment_ids):
    rate_gate = jax.nn.sigmoid(rate_pre)
    opened = jax.nn.sigmoid(input_pre)
    log_keep = -RATE_SCALE * rate_gate * jax.nn.softplus(-decay_vec)
    factor = jnp.exp(log_keep)
    weight_in = jnp.sqrt(-jnp.expm1(2.0 * log_keep))
    same_run = (earlier_ids(segment_ids, 1) == segment_ids).astype(factor.dtype)
    carried, states = lax.associative_scan(
        combine_pairs, (factor * same_run[:, None], weight_in * opened * inflow), axis=0
    )
    return states


def gated_gelu(gate_vals, up_vals):
    return jax.nn.gelu(gate_vals) * up_vals


def product(left, right):
    return jnp.dot(left, right, preferred_element_type=jnp.float32)


def contract(left, right):
    return jnp.einsum("ti,tj->ij", left, right, preferred_element_type=jnp.float32)


def back_dot(grad_vals, weight):
    return jnp.einsum("tj,ij->ti", grad_vals, weight, preferred_element_type=jnp.float32)


def blocked(values, weight):
    row_count = values.shape[0]
    size = weight.shape[1]
    heads = weight.shape[0] // size
    return jnp.einsum(
        "thj,hjk->thk",
        values.reshape(row_count, heads, size),
        weight.reshape(heads, size, size),
        preferred_element_type=jnp.float32,
    ).reshape(row_count, heads * size)


def block_terms(values, grad_vals, size):
    row_count = values.shape[0]
    heads = values.shape[1] // size
    terms = jnp.einsum(
        "thj,thk->hjk",
        values.reshape(row_count, heads, size),
        grad_vals.reshape(row_count, heads, size),
        preferred_element_type=jnp.float32,
    )
    return terms.reshape(heads * size, size)


def block_back(grad_vals, weight):
    row_count = grad_vals.shape[0]
    size = weight.shape[1]
    heads = weight.shape[0] // size
    return jnp.einsum(
        "thk,hjk->thj",
        grad_vals.reshape(row_count, heads, size),
        weight.reshape(heads, size, size),
        preferred_element_type=jnp.float32,
    ).reshape(row_count, heads * size)


def per_device_general(
    tokens,
    lengths,
    cotangent,
    norm1_gain,
    gate_in,
    linear_in,
    conv_kernel,
    conv_bias,
    rate_weight,
    rate_bias,
    input_weight,
    input_bias,
    decay_param,
    out_proj,
    norm2_gain,
    mlp_gate,
    mlp_up,
    mlp_down,
):
    row_count = tokens.shape[0]
    segment_ids, live_rows = layout(lengths[0], row_count)
    live_col = live_rows[:, None]
    mixer_full = (
        lax.all_gather(norm1_gain, "shard", axis=0, tiled=True),
        lax.all_gather(gate_in, "shard", axis=0, tiled=True),
        lax.all_gather(linear_in, "shard", axis=0, tiled=True),
        lax.all_gather(conv_kernel, "shard", axis=1, tiled=True),
        lax.all_gather(conv_bias, "shard", axis=0, tiled=True),
        lax.all_gather(rate_weight, "shard", axis=0, tiled=True),
        lax.all_gather(rate_bias, "shard", axis=0, tiled=True),
        lax.all_gather(input_weight, "shard", axis=0, tiled=True),
        lax.all_gather(input_bias, "shard", axis=0, tiled=True),
        lax.all_gather(decay_param, "shard", axis=0, tiled=True),
        lax.all_gather(out_proj, "shard", axis=0, tiled=True),
    )
    gain_first = mixer_full[0].astype(jnp.float32)
    kernel_full = mixer_full[3].astype(jnp.float32)
    kernel_shift = mixer_full[4].astype(jnp.float32)
    rate_shift = mixer_full[6].astype(jnp.float32)
    input_shift = mixer_full[8].astype(jnp.float32)
    decay_full = mixer_full[9].astype(jnp.float32)
    block_size = mixer_full[5].shape[1]
    masked_in = tokens.astype(jnp.float32) * live_col
    normed_low = normalize(masked_in, gain_first).astype(jnp.bfloat16)
    gate_pre = product(normed_low, mixer_full[1])
    linear_out = product(normed_low, mixer_full[2])
    gate_act = jax.nn.gelu(gate_pre)
    conv_out = convolve(linear_out, kernel_full, kernel_shift, segment_ids)
    conv_low = conv_out.astype(jnp.bfloat16)
    rate_pre = blocked(conv_low, mixer_full[5]) + rate_shift
    input_pre = blocked(conv_low, mixer_full[7]) + input_shift
    states = recurrence(rate_pre, input_pre, conv_out, decay_full, segment_ids)
    merged_low = (gate_act * states).astype(jnp.bfloat16)
    middle = masked_in + product(merged_low, mixer_full[10])
    mlp_full = (
        lax.all_gather(norm2_gain, "shard", axis=0, tiled=True),
        lax.all_gather(mlp_gate, "shard", axis=0, tiled=True),
        lax.all_gather(mlp_up, "shard", axis=0, tiled=True),
        lax.all_gather(mlp_down, "shard", axis=0, tiled=True),
    )
    gain_second = mlp_full[0].astype(jnp.float32)
    normed_two = normalize(middle, gain_second).astype(jnp.bfloat16)
    gate_mlp = product(normed_two, mlp_full[1])
    up_mlp = product(normed_two, mlp_full[2])
    hidden_low = gated_gelu(gate_mlp, up_mlp).astype(jnp.bfloat16)
    mixed_out = ((middle + product(hidden_low, mlp_full[3])) * live_col).astype(jnp.bfloat16)
    grad_out = cotangent.astype(jnp.float32) * live_col
    grad_down = grad_out.astype(jnp.bfloat16)
    again_mlp = (
        lax.all_gather(mlp_gate, "shard", axis=0, tiled=True),
        lax.all_gather(mlp_up, "shard", axis=0, tiled=True),
        lax.all_gather(mlp_down, "shard", axis=0, tiled=True),
    )
    term_down = contract(hidden_low, grad_down)
    part_down = lax.psum_scatter(
        term_down.astype(jnp.bfloat16), "shard", scatter_dimension=0, tiled=True
    ).astype(jnp.float32)
    grad_hidden = back_dot(grad_down, again_mlp[2])
    unused_val, hidden_back = jax.vjp(gated_gelu, gate_mlp, up_mlp)
    grad_gate_mlp, grad_up_mlp = hidden_back(grad_hidden)
    gate_mlp_low = grad_gate_mlp.astype(jnp.bfloat16)
    up_mlp_low = grad_up_mlp.astype(jnp.bfloat16)
    term_gate_mlp = contract(normed_two, gate_mlp_low)
    term_up_mlp = contract(normed_two, up_mlp_low)
    grad_normed_two = back_dot(gate_mlp_low, again_mlp[0]) + back_dot(up_mlp_low, again_mlp[1])
    unused_two, second_back = jax.vjp(normalize, middle, gain_second)
    grad_middle_norm, term_gain_two = second_back(grad_normed_two)
    parts_mlp = (
        lax.psum_scatter(
            term_gain_two.astype(jnp.bfloat16), "shard", scatter_dimension=0, tiled=True
        ).astype(jnp.float32),
        lax.psum_scatter(
            term_gate_mlp.astype(jnp.bfloat16), "shard", scatter_dimension=0, tiled=True
        ).astype(jnp.float32),
        lax.psum_scatter(
            term_up_mlp.astype(jnp.bfloat16), "shard", scatter_dimension=0, tiled=True
        ).astype(jnp.float32),
    )
    grad_middle = grad_out + grad_middle_norm
    grad_mix_low = grad_middle.astype(jnp.bfloat16)
    again_mixer = (
        lax.all_gather(gate_in, "shard", axis=0, tiled=True),
        lax.all_gather(linear_in, "shard", axis=0, tiled=True),
        lax.all_gather(rate_weight, "shard", axis=0, tiled=True),
        lax.all_gather(input_weight, "shard", axis=0, tiled=True),
        lax.all_gather(out_proj, "shard", axis=0, tiled=True),
    )
    term_out = contract(merged_low, grad_mix_low)
    grad_merged = back_dot(grad_mix_low, again_mixer[4])
    grad_states = grad_merged * gate_act
    unused_three, gelu_back = jax.vjp(jax.nn.gelu, gate_pre)
    gate_low = gelu_back(grad_merged * states)[0].astype(jnp.bfloat16)
    unused_four, scan_back = jax.vjp(
        partial(recurrence, segment_ids=segment_ids), rate_pre, input_pre, conv_out, decay_full
    )
    grad_rate, grad_input, grad_flow, term_decay = scan_back(grad_states)
    rate_low = grad_rate.astype(jnp.bfloat16)
    input_low = grad_input.astype(jnp.bfloat16)
    term_rate = block_terms(conv_low, rate_low, block_size)
    term_input = block_terms(conv_low, input_low, block_size)
    term_rate_shift = jnp.sum(rate_low.astype(jnp.float32), axis=0)
    term_input_shift = jnp.sum(input_low.astype(jnp.float32), axis=0)
    grad_conv = (
        grad_flow + block_back(rate_low, again_mixer[2]) + block_back(input_low, again_mixer[3])
    )
    unused_five, conv_back = jax.vjp(
        partial(convolve, segment_ids=segment_ids), linear_out, kernel_full, kernel_shift
    )
    grad_linear, term_kernel, term_kernel_shift = conv_back(grad_conv)
    linear_low = grad_linear.astype(jnp.bfloat16)
    term_gate_in = contract(normed_low, gate_low)
    term_linear = contract(normed_low, linear_low)
    grad_normed = back_dot(gate_low, again_mixer[0]) + back_dot(linear_low, again_mixer[1])
    unused_six, first_back = jax.vjp(normalize, masked_in, gain_first)
    grad_masked, term_gain_one = first_back(grad_normed)
    grad_tokens = ((grad_middle + grad_masked) * live_col).astype(jnp.bfloat16)
    small_terms = (
        term_gain_one,
        term_kernel,
        term_kernel_shift,
        term_rate,
        term_rate_shift,
        term_input,
        term_input_shift,
        term_decay,
    )
    placed = tuple((term for term in small_terms))
    mixer_terms = (
        placed[0],
        term_gate_in,
        term_linear,
        placed[1],
        placed[2],
        placed[3],
        placed[4],
        placed[5],
        placed[6],
        placed[7],
        term_out,
    )
    parts_mixer = (
        lax.psum_scatter(
            mixer_terms[0].astype(jnp.bfloat16), "shard", scatter_dimension=0, tiled=True
        ).astype(jnp.float32),
        lax.psum_scatter(
            mixer_terms[1].astype(jnp.bfloat16), "shard", scatter_dimension=0, tiled=True
        ).astype(jnp.float32),
        lax.psum_scatter(
            mixer_terms[2].astype(jnp.bfloat16), "shard", scatter_dimension=0, tiled=True
        ).astype(jnp.float32),
        lax.psum_scatter(
            mixer_terms[3].astype(jnp.bfloat16), "shard", scatter_dimension=1, tiled=True
        ).astype(jnp.float32),
        lax.psum_scatter(
            mixer_terms[4].astype(jnp.bfloat16), "shard", scatter_dimension=0, tiled=True
        ).astype(jnp.float32),
        lax.psum_scatter(
            mixer_terms[5].astype(jnp.bfloat16), "shard", scatter_dimension=0, tiled=True
        ).astype(jnp.float32),
        lax.psum_scatter(
            mixer_terms[6].astype(jnp.bfloat16), "shard", scatter_dimension=0, tiled=True
        ).astype(jnp.float32),
        lax.psum_scatter(
            mixer_terms[7].astype(jnp.bfloat16), "shard", scatter_dimension=0, tiled=True
        ).astype(jnp.float32),
        lax.psum_scatter(
            mixer_terms[8].astype(jnp.bfloat16), "shard", scatter_dimension=0, tiled=True
        ).astype(jnp.float32),
        lax.psum_scatter(
            mixer_terms[9].astype(jnp.bfloat16), "shard", scatter_dimension=0, tiled=True
        ).astype(jnp.float32),
        lax.psum_scatter(
            mixer_terms[10].astype(jnp.bfloat16), "shard", scatter_dimension=0, tiled=True
        ).astype(jnp.float32),
    )
    shard_parts = tuple(parts_mixer) + (parts_mlp[0], parts_mlp[1], parts_mlp[2], part_down)
    totals = jax.tree.map(
        lambda part: part.astype(jnp.float32), lax.psum(as_sent(shard_parts), "group")
    )
    return (mixed_out, grad_tokens) + tuple(totals)


def solution(mesh):
    placed = (
        P(("group", "shard"), None),
        P(("group", "shard"), None),
        P(("group", "shard"), None),
        P("shard"),
        P("shard", None),
        P("shard", None),
        P(None, "shard"),
        P("shard"),
        P("shard", None),
        P("shard"),
        P("shard", None),
        P("shard"),
        P("shard"),
        P("shard", None),
        P("shard"),
        P("shard", None),
        P("shard", None),
        P("shard", None),
    )
    split_fits = FAST_MESH == tuple(mesh.shape[axis] for axis in ("group", "shard"))
    return jax.shard_map(
        per_device_split if split_fits else per_device_general,
        mesh=mesh,
        in_specs=placed,
        out_specs=(
            P(("group", "shard"), None),
            P(("group", "shard"), None),
            P("shard"),
            P("shard", None),
            P("shard", None),
            P(None, "shard"),
            P("shard"),
            P("shard", None),
            P("shard"),
            P("shard", None),
            P("shard"),
            P("shard"),
            P("shard", None),
            P("shard"),
            P("shard", None),
            P("shard", None),
            P("shard", None),
        ),
        check_vma=False,
    )
```

```python
from functools import partial

import jax
import jax.numpy as jnp
from jax import lax
from jax.experimental import pallas as pl
from jax.experimental.pallas import tpu as pltpu
from jax.sharding import PartitionSpec as P

FAST_MESH = (4, 8)
RATE_SCALE = 8.0
EPSILON = 1e-06
F32 = jnp.float32
BF16 = jnp.bfloat16
GELU_C = 0.7978845608028654
GELU_K = 0.044715
CAP = 128


def positions_in_run(counts, row_count):
    first = counts[0]
    second = first + counts[1]
    third = second + counts[2]
    rows = lax.broadcasted_iota(jnp.int32, (row_count, 1), 0)
    start = jnp.where(rows >= first, first, 0)
    start = jnp.where(rows >= second, second, start)
    start = jnp.where(rows >= third, third, start)
    return rows - start, (rows < third).astype(F32)


def gelu_parts(x):
    t = jnp.tanh(GELU_C * (x + GELU_K * x * x * x))
    value = 0.5 * x * (1.0 + t)
    slope = 0.5 * (1.0 + t) + 0.5 * x * (1.0 - t * t) * GELU_C * (1.0 + 3.0 * GELU_K * x * x)
    return value, slope


def gelu_value(x):
    return 0.5 * x * (1.0 + jnp.tanh(GELU_C * (x + GELU_K * x * x * x)))


def sigmoid(x):
    return 0.5 * (1.0 + jnp.tanh(0.5 * x))


def one_less_exp(z):
    series = 1.0 - z * (1.0 / 7.0)
    for k in (6.0, 5.0, 4.0, 3.0, 2.0):
        series = 1.0 - z * (1.0 / k) * series
    return jnp.where(z < 0.35, z * series, 1.0 - jnp.exp(-z))


def softplus_neg(x):
    return jnp.maximum(-x, 0.0) + jnp.log1p(jnp.exp(-jnp.abs(x)))


def mm(a, b):
    return jnp.dot(a, b, preferred_element_type=F32)


def mm_nt(a, b):
    return lax.dot_general(a, b, (((1,), (1,)), ((), ())), preferred_element_type=F32)


def mm_tn(a, b):
    return lax.dot_general(a, b, (((0,), (0,)), ((), ())), preferred_element_type=F32)


def roll_rows(x, n):
    return pltpu.roll(x, n % x.shape[0], 0)


def conv_rows(linear, kernel, bias, masks):
    out = linear * kernel[0:1] + bias
    for k in range(1, 4):
        out = out + kernel[k : k + 1] * (roll_rows(linear, k) * masks[k - 1])
    return out


def decay_terms(rate_pre, decay):
    rate = sigmoid(rate_pre)
    keep = RATE_SCALE * rate * softplus_neg(decay)
    return rate, jnp.exp(-keep), jnp.sqrt(one_less_exp(2.0 * keep))


MESH_ID = pl.DeviceIdType.MESH
VMEM_LIMIT = 62 * 2**20
N_Z, N_X = 4, 2


def place():
    shard = lax.axis_index("shard")
    return lax.axis_index("group"), shard, shard // N_X, shard % N_X


def greet(peers):
    bar = pltpu.get_barrier_semaphore()
    count = 0
    for device, there in peers:
        if there is True:
            pl.semaphore_signal(bar, inc=1, device_id=device, device_id_type=MESH_ID)
            count = count + 1
        else:
            @pl.when(there)
            def _(device=device):
                pl.semaphore_signal(bar, inc=1, device_id=device, device_id_type=MESH_ID)
            count = count + there.astype(jnp.int32)
    pl.semaphore_wait(bar, count)


def line_peers():
    group, shard, z, x = place()
    return [
        ((group, shard + N_X), z < N_Z - 1),
        ((group, shard - N_X), z > 0),
        ((group, z * N_X + 1 - x), True),
    ]


class Gather:
    CHUNKS = 2

    @classmethod
    def scratch(cls):
        return [pltpu.SemaphoreType.DMA((3, N_Z, cls.CHUNKS)), pltpu.SemaphoreType.DMA((N_Z * N_X, cls.CHUNKS))]

    def __init__(self, buf, sems):
        self.buf, (self.send, self.recv) = buf, sems
        self.group, self.shard, self.z, self.x = place()
        self.rows = buf.shape[1] // self.CHUNKS

    def copy(self, origin, column, c, way):
        slot = origin * N_X + column
        z = (self.z + 1, self.z - 1, self.z)[way]
        x = 1 - self.x if way == 2 else self.x
        piece = self.buf.at[slot, pl.ds(c * self.rows, self.rows)]
        return pltpu.make_async_remote_copy(
            src_ref=piece, dst_ref=piece, send_sem=self.send.at[way, origin, c],
            recv_sem=self.recv.at[slot, c], device_id=(self.group, z * N_X + x), device_id_type=MESH_ID,
        )

    def start(self):
        for c in range(self.CHUNKS):
            self.forward(self.z, c, True, True)

    def forward(self, origin, c, up, down):
        if up:
            @pl.when(self.z < N_Z - 1)
            def _():
                self.copy(origin, self.x, c, 0).start()
        if down:
            @pl.when(self.z > 0)
            def _():
                self.copy(origin, self.x, c, 1).start()
        self.copy(origin, self.x, c, 2).start()

    def step(self, k):
        for c in range(self.CHUNKS):
            @pl.when(self.z >= k)
            def _(c=c):
                self.copy(self.z - k, self.x, c, 2).wait_recv()
                self.forward(self.z - k, c, True, False)

            @pl.when(self.z + k < N_Z)
            def _(c=c):
                self.copy(self.z + k, self.x, c, 2).wait_recv()
                self.forward(self.z + k, c, False, True)

    def wait_across(self, origin):
        for c in range(self.CHUNKS):
            self.copy(origin, 1 - self.x, c, 2).wait_recv()

    def finish(self):
        for c in range(self.CHUNKS):
            for origin in range(N_Z):
                @pl.when((self.z < N_Z - 1) & (origin <= self.z))
                def _():
                    self.copy(origin, self.x, c, 0).wait_send()

                @pl.when((self.z > 0) & (origin >= self.z))
                def _():
                    self.copy(origin, self.x, c, 1).wait_send()
                self.copy(origin, self.x, c, 2).wait_send()


class Scatter:
    CHUNKS = 2

    @classmethod
    def scratch(cls, rows, width):
        dma = pltpu.SemaphoreType.DMA
        return [
            pltpu.VMEM((N_Z, rows, width), BF16),
            pltpu.VMEM((N_Z + 1, rows, width), BF16),
            dma((2, N_Z, cls.CHUNKS)), dma((N_Z, cls.CHUNKS)), dma((N_Z + 1, cls.CHUNKS)),
        ]

    def __init__(self, away, own, scratch):
        self.away, self.own = away, own
        self.across, self.along, self.send, self.recv_x, self.recv_z = scratch
        self.group, self.shard, self.z, self.x = place()
        self.rows = self.across.shape[1] // self.CHUNKS

    @classmethod
    def of(cls, parts, scratch):
        _, _, _, x = place()
        return cls(lambda k: parts.at[k * N_X + 1 - x], lambda k: parts.at[k * N_X + x], scratch)

    def dest(self, i):
        low = jnp.minimum(self.z, N_Z - 1 - self.z)
        value = (N_Z - 1, N_Z - 2, jnp.where(low == 0, 1, 0), low)[i]
        return jnp.where(self.z >= N_Z // 2, N_Z - 1 - value, value)

    def span(self, c):
        return pl.ds(c * self.rows, self.rows)

    def copy_x(self, dest, c):
        return pltpu.make_async_remote_copy(
            src_ref=self.away(dest).at[self.span(c)], dst_ref=self.across.at[dest, self.span(c)],
            send_sem=self.send.at[0, dest, c], recv_sem=self.recv_x.at[dest, c],
            device_id=(self.group, self.z * N_X + 1 - self.x), device_id_type=MESH_ID,
        )

    def copy_z(self, dest, slot, c, step):
        return pltpu.make_async_remote_copy(
            src_ref=self.own(dest).at[self.span(c)], dst_ref=self.along.at[slot, self.span(c)],
            send_sem=self.send.at[1, dest, c], recv_sem=self.recv_z.at[slot, c],
            device_id=(self.group, (self.z + step) * N_X + self.x), device_id_type=MESH_ID,
        )

    def start(self, i):
        for c in range(self.CHUNKS):
            self.copy_x(self.dest(i), c).start()

    def arrived(self, slot, c):
        self.copy_z(0, slot, c, 0).wait_recv()
        return self.along[slot, self.span(c)].astype(F32)

    def half(self, dest, c):
        return self.own(dest)[self.span(c)].astype(F32) + self.across[dest, self.span(c)].astype(F32)

    def step(self, i):
        dest = self.dest(i)
        own = self.own(dest)
        for c in range(self.CHUNKS):
            self.copy_x(dest, c).wait_recv()
            inner = ((dest > self.z) & (self.z > 0)) | ((dest < self.z) & (self.z < N_Z - 1))

            @pl.when(inner)
            def _(c=c):
                own[self.span(c)] = (self.half(dest, c) + self.arrived(dest, c)).astype(BF16)

            @pl.when(jnp.logical_not(inner))
            def _(c=c):
                own[self.span(c)] = self.half(dest, c).astype(BF16)

            @pl.when(dest > self.z)
            def _(c=c):
                self.copy_z(dest, dest, c, 1).start()

            @pl.when(dest < self.z)
            def _(c=c):
                self.copy_z(dest, jnp.where(dest == self.z - 1, N_Z, dest), c, -1).start()

    def last(self, out):
        for c in range(self.CHUNKS):
            self.copy_x(self.z, c).wait_recv()
            out[self.span(c)] = self.half(self.z, c)

            @pl.when(self.z > 0)
            def _(c=c):
                out[self.span(c)] += self.arrived(self.z, c)

            @pl.when(self.z < N_Z - 1)
            def _(c=c):
                out[self.span(c)] += self.arrived(N_Z, c)

    def finish(self):
        for c in range(self.CHUNKS):
            for dest in range(N_Z):
                self.copy_x(dest, c).wait_send()

                @pl.when(dest != self.z)
                def _():
                    self.copy_z(dest, 0, c, 0).wait_send()


class Exchange:
    @classmethod
    def scratch(cls, blocks, count):
        dma = pltpu.SemaphoreType.DMA
        return [dma((count, blocks)), dma((count, blocks)), dma((3, count, blocks)), dma((3, count, blocks))]

    def __init__(self, sources, views, blocks, sems):
        self.sources, self.views, self.blocks = sources, views, blocks
        self.send_first, self.recv_first, self.send, self.recv = sems
        self.group, self.shard, _, _ = place()
        self.home = self.shard if blocks > 1 else 0
        self.core_mate, self.y_mate = mates()
        self.count = len(sources)

    def first(self, j, to, origin):
        return pltpu.make_async_remote_copy(
            src_ref=self.sources[j](to), dst_ref=self.views[j](origin, self.group),
            send_sem=self.send_first.at[j, to], recv_sem=self.recv_first.at[j, origin],
            device_id=(self.group, to), device_id_type=MESH_ID,
        )

    def own(self, j):
        return pltpu.make_async_copy(
            self.sources[j](self.home), self.views[j](self.home, self.group), self.recv_first.at[j, self.home]
        )

    def pass_on(self, j, origin, quarter, mate, way, source=None):
        piece = self.views[j](origin, quarter)
        return pltpu.make_async_remote_copy(
            src_ref=piece if source is None else source, dst_ref=piece, send_sem=self.send.at[way, j, origin], recv_sem=self.recv.at[way, j, origin],
            device_id=(mate, self.shard), device_id_type=MESH_ID,
        )

    def others(self, body):
        if self.blocks > 1:
            pl.loop(1, self.blocks)(lambda i: body((self.home + i) % self.blocks))

    def start(self):
        for j in range(self.count):
            self.own(j).start()

        def send(to):
            for j in range(self.count):
                self.first(j, to, self.home).start()

        self.others(send)

    def both(self, j, origin, source=None):
        self.pass_on(j, origin, self.group, self.y_mate, 1, source).start()
        self.pass_on(j, origin, self.group, self.core_mate, 0, source).start()

    def spread(self):
        for j in range(self.count):
            self.both(j, self.home, self.sources[j](self.home))

        def forward(origin):
            for j in range(self.count):
                self.first(j, origin, origin).wait_recv()
                self.both(j, origin)

        self.others(forward)

    def each(self, body):
        for j in range(self.count):
            body(j, self.home)

        def rest(origin):
            for j in range(self.count):
                body(j, origin)

        self.others(rest)

    def relay(self):
        def forward(j, origin):
            self.pass_on(j, origin, self.y_mate, self.core_mate, 1).wait_recv()
            self.pass_on(j, origin, self.y_mate, self.core_mate, 2).start()

        self.each(forward)

    def arrive(self):
        def wait(j, origin):
            self.pass_on(j, origin, self.group, self.core_mate, 0).wait_recv()
            self.pass_on(j, origin, self.group, self.core_mate, 2).wait_recv()

        for j in range(self.count):
            self.own(j).wait()
        self.each(wait)

    def finish(self):
        def sent(to):
            for j in range(self.count):
                self.first(j, to, self.home).wait_send()

        def passed(j, origin):
            for way in range(3):
                self.pass_on(j, origin, self.group, self.core_mate, way).wait_send()

        self.others(sent)
        self.each(passed)


def mates():
    group = lax.axis_index("group")
    return group + 1 - 2 * (group % 2), group + 2 - 4 * (group // 2)


def all_peers():
    group, shard, _, _ = place()
    core_mate, y_mate = mates()
    others = [((group, (shard + i) % (N_Z * N_X)), True) for i in range(1, N_Z * N_X)]
    return others + [((core_mate, shard), True), ((y_mate, shard), True)]


def mixer_forward(linear, gate, pos, vec, gates):
    masks = [(pos >= k).astype(F32) for k in (1, 2, 3)]
    conv = conv_rows(linear, vec[0:4], vec[4:5], masks)
    width = linear.shape[1]
    both = mm_nt(conv.astype(BF16), gates)
    rate_pre = both[:, :width] + vec[5:6]
    input_pre = both[:, width:] + vec[6:7]
    _, a, weight_in = decay_terms(rate_pre, vec[7:8])
    mult = a * masks[0]
    total = weight_in * sigmoid(input_pre) * conv
    step = 1
    while step < CAP:
        total = total + mult * roll_rows(total, step)
        if 2 * step < CAP:
            mult = mult * roll_rows(mult, step)
        step *= 2
    return rate_pre, input_pre, total, (gelu_value(gate) * total).astype(BF16)


def rms_scale(values):
    return lax.rsqrt(jnp.mean(values * values, axis=1, keepdims=True) + EPSILON)


def forward_kernel(
    lengths_ref, tokens_ref, cotangent_ref, gain1_ref, gain2_ref, kernel_ref, bias_ref, rate_bias_ref, input_bias_ref, decay_ref, rate_weight_ref,
    input_weight_ref, out_proj_ref, gate_in_ref, linear_in_ref, mlp_gate_ref, mlp_up_ref,
    gather_out, weights_out, mlp_out, gains_out, saved_out, merged_out, middle_ref, normed_two_ref, vec_ref, gates_ref, g_low_out,
    gains_ref, g_low, buf, weights, quarter, raw, masked, saved, merged, parts,
    gather_a, gather_b, ex_a, ex_b, ex_c, ex_d, mx_a, mx_b, mx_c, mx_d, *rest,
):
    scatter_scratch, rest = rest[:-8], rest[-8:]
    gain_send, gain_recv, raw_sem, out_sem, pair_sem, g_sem, g_send, g_recv = rest
    group, shard, z, x = place()
    shards = N_Z * N_X
    rows, width = tokens_ref.shape
    quarter_rows = raw.shape[1]
    chans = linear_in_ref.shape[1] // shards
    padded = vec_ref.shape[1]
    fetch = [
        pltpu.make_async_copy(ref.at[pl.ds(group * quarter_rows, quarter_rows)], raw.at[i], raw_sem.at[i])
        for i, ref in enumerate((gate_in_ref, linear_in_ref))
    ]
    for copy in fetch:
        copy.start()
    gains_ref[...] = jnp.zeros_like(gains_ref)
    gains_ref[0:1] = gain1_ref[...].astype(F32).reshape(1, -1)
    gains_ref[1:2] = gain2_ref[...].astype(F32).reshape(1, -1)
    greet(all_peers())

    def gain_copy(to, origin):
        return pltpu.make_async_remote_copy(
            src_ref=gains_ref, dst_ref=gains_out.at[origin], send_sem=gain_send.at[to], recv_sem=gain_recv.at[origin],
            device_id=(group, to), device_id_type=MESH_ID,
        )

    for i in range(1, shards):
        gain_copy((shard + i) % shards, shard).start()
    gains_out[shard] = gains_ref[...]
    inside = lax.broadcasted_iota(jnp.int32, (quarter_rows, padded), 1) < chans
    for i, copy in enumerate(fetch):
        copy.wait()
        for to in range(shards):
            piece = raw[i, :, to * chans : (to + 1) * chans].astype(F32)
            piece = jnp.concatenate([piece, jnp.zeros((quarter_rows, padded - chans), F32)], axis=1)
            quarter[to, :, i * padded : (i + 1) * padded] = piece.astype(BF16)
    exchange = Exchange(
        [lambda to: quarter.at[to]], [lambda origin, q: weights.at[origin, q]], shards, (ex_a, ex_b, ex_c, ex_d)
    )
    exchange.start()
    hidden = mlp_up_ref.shape[1] // shards

    def part_of(ref):
        return lambda to: ref.at[pl.ds(group * quarter_rows, quarter_rows), pl.ds(to * hidden, hidden)]

    mlp_exchange = Exchange(
        [part_of(mlp_gate_ref), part_of(mlp_up_ref)],
        [lambda origin, q: mlp_out.at[origin, q, :, 0:hidden], lambda origin, q: mlp_out.at[origin, q, :, hidden : 2 * hidden]],
        shards, (mx_a, mx_b, mx_c, mx_d),
    )
    pos, live = positions_in_run([lengths_ref[0, i] for i in range(3)], rows)
    masked[...] = tokens_ref[...].astype(F32) * live
    g_low[...] = (cotangent_ref[...].astype(F32) * live).astype(BF16)
    g_copy = pltpu.make_async_copy(g_low, g_low_out.at[shard], g_sem)
    g_copy.start()
    g_gather = Gather(g_low_out, (g_send, g_recv))
    for i in range(1, shards):
        gain_copy(shard, (shard + i) % shards).wait_recv()
    gains = jnp.concatenate([gains_out[i] for i in range(shards)], axis=1)
    gather = Gather(buf, (gather_a, gather_b))
    buf[shard, :, :width] = (masked[...] * rms_scale(masked[...]) * gains[0:1]).astype(BF16)
    buf[shard, :, width:] = jnp.broadcast_to(pos.astype(F32).astype(BF16), (rows, buf.shape[2] - width))
    gather.start()
    vec_ref[...] = jnp.zeros_like(vec_ref)
    vec_ref[0:4, :chans] = kernel_ref[...].astype(F32)
    for i, ref in enumerate((bias_ref, rate_bias_ref, input_bias_ref, decay_ref)):
        vec_ref[4 + i : 5 + i, :chans] = ref[...].astype(F32).reshape(1, -1)
    gates_ref[...] = jnp.zeros_like(gates_ref)
    size = rate_weight_ref.shape[0]
    for i, ref in enumerate((rate_weight_ref, input_weight_ref)):
        for h in range(chans // size):
            part = slice(h * size, (h + 1) * size)
            gates_ref[i * padded + h * size : i * padded + (h + 1) * size, part] = ref[:, part]
    gather.step(1)
    exchange.spread()
    gather.step(2)
    exchange.relay()
    mlp_exchange.start()
    exchange.arrive()
    scatter = Scatter.of(parts, scatter_scratch)

    def pair_copies(origin):
        return [
            pltpu.make_async_copy(saved.at[origin], saved_out.at[origin], pair_sem.at[0, origin]),
            pltpu.make_async_copy(merged.at[origin], merged_out.at[origin], pair_sem.at[1, origin]),
        ]

    @pl.loop(0, N_Z)
    def _(i):
        @pl.when(i == 1)
        def _():
            gather.step(3)
            g_copy.wait()
            g_gather.start()

        origin = nearest(z, i)
        gather.wait_across(origin)
        pair = pl.ds(origin * N_X, N_X)
        both = buf[pair].reshape(N_X * rows, buf.shape[2])
        pre = mm(both[:, :width], weights[...].reshape(width, 2 * padded))
        gate, linear = pre[:, :padded], pre[:, padded:]
        where = both[:, width : width + 1].astype(F32)
        rate_pre, input_pre, state, merge = mixer_forward(linear, gate, where, vec_ref[...], gates_ref[...])
        for j, value in enumerate((gate, linear, rate_pre, input_pre, state)):
            saved[origin, j] = value
        merged[origin] = merge
        for copy in pair_copies(origin):
            copy.start()
        parts[pair] = mm(merge[:, :chans], out_proj_ref[...]).astype(BF16).reshape(N_X, rows, width)

    outs = [
        pltpu.make_async_copy(buf, gather_out, out_sem.at[0]),
        pltpu.make_async_copy(weights, weights_out, out_sem.at[1]),
    ]
    for copy in outs:
        copy.start()
    for i in range(N_Z):
        scatter.start(i)
    mlp_exchange.spread()
    scatter.step(0)
    g_gather.step(1)
    mlp_exchange.relay()
    scatter.step(1)
    g_gather.step(2)
    scatter.step(2)
    g_gather.step(3)
    scatter.last(middle_ref)
    middle_ref[...] += masked[...]
    normed_two_ref[...] = (middle_ref[...] * rms_scale(middle_ref[...]) * gains[1:2]).astype(BF16)
    for i in range(1, shards):
        gain_copy((shard + i) % shards, shard).wait_send()
    gather.finish()
    exchange.finish()
    for origin in range(N_Z):
        g_gather.wait_across(origin)
    g_gather.finish()
    mlp_exchange.arrive()
    mlp_exchange.finish()
    scatter.finish()
    for copy in outs:
        copy.wait()

    @pl.loop(0, N_Z)
    def _(origin):
        for copy in pair_copies(origin):
            copy.wait()


def nearest(z, i):
    low = jnp.minimum(z, N_Z - 1 - z)
    value = jnp.where(low == 0, i, jnp.where(i == 0, 1, jnp.where(i == 1, 0, i)))
    return jnp.where(z >= N_Z // 2, N_Z - 1 - value, value)


def any_spec():
    return pl.BlockSpec(memory_space=pl.ANY)


def vmem_spec():
    return pl.BlockSpec(memory_space=pltpu.VMEM)


def forward_call(lengths, tokens, cotangent, small, out_proj, gate_in, linear_in, mlp_gate, mlp_up):
    rows, width = tokens.shape
    shards, groups = lax.axis_size("shard"), lax.axis_size("group")
    padded = -(-out_proj.shape[0] // 128) * 128
    gains = (8, width // shards)
    quarter_rows = gate_in.shape[0] // groups
    hidden = mlp_up.shape[1] // shards
    dma = pltpu.SemaphoreType.DMA
    shape = jax.ShapeDtypeStruct
    out_shape = [
        shape((shards, rows, width + 128), BF16),
        shape((shards, groups, quarter_rows, 2 * padded), BF16),
        shape((shards, groups, quarter_rows, 2 * hidden), BF16),
        shape((shards,) + gains, F32),
        shape((N_Z, 5, N_X * rows, padded), F32),
        shape((N_Z, N_X * rows, padded), BF16),
        shape((rows, width), F32),
        shape((rows, width), BF16),
        shape((8, padded), F32),
        shape((2 * padded, padded), BF16),
        shape((shards, rows, width), BF16),
    ]
    return pl.pallas_call(
        forward_kernel,
        out_shape=out_shape,
        in_specs=[pl.BlockSpec(memory_space=pltpu.SMEM)] + [vmem_spec()] * 12 + [any_spec()] * 4,
        out_specs=[any_spec()] * 3 + [vmem_spec()] + [any_spec()] * 2 + [vmem_spec()] * 4 + [any_spec()],
        scratch_shapes=[
            pltpu.VMEM(gains, F32),
            pltpu.VMEM((rows, width), BF16),
            pltpu.VMEM((shards, rows, width + 128), BF16),
            pltpu.VMEM((shards, groups, quarter_rows, 2 * padded), BF16),
            pltpu.VMEM((shards, quarter_rows, 2 * padded), BF16),
            pltpu.VMEM((2, quarter_rows, gate_in.shape[1]), BF16),
            pltpu.VMEM((rows, width), F32),
            pltpu.VMEM((N_Z, 5, N_X * rows, padded), F32),
            pltpu.VMEM((N_Z, N_X * rows, padded), BF16),
            pltpu.VMEM((shards, rows, width), BF16),
        ]
        + Gather.scratch()
        + Exchange.scratch(shards, 1)
        + Exchange.scratch(shards, 2)
        + Scatter.scratch(rows, width)
        + [dma((shards,)), dma((shards,)), dma((2,)), dma((2,)), dma((2, N_Z)), dma]
        + Gather.scratch(),
        compiler_params=pltpu.CompilerParams(collective_id=1, has_side_effects=True, vmem_limit_bytes=VMEM_LIMIT),
        name="mixer_forward",
    )(lengths, tokens, cotangent, *small, out_proj, gate_in, linear_in, mlp_gate, mlp_up)


class CoreSum:
    @classmethod
    def scratch(cls, count):
        return [pltpu.SemaphoreType.DMA((count, 2))] * 2

    def __init__(self, terms, arrived, sems):
        self.terms, self.arrived = terms, arrived
        self.send, self.recv = sems
        group, self.shard, _, _ = place()
        self.core, self.y = group % 2, group // 2
        self.core_mate, _ = mates()

    def copy(self, j, half):
        return pltpu.make_async_remote_copy(
            src_ref=self.terms[j](2 * half + 1 - self.core), dst_ref=self.arrived[j].at[half],
            send_sem=self.send.at[j, half], recv_sem=self.recv.at[j, half],
            device_id=(self.core_mate, self.shard), device_id_type=MESH_ID,
        )

    def mine(self, j, half):
        return self.terms[j](2 * half + self.core)

    def start(self, j):
        for half in (1 - self.y, self.y):
            self.copy(j, half).start()

    def add(self, j, half):
        self.copy(j, half).wait_recv()
        own = self.mine(j, half)

        @pl.loop(0, self.arrived[j].shape[1])
        def _(i):
            own[i] = (own[i].astype(F32) + self.arrived[j][half, i].astype(F32)).astype(BF16)

    def finish(self):
        for half in (0, 1):
            for j in range(len(self.terms)):
                self.copy(j, half).wait_send()


class LineSum:
    @classmethod
    def scratch(cls, count):
        return [pltpu.SemaphoreType.DMA((count,))] * 2

    def __init__(self, core_sum, arrived, sems):
        self.core_sum, self.arrived = core_sum, arrived
        self.send, self.recv = sems
        self.shard, self.y = core_sum.shard, core_sum.y
        _, self.y_mate = mates()

    def copy(self, j):
        return pltpu.make_async_remote_copy(
            src_ref=self.core_sum.mine(j, 1 - self.y), dst_ref=self.arrived[j],
            send_sem=self.send.at[j], recv_sem=self.recv.at[j],
            device_id=(self.y_mate, self.shard), device_id_type=MESH_ID,
        )

    def start(self, j):
        self.core_sum.add(j, 1 - self.y)
        self.copy(j).start()
        self.core_sum.add(j, self.y)

    def add(self, j):
        self.copy(j).wait_recv()
        own = self.core_sum.mine(j, self.y)

        @pl.loop(0, self.arrived[j].shape[0])
        def _(i):
            own[i] = (own[i].astype(F32) + self.arrived[j][i].astype(F32)).astype(BF16)

    def finish(self):
        self.core_sum.finish()
        for j in range(len(self.arrived)):
            self.copy(j).wait_send()


def split_gains(ref, row, values):
    size = ref.shape[2]
    for i in range(ref.shape[0]):
        ref[i, row : row + 1] = values[:, i * size : (i + 1) * size]


def norm_backward(values, gain, grad):
    scale = rms_scale(values)
    e = grad * gain
    back = scale * e - values * (scale * scale * scale) * jnp.mean(values * e, axis=1, keepdims=True)
    return back, jnp.sum(grad * values * scale, axis=0, keepdims=True)


def mlp_kernel(
    lengths_ref, normed_ref, middle_ref, gains_ref, g_low_ref, weights_ref, down_ref,
    quarter_gu_out, quarter_down_out, mixed_ref, g_middle_ref, gain_ref,
    normed, g_low, weights, down, hidden, grads, parts, mixed_parts, term_down,
    core_down, core_first, core_second, line_down, line_first, line_second, *sems,
):
    sems = list(sems)

    def take(n):
        taken = tuple(sems[:n])
        del sems[:n]
        return taken

    group, shard, z, x = place()
    core_mate, y_mate = mates()
    rows, width = normed_ref.shape
    size = hidden.shape[2]
    load_sem, out_sem = take(2)
    loads = [
        pltpu.make_async_copy(source, target, load_sem.at[i])
        for i, (source, target) in enumerate(((weights_ref, weights), (down_ref, down), (g_low_ref, g_low)))
    ]
    for copy in loads:
        copy.start()
    gather = Gather(normed, take(2))
    scatter = Scatter.of(parts, take(5))
    mixed_scatter = Scatter.of(mixed_parts, take(5))
    middle_tile = N_Z * N_X // 2
    core_sum = CoreSum(
        [lambda q: term_down.at[q], lambda q: weights.at[0:middle_tile, q], lambda q: weights.at[middle_tile : 2 * middle_tile, q]],
        [core_down, core_first, core_second], take(2),
    )
    line_sum = LineSum(core_sum, [line_down, line_first, line_second], take(2))
    greet(line_peers() + [((core_mate, shard), True), ((y_mate, shard), True)])
    normed[shard] = normed_ref[...]
    gather.start()
    gather.step(1)
    gather.step(2)
    for copy in loads:
        copy.wait()

    @pl.loop(0, N_Z)
    def _(i):
        @pl.when(i == 1)
        def _():
            gather.step(3)

        @pl.when(i == N_Z - 1)
        def _():
            for k in range(1, N_Z):
                mixed_scatter.start(k)

        origin = nearest(z, i)
        gather.wait_across(origin)
        pair = pl.ds(origin * N_X, N_X)
        left = normed[pair].reshape(N_X * rows, width)
        g_left = g_low[pair].reshape(N_X * rows, width)
        for first in range(0, size, size // 2):
            part, up_part = slice(first, first + size // 2), slice(size + first, size + first + size // 2)
            act, slope = gelu_parts(mm(left, weights[:, :, :, part].reshape(width, size // 2)))
            up = mm(left, weights[:, :, :, up_part].reshape(width, size // 2))
            g_hidden = mm_nt(g_left, down[part])
            hidden[origin, :, part] = (act * up).astype(BF16)
            grads[origin, :, part] = (g_hidden * up * slope).astype(BF16)
            grads[origin, :, up_part] = (g_hidden * act).astype(BF16)
        back = mm_nt(grads[origin], weights[...].reshape(width, 2 * size))
        parts[pair] = back.astype(BF16).reshape(N_X, rows, width)
        mixed_parts[pair] = mm(hidden[origin], down[...]).astype(BF16).reshape(N_X, rows, width)

    mixed_scatter.start(0)
    for i in range(N_Z):
        scatter.start(i)
    tile = normed.shape[2] // (N_Z * N_X)
    total = N_Z * N_X * rows

    @pl.loop(0, size // tile)
    def _(i):
        left = hidden[:, :, pl.ds(i * tile, tile)].reshape(total, tile)
        term = mm_tn(left, g_low[...].reshape(total, width)).astype(BF16)
        step = term_down.shape[2]
        for j in range(tile // step):
            chunk = i * (tile // step) + j
            term_down[chunk // term_down.shape[1], chunk % term_down.shape[1]] = term[j * step : (j + 1) * step]

    core_sum.start(0)

    def gu_terms(first, last):
        @pl.loop(first, last)
        def _(i):
            left = normed[:, :, pl.ds(i * tile, tile)].reshape(total, tile)
            term = mm_tn(left, grads[...].reshape(total, 2 * size)).astype(BF16)
            weights[i] = term.reshape(weights.shape[1:])

    gu_terms(0, middle_tile)
    core_sum.start(1)
    line_sum.start(0)
    gu_terms(middle_tile, 2 * middle_tile)
    core_sum.start(2)
    line_sum.start(1)
    mixed_scatter.step(0)
    line_sum.start(2)
    mixed_scatter.step(1)
    mixed_scatter.step(2)
    scatter.step(0)
    mixed_scatter.last(g_middle_ref)
    _, live = positions_in_run([lengths_ref[0, i] for i in range(3)], rows)
    mixed_ref[...] = ((middle_ref[...] + g_middle_ref[...]) * live).astype(BF16)
    scatter.step(1)
    scatter.step(2)
    outs = []
    for j, out in enumerate((quarter_down_out, quarter_gu_out.at[0:middle_tile], quarter_gu_out.at[middle_tile : 2 * middle_tile])):
        line_sum.add(j)
        outs.append(pltpu.make_async_copy(core_sum.mine(j, group // 2), out, out_sem.at[j]))
        outs[-1].start()
    scatter.last(g_middle_ref)
    gain = jnp.concatenate([gains_ref[i] for i in range(N_Z * N_X)], axis=1)[1:2]
    back, gain_term = norm_backward(middle_ref[...], gain, g_middle_ref[...])
    g_middle_ref[...] = g_low[shard].astype(F32) + back
    gain_ref[...] = jnp.zeros_like(gain_ref)
    split_gains(gain_ref, 1, gain_term)
    gather.finish()
    line_sum.finish()
    mixed_scatter.finish()
    scatter.finish()
    for copy in outs:
        copy.wait()


def mlp_call(lengths, normed, middle, gains, g_low, weights, down):
    rows, width = normed.shape
    shards, groups, quarter_rows, both = weights.shape
    size = down.shape[0]
    dma = pltpu.SemaphoreType.DMA
    shape = jax.ShapeDtypeStruct
    down_term = (size // groups // 64, 64, width)
    gu_term = (shards, quarter_rows, both)
    terms = [down_term] + [(shards // 2, quarter_rows, both)] * 2
    pairs = (N_Z, N_X * rows)
    scratch = [
        (shards, rows, width), (shards, rows, width), weights.shape, down.shape, pairs + (size,), pairs + (both,),
        (shards, rows, width), (shards, rows, width), (groups,) + down_term,
        *[(2,) + term for term in terms], *terms,
    ]
    return pl.pallas_call(
        mlp_kernel,
        out_shape=[
            shape(gu_term, BF16),
            shape(down_term, BF16),
            shape((rows, width), BF16),
            shape((rows, width), F32),
            shape(gains.shape, F32),
        ],
        in_specs=[pl.BlockSpec(memory_space=pltpu.SMEM)] + [vmem_spec()] * 3 + [any_spec()] * 3,
        out_specs=[any_spec()] * 2 + [vmem_spec()] * 3,
        scratch_shapes=[pltpu.VMEM(dims, BF16) for dims in scratch]
        + [dma((3,)), dma((3,))]
        + Gather.scratch()
        + Scatter.scratch(rows, width)
        + Scatter.scratch(rows, width)
        + CoreSum.scratch(3)
        + LineSum.scratch(3),
        compiler_params=pltpu.CompilerParams(collective_id=2, has_side_effects=True, vmem_limit_bytes=VMEM_LIMIT),
        name="mlp",
    )(lengths, normed, middle, gains, g_low, weights, down)


def mixer_backward(g_merged, saved, pos, vec, gates):
    gate, linear, rate_pre, input_pre, state = saved
    width = linear.shape[1]
    masks = [(pos >= k).astype(F32) for k in (1, 2, 3)]
    later = [roll_rows(jnp.broadcast_to(masks[k - 1], linear.shape), -k) for k in (1, 2, 3)]
    conv = conv_rows(linear, vec[0:4], vec[4:5], masks)
    input_gate = sigmoid(input_pre)
    decay = vec[7:8]
    rate, a, weight_in = decay_terms(rate_pre, decay)
    act, slope = gelu_parts(gate)
    g_gate = (g_merged * state * slope).astype(BF16)
    lam = g_merged * act
    mult = roll_rows(a, -1) * later[0]
    step = 1
    while step < CAP:
        lam = lam + mult * roll_rows(lam, -step)
        if 2 * step < CAP:
            mult = mult * roll_rows(mult, -step)
        step *= 2
    g_a = lam * (roll_rows(state, 1) * masks[0])
    g_keep = g_a * a - lam * (input_gate * conv) * (a * a) / weight_in
    g_rate = (g_keep * (-RATE_SCALE * softplus_neg(decay)) * (rate * (1.0 - rate))).astype(BF16)
    g_decay = g_keep * (RATE_SCALE * rate) * sigmoid(-decay)
    flow = lam * weight_in
    g_inp = (flow * conv * (input_gate * (1.0 - input_gate))).astype(BF16)
    g_conv = flow * input_gate + mm(jnp.concatenate([g_rate, g_inp], axis=1), gates)
    g_linear = g_conv * vec[0:1]
    sums = [jnp.sum(g_conv * linear, axis=0, keepdims=True)]
    for k in (1, 2, 3):
        g_linear = g_linear + vec[k : k + 1] * (roll_rows(g_conv, -k) * later[k - 1])
        sums.append(jnp.sum(g_conv * (roll_rows(linear, k) * masks[k - 1]), axis=0, keepdims=True))
    for value in (g_conv, g_rate.astype(F32), g_inp.astype(F32), g_decay):
        sums.append(jnp.sum(value, axis=0, keepdims=True))
    return g_gate, g_linear.astype(BF16), jnp.concatenate(sums, axis=0), conv.astype(BF16), g_rate, g_inp


def backward_kernel(
    lengths_ref, tokens_ref, g_middle_ref, gains_ref, gain_in_ref, vec_ref, gates_ref, out_proj_ref,
    quarter_gu_ref, quarter_down_ref, weights_ref, saved_ref, merged_ref, gathered_ref,
    grad_gate_out, grad_up_out, grad_down_out, gl_out, out_out, bd_out, grad_tokens_ref, small_out_ref,
    g_mix, normed, weights, saved, merged, grads, parts, term_gl, term_out, term_bd, total_bd, total_small, result,
    core_gl, core_out, core_bd, line_gl, line_out, line_bd,
    gain_terms, gains_got, packed, packs, *sems,
):
    sems = list(sems)

    def take(n):
        taken = tuple(sems[:n])
        del sems[:n]
        return taken

    group, shard, z, x = place()
    core_mate, y_mate = mates()
    shards = N_Z * N_X
    rows, width = tokens_ref.shape
    padded = vec_ref.shape[1]
    total = shards * rows
    chans = out_proj_ref.shape[0]
    half = quarter_gu_ref.shape[2] // 2
    quarter_rows = quarter_gu_ref.shape[1]
    load_sem, saved_sem, gain_send, gain_recv, pack_send, pack_recv = take(6)
    gather = Gather(g_mix, take(2))
    scatter = Scatter.of(parts, take(5))
    core_sum = CoreSum(
        [lambda q: term_gl.at[q], lambda q: term_out.at[q], lambda q: term_bd.at[q]], [core_gl, core_out, core_bd], take(2)
    )
    line_sum = LineSum(core_sum, [line_gl, line_out, line_bd], take(2))

    def columns(ref):
        return lambda origin, quarter: ref.at[pl.ds(quarter * quarter_rows, quarter_rows), pl.ds(origin * half, half)]

    gate_exchange = Exchange([lambda to: quarter_gu_ref.at[to, :, 0:half]], [columns(grad_gate_out)], shards, take(4))
    up_exchange = Exchange([lambda to: quarter_gu_ref.at[to, :, half : 2 * half]], [columns(grad_up_out)], shards, take(4))
    down_exchange = Exchange([lambda to: quarter_down_ref], [lambda origin, quarter: grad_down_out.at[quarter]], 1, take(4))
    gl_exchange = Exchange(
        [lambda to: term_gl.at[group, to]], [lambda origin, quarter: gl_out.at[origin, quarter]], shards, take(4)
    )
    out_exchange = Exchange([lambda to: term_out.at[group]], [lambda origin, quarter: out_out.at[quarter]], 1, take(4))
    bd_exchange = Exchange([lambda to: term_bd.at[group]], [lambda origin, quarter: bd_out.at[quarter]], 1, take(4))

    def gain_copy(to, origin):
        return pltpu.make_async_remote_copy(
            src_ref=gain_terms.at[to], dst_ref=gains_got.at[origin], send_sem=gain_send.at[to], recv_sem=gain_recv.at[origin],
            device_id=(group, to), device_id_type=MESH_ID,
        )

    def pack_copy(i):
        return pltpu.make_async_remote_copy(
            src_ref=packed, dst_ref=packs.at[i], send_sem=pack_send.at[i], recv_sem=pack_recv.at[i],
            device_id=((core_mate, y_mate, 3 - group)[i], shard), device_id_type=MESH_ID,
        )

    def saved_copy(i):
        return pltpu.make_async_copy(saved_ref.at[nearest(z, i)], saved.at[i % 2], saved_sem.at[i % 2])

    loads = [
        pltpu.make_async_copy(source, target, load_sem.at[i])
        for i, (source, target) in enumerate((
            (weights_ref, weights), (gathered_ref, normed), (merged_ref, merged),
        ))
    ]
    for copy in loads:
        copy.start()
    saved_copy(0).start()
    greet(all_peers() + [((3 - group, shard), True)])
    g_mix[shard] = g_middle_ref[...].astype(BF16)
    gather.start()
    gate_exchange.start()
    down_exchange.start()
    down_exchange.spread()
    total_small[...] = jnp.zeros_like(total_small)
    total_bd[...] = jnp.zeros_like(total_bd)
    gather.step(1)
    gather.step(2)
    for copy in loads:
        copy.wait()

    @pl.loop(0, N_Z)
    def _(i):
        @pl.when(i == 1)
        def _():
            gather.step(3)
            up_exchange.start()

        @pl.when(i == 2)
        def _():
            gate_exchange.spread()

        origin = nearest(z, i)
        gather.wait_across(origin)
        saved_copy(i).wait()

        @pl.when(i < N_Z - 1)
        def _():
            saved_copy(i + 1).start()

        pair = pl.ds(origin * N_X, N_X)
        g_merged = mm_nt(g_mix[pair].reshape(N_X * rows, width), out_proj_ref[...])
        g_merged = jnp.concatenate([g_merged, jnp.zeros((N_X * rows, padded - chans), F32)], axis=1)
        where = normed[pair, :, width:].reshape(N_X * rows, normed.shape[2] - width)[:, :1].astype(F32)
        g_gate, g_linear, sums, low, g_rate, g_inp = mixer_backward(
            g_merged, [saved[i % 2, j] for j in range(5)], where, vec_ref[...], gates_ref[...]
        )
        grads[origin, :, :padded] = g_gate
        grads[origin, :, padded:] = g_linear
        total_small[...] += sums
        total_bd[0] += mm_tn(g_rate, low)
        total_bd[1] += mm_tn(g_inp, low)
        back = mm_nt(grads[origin], weights[...].reshape(width, 2 * padded))
        parts[pair] = back.astype(BF16).reshape(N_X, rows, width)

    for i in range(N_Z):
        scatter.start(i)
    tile = width // shards

    @pl.loop(0, shards)
    def _(i):
        left = normed[:, :, pl.ds(i * tile, tile)].reshape(total, tile)
        term = mm_tn(left, grads[...].reshape(total, 2 * padded)).astype(BF16)
        term_gl[:, i] = term.reshape(term_gl.shape[0], term_gl.shape[2], 2 * padded)

    core_sum.start(0)
    up_exchange.spread()
    scatter.step(0)
    term = mm_tn(merged[...].reshape(total, padded), g_mix[...].reshape(total, width))
    term_out[...] = term[:chans].astype(BF16).reshape(term_out.shape)
    size = term_bd.shape[0] * term_bd.shape[1] * term_bd.shape[2] // 2
    both = []
    for i in range(2):
        heads = [slice(h * size, (h + 1) * size) for h in range(chans // size)]
        both.append(jnp.concatenate([total_bd[i, part, part] for part in heads], axis=1))
    term_bd[...] = jnp.concatenate(both, axis=0).astype(BF16).reshape(term_bd.shape)
    core_sum.start(1)
    core_sum.start(2)
    for j in range(3):
        line_sum.start(j)
    scatter.step(1)
    scatter.step(2)
    scatter.last(result)
    _, live = positions_in_run([lengths_ref[0, i] for i in range(3)], rows)
    masked = tokens_ref[...].astype(F32) * live
    gain = jnp.concatenate([gains_ref[i] for i in range(shards)], axis=1)[0:1]
    back, gain_term = norm_backward(masked, gain, result[...])
    grad_tokens_ref[...] = ((g_middle_ref[...] + back) * live).astype(BF16)
    gain_terms[...] = gain_in_ref[...]
    split_gains(gain_terms, 0, gain_term)
    for i in range(1, shards):
        gain_copy((shard + i) % shards, shard).start()
    line_sum.add(0)
    gl_exchange.start()
    for j, one in ((1, out_exchange), (2, bd_exchange)):
        line_sum.add(j)
        one.start()
        one.spread()
    gl_exchange.spread()
    down_exchange.relay()
    gate_exchange.relay()
    up_exchange.relay()
    gain_sum = gain_terms[shard]
    for i in range(1, shards):
        origin = (shard + i) % shards
        gain_copy(origin, origin).wait_recv()
        gain_sum = gain_sum + gains_got[origin]
    packed[0:8] = total_small[...]
    packed[8:16] = jnp.concatenate([gain_sum, jnp.zeros((8, padded - gain_sum.shape[1]), F32)], axis=1)
    for i in range(3):
        pack_copy(i).start()
    packs_sum = packed[...]
    for i in range(3):
        pack_copy(i).wait_recv()
        packs_sum = packs_sum + packs[i]
    small_out_ref[...] = packs_sum
    for one in (out_exchange, bd_exchange, gl_exchange):
        one.relay()
    for i in range(1, shards):
        gain_copy((shard + i) % shards, shard).wait_send()
    for i in range(3):
        pack_copy(i).wait_send()
    for one in (gather, scatter, line_sum):
        one.finish()
    for one in (down_exchange, gate_exchange, up_exchange, out_exchange, bd_exchange, gl_exchange):
        one.arrive()
        one.finish()


def backward_call(
    head, lengths, tokens, g_middle, gains, gain_terms, vec, gates, out_proj, quarter_gu, quarter_down, weights, saved, merged,
    gathered,
):
    rows, width = tokens.shape
    shards, groups = N_Z * N_X, weights.shape[1]
    quarter_rows, both = quarter_gu.shape[1:]
    padded = vec.shape[1]
    chans = out_proj.shape[0]
    dma = pltpu.SemaphoreType.DMA
    shape = jax.ShapeDtypeStruct
    terms = [
        (groups, shards, quarter_rows, 2 * padded),
        (groups, chans // groups // 16, 16, width),
        (groups, 2 * head // groups // 16, 16, chans),
    ]
    packed = (16, padded)
    scratch = [
        ((shards, rows, width), BF16), (gathered.shape, BF16), (weights.shape, BF16), ((2,) + saved.shape[1:], F32),
        (merged.shape, BF16), ((N_Z, N_X * rows, 2 * padded), BF16), ((shards, rows, width), BF16),
        *[(term, BF16) for term in terms], ((2, padded, padded), F32), (vec.shape, F32), ((rows, width), F32),
        *[((2,) + term[1:], BF16) for term in terms], *[(term[1:], BF16) for term in terms],
        (gains.shape, F32), (gains.shape, F32), (packed, F32), ((3,) + packed, F32),
    ]
    return pl.pallas_call(
        backward_kernel,
        out_shape=[
            shape((groups * quarter_rows, shards * both // 2), BF16),
            shape((groups * quarter_rows, shards * both // 2), BF16),
            shape((groups,) + quarter_down.shape, BF16),
            shape((shards, groups) + terms[0][2:], BF16),
            shape(terms[1], BF16),
            shape(terms[2], BF16),
            shape((rows, width), BF16),
            shape(packed, F32),
        ],
        in_specs=[pl.BlockSpec(memory_space=pltpu.SMEM)] + [vmem_spec()] * 7 + [any_spec()] * 6,
        out_specs=[any_spec()] * 6 + [vmem_spec()] * 2,
        scratch_shapes=[pltpu.VMEM(dims, kind) for dims, kind in scratch]
        + [dma((3,)), dma((2,)), dma((shards,)), dma((shards,)), dma((3,)), dma((3,))]
        + Gather.scratch()
        + Scatter.scratch(rows, width)
        + CoreSum.scratch(3)
        + LineSum.scratch(3)
        + Exchange.scratch(shards, 1)
        + Exchange.scratch(shards, 1)
        + Exchange.scratch(1, 1)
        + Exchange.scratch(shards, 1)
        + Exchange.scratch(1, 1) * 2,
        compiler_params=pltpu.CompilerParams(collective_id=3, has_side_effects=True, vmem_limit_bytes=VMEM_LIMIT),
        name="mixer_backward",
    )(
        lengths, tokens, g_middle, gains, gain_terms, vec, gates, out_proj, quarter_gu, quarter_down, weights, saved, merged,
        gathered,
    )


def widen_kernel(
    mixed_ref, tokens_ref, small_ref, gate_ref, up_ref, down_ref, gl_ref, out_ref, bd_ref,
    mixed_out, tokens_out, gain1_out, gate_in_out, linear_in_out, kernel_out, bias_out, rate_out, rate_bias_out, input_out,
    input_bias_out, decay_out, out_out, gain2_out, gate_out, up_out, down_out,
):
    mixed_out[...] = mixed_ref[...]
    tokens_out[...] = tokens_ref[...]
    for out, ref in ((gate_out, gate_ref), (up_out, up_ref), (down_out, down_ref), (out_out, out_ref)):
        out[...] = ref[...].astype(F32)
    shards = gl_ref.shape[0]
    chans, padded = gate_in_out.shape[1] // shards, gl_ref.shape[3] // 2
    for out, first in ((gate_in_out, 0), (linear_in_out, padded)):
        for s in range(shards):
            out[:, s * chans : (s + 1) * chans] = gl_ref[s, 0, :, first : first + chans].astype(F32)

    @pl.when(pl.program_id(0) == 0)
    def _():
        size = rate_out.shape[0]
        rate_out[...] = bd_ref[:size].astype(F32)
        input_out[...] = bd_ref[size:].astype(F32)
        kernel_out[...] = small_ref[0:4, :chans]
        for i, out in ((4, bias_out), (5, rate_bias_out), (6, input_bias_out), (7, decay_out), (8, gain1_out), (9, gain2_out)):
            out[...] = small_ref[i, : out.shape[0]]


def widen_call(mixed, grad_tokens, small, gate, up, down, gl, out, bd, gain_size):
    shards, groups, quarter_rows, both = gl.shape
    chans = out.shape[0]

    def rows_of(dims):
        return pl.BlockSpec((dims[0] // groups, dims[1]), lambda i: (i, 0))

    def whole(dims):
        return pl.BlockSpec(dims, lambda i: (0,) * len(dims))

    wide = (groups * quarter_rows, shards * chans)
    block = (bd.shape[0] // 2, bd.shape[1])
    shapes = [
        mixed.shape, grad_tokens.shape, (gain_size,), wide, wide, (4, chans), (chans,), block, (chans,), block, (chans,), (chans,),
        out.shape, (gain_size,), gate.shape, up.shape, down.shape,
    ]
    specs = [whole(dims) if len(dims) == 1 or dims in ((4, chans), block) else rows_of(dims) for dims in shapes]
    return pl.pallas_call(
        widen_kernel,
        grid=(groups,),
        in_specs=[rows_of(mixed.shape), rows_of(grad_tokens.shape), whole(small.shape)]
        + [rows_of(a.shape) for a in (gate, up, down)]
        + [pl.BlockSpec((shards, 1, quarter_rows, both), lambda i: (0, i, 0, 0)), rows_of(out.shape), whole(bd.shape)],
        out_specs=specs,
        out_shape=[jax.ShapeDtypeStruct(dims, BF16 if i < 2 else F32) for i, dims in enumerate(shapes)],
        compiler_params=pltpu.CompilerParams(vmem_limit_bytes=VMEM_LIMIT),
        name="widen",
    )(mixed, grad_tokens, small, gate, up, down, gl, out, bd)


def per_device_split(
    tokens, lengths, cotangent, norm1_gain, gate_in, linear_in, conv_kernel, conv_bias, rate_weight,
    rate_bias, input_weight, input_bias, decay_param, out_proj, norm2_gain, mlp_gate, mlp_up, mlp_down,
):
    chans, size = rate_weight.shape
    gathered, weights, mlp_weights, gains, saved, merged, middle, normed_two, vec, gates, g_low = forward_call(
        lengths, tokens, cotangent,
        (norm1_gain, norm2_gain, conv_kernel, conv_bias, rate_bias, input_bias, decay_param, rate_weight.T, input_weight.T),
        out_proj, gate_in, linear_in, mlp_gate, mlp_up,
    )
    quarter_gu, quarter_down, mixed, g_middle, gain_terms = mlp_call(
        lengths, normed_two, middle, gains, g_low, mlp_weights, mlp_down
    )
    grad_gate, grad_up, grad_down, gl, grad_out, bd, grad_tokens, small = backward_call(
        size, lengths, tokens, g_middle, gains, gain_terms, vec, gates, out_proj, quarter_gu, quarter_down, weights, saved, merged,
        gathered,
    )
    outs = list(widen_call(
        mixed, grad_tokens, small, grad_gate, grad_up, grad_down.reshape(mlp_down.shape), gl, grad_out.reshape(out_proj.shape),
        bd.reshape(2 * size, chans), norm1_gain.shape[0],
    ))
    for i in (7, 9):
        outs[i] = outs[i].T
    return tuple(outs)


def as_sent(shard):
    return jax.tree.map(lambda a: a.astype(jnp.bfloat16) if a.dtype == jnp.float32 else a, shard)


def layout(counts, row_count):
    first = counts[0]
    second = first + counts[1]
    run_ends = jnp.stack([first, second, second + counts[2], second + counts[2] + counts[3]])
    positions = jnp.arange(row_count, dtype=jnp.int32)
    segment_ids = jnp.sum((positions[:, None] >= run_ends[None, :-1]).astype(jnp.int32), axis=1)
    live_rows = (positions < run_ends[-2]).astype(jnp.float32)
    return (segment_ids, live_rows)


def earlier_ids(segment_ids, offset):
    filler = jnp.full((offset,), -1, dtype=jnp.int32)
    return jnp.concatenate([filler, segment_ids[:-offset]])


def normalize(values, gain_vec):
    scale = lax.rsqrt(jnp.mean(values * values, axis=1, keepdims=True) + EPSILON)
    return values * scale * gain_vec


def convolve(linear_out, kernel, shift_vec, segment_ids):
    summed = linear_out * kernel[0] + shift_vec
    for offset in range(1, kernel.shape[0]):
        shifted = jnp.concatenate(
            [jnp.zeros((offset, linear_out.shape[1]), linear_out.dtype), linear_out[:-offset]],
            axis=0,
        )
        same_seq = (earlier_ids(segment_ids, offset) == segment_ids).astype(linear_out.dtype)
        summed = summed + kernel[offset] * shifted * same_seq[:, None]
    return summed


def combine_pairs(earlier_pair, later_pair):
    return (earlier_pair[0] * later_pair[0], later_pair[0] * earlier_pair[1] + later_pair[1])


def recurrence(rate_pre, input_pre, inflow, decay_vec, segment_ids):
    rate_gate = jax.nn.sigmoid(rate_pre)
    opened = jax.nn.sigmoid(input_pre)
    log_keep = -RATE_SCALE * rate_gate * jax.nn.softplus(-decay_vec)
    factor = jnp.exp(log_keep)
    weight_in = jnp.sqrt(-jnp.expm1(2.0 * log_keep))
    same_run = (earlier_ids(segment_ids, 1) == segment_ids).astype(factor.dtype)
    carried, states = lax.associative_scan(
        combine_pairs, (factor * same_run[:, None], weight_in * opened * inflow), axis=0
    )
    return states


def gated_gelu(gate_vals, up_vals):
    return jax.nn.gelu(gate_vals) * up_vals


def product(left, right):
    return jnp.dot(left, right, preferred_element_type=jnp.float32)


def contract(left, right):
    return jnp.einsum("ti,tj->ij", left, right, preferred_element_type=jnp.float32)


def back_dot(grad_vals, weight):
    return jnp.einsum("tj,ij->ti", grad_vals, weight, preferred_element_type=jnp.float32)


def blocked(values, weight):
    row_count = values.shape[0]
    size = weight.shape[1]
    heads = weight.shape[0] // size
    return jnp.einsum(
        "thj,hjk->thk",
        values.reshape(row_count, heads, size),
        weight.reshape(heads, size, size),
        preferred_element_type=jnp.float32,
    ).reshape(row_count, heads * size)


def block_terms(values, grad_vals, size):
    row_count = values.shape[0]
    heads = values.shape[1] // size
    terms = jnp.einsum(
        "thj,thk->hjk",
        values.reshape(row_count, heads, size),
        grad_vals.reshape(row_count, heads, size),
        preferred_element_type=jnp.float32,
    )
    return terms.reshape(heads * size, size)


def block_back(grad_vals, weight):
    row_count = grad_vals.shape[0]
    size = weight.shape[1]
    heads = weight.shape[0] // size
    return jnp.einsum(
        "thk,hjk->thj",
        grad_vals.reshape(row_count, heads, size),
        weight.reshape(heads, size, size),
        preferred_element_type=jnp.float32,
    ).reshape(row_count, heads * size)


def per_device_general(
    tokens,
    lengths,
    cotangent,
    norm1_gain,
    gate_in,
    linear_in,
    conv_kernel,
    conv_bias,
    rate_weight,
    rate_bias,
    input_weight,
    input_bias,
    decay_param,
    out_proj,
    norm2_gain,
    mlp_gate,
    mlp_up,
    mlp_down,
):
    row_count = tokens.shape[0]
    segment_ids, live_rows = layout(lengths[0], row_count)
    live_col = live_rows[:, None]
    mixer_full = (
        lax.all_gather(norm1_gain, "shard", axis=0, tiled=True),
        lax.all_gather(gate_in, "shard", axis=0, tiled=True),
        lax.all_gather(linear_in, "shard", axis=0, tiled=True),
        lax.all_gather(conv_kernel, "shard", axis=1, tiled=True),
        lax.all_gather(conv_bias, "shard", axis=0, tiled=True),
        lax.all_gather(rate_weight, "shard", axis=0, tiled=True),
        lax.all_gather(rate_bias, "shard", axis=0, tiled=True),
        lax.all_gather(input_weight, "shard", axis=0, tiled=True),
        lax.all_gather(input_bias, "shard", axis=0, tiled=True),
        lax.all_gather(decay_param, "shard", axis=0, tiled=True),
        lax.all_gather(out_proj, "shard", axis=0, tiled=True),
    )
    gain_first = mixer_full[0].astype(jnp.float32)
    kernel_full = mixer_full[3].astype(jnp.float32)
    kernel_shift = mixer_full[4].astype(jnp.float32)
    rate_shift = mixer_full[6].astype(jnp.float32)
    input_shift = mixer_full[8].astype(jnp.float32)
    decay_full = mixer_full[9].astype(jnp.float32)
    block_size = mixer_full[5].shape[1]
    masked_in = tokens.astype(jnp.float32) * live_col
    normed_low = normalize(masked_in, gain_first).astype(jnp.bfloat16)
    gate_pre = product(normed_low, mixer_full[1])
    linear_out = product(normed_low, mixer_full[2])
    gate_act = jax.nn.gelu(gate_pre)
    conv_out = convolve(linear_out, kernel_full, kernel_shift, segment_ids)
    conv_low = conv_out.astype(jnp.bfloat16)
    rate_pre = blocked(conv_low, mixer_full[5]) + rate_shift
    input_pre = blocked(conv_low, mixer_full[7]) + input_shift
    states = recurrence(rate_pre, input_pre, conv_out, decay_full, segment_ids)
    merged_low = (gate_act * states).astype(jnp.bfloat16)
    middle = masked_in + product(merged_low, mixer_full[10])
    mlp_full = (
        lax.all_gather(norm2_gain, "shard", axis=0, tiled=True),
        lax.all_gather(mlp_gate, "shard", axis=0, tiled=True),
        lax.all_gather(mlp_up, "shard", axis=0, tiled=True),
        lax.all_gather(mlp_down, "shard", axis=0, tiled=True),
    )
    gain_second = mlp_full[0].astype(jnp.float32)
    normed_two = normalize(middle, gain_second).astype(jnp.bfloat16)
    gate_mlp = product(normed_two, mlp_full[1])
    up_mlp = product(normed_two, mlp_full[2])
    hidden_low = gated_gelu(gate_mlp, up_mlp).astype(jnp.bfloat16)
    mixed_out = ((middle + product(hidden_low, mlp_full[3])) * live_col).astype(jnp.bfloat16)
    grad_out = cotangent.astype(jnp.float32) * live_col
    grad_down = grad_out.astype(jnp.bfloat16)
    again_mlp = (
        lax.all_gather(mlp_gate, "shard", axis=0, tiled=True),
        lax.all_gather(mlp_up, "shard", axis=0, tiled=True),
        lax.all_gather(mlp_down, "shard", axis=0, tiled=True),
    )
    term_down = contract(hidden_low, grad_down)
    part_down = lax.psum_scatter(
        term_down.astype(jnp.bfloat16), "shard", scatter_dimension=0, tiled=True
    ).astype(jnp.float32)
    grad_hidden = back_dot(grad_down, again_mlp[2])
    unused_val, hidden_back = jax.vjp(gated_gelu, gate_mlp, up_mlp)
    grad_gate_mlp, grad_up_mlp = hidden_back(grad_hidden)
    gate_mlp_low = grad_gate_mlp.astype(jnp.bfloat16)
    up_mlp_low = grad_up_mlp.astype(jnp.bfloat16)
    term_gate_mlp = contract(normed_two, gate_mlp_low)
    term_up_mlp = contract(normed_two, up_mlp_low)
    grad_normed_two = back_dot(gate_mlp_low, again_mlp[0]) + back_dot(up_mlp_low, again_mlp[1])
    unused_two, second_back = jax.vjp(normalize, middle, gain_second)
    grad_middle_norm, term_gain_two = second_back(grad_normed_two)
    parts_mlp = (
        lax.psum_scatter(
            term_gain_two.astype(jnp.bfloat16), "shard", scatter_dimension=0, tiled=True
        ).astype(jnp.float32),
        lax.psum_scatter(
            term_gate_mlp.astype(jnp.bfloat16), "shard", scatter_dimension=0, tiled=True
        ).astype(jnp.float32),
        lax.psum_scatter(
            term_up_mlp.astype(jnp.bfloat16), "shard", scatter_dimension=0, tiled=True
        ).astype(jnp.float32),
    )
    grad_middle = grad_out + grad_middle_norm
    grad_mix_low = grad_middle.astype(jnp.bfloat16)
    again_mixer = (
        lax.all_gather(gate_in, "shard", axis=0, tiled=True),
        lax.all_gather(linear_in, "shard", axis=0, tiled=True),
        lax.all_gather(rate_weight, "shard", axis=0, tiled=True),
        lax.all_gather(input_weight, "shard", axis=0, tiled=True),
        lax.all_gather(out_proj, "shard", axis=0, tiled=True),
    )
    term_out = contract(merged_low, grad_mix_low)
    grad_merged = back_dot(grad_mix_low, again_mixer[4])
    grad_states = grad_merged * gate_act
    unused_three, gelu_back = jax.vjp(jax.nn.gelu, gate_pre)
    gate_low = gelu_back(grad_merged * states)[0].astype(jnp.bfloat16)
    unused_four, scan_back = jax.vjp(
        partial(recurrence, segment_ids=segment_ids), rate_pre, input_pre, conv_out, decay_full
    )
    grad_rate, grad_input, grad_flow, term_decay = scan_back(grad_states)
    rate_low = grad_rate.astype(jnp.bfloat16)
    input_low = grad_input.astype(jnp.bfloat16)
    term_rate = block_terms(conv_low, rate_low, block_size)
    term_input = block_terms(conv_low, input_low, block_size)
    term_rate_shift = jnp.sum(rate_low.astype(jnp.float32), axis=0)
    term_input_shift = jnp.sum(input_low.astype(jnp.float32), axis=0)
    grad_conv = (
        grad_flow + block_back(rate_low, again_mixer[2]) + block_back(input_low, again_mixer[3])
    )
    unused_five, conv_back = jax.vjp(
        partial(convolve, segment_ids=segment_ids), linear_out, kernel_full, kernel_shift
    )
    grad_linear, term_kernel, term_kernel_shift = conv_back(grad_conv)
    linear_low = grad_linear.astype(jnp.bfloat16)
    term_gate_in = contract(normed_low, gate_low)
    term_linear = contract(normed_low, linear_low)
    grad_normed = back_dot(gate_low, again_mixer[0]) + back_dot(linear_low, again_mixer[1])
    unused_six, first_back = jax.vjp(normalize, masked_in, gain_first)
    grad_masked, term_gain_one = first_back(grad_normed)
    grad_tokens = ((grad_middle + grad_masked) * live_col).astype(jnp.bfloat16)
    small_terms = (
        term_gain_one,
        term_kernel,
        term_kernel_shift,
        term_rate,
        term_rate_shift,
        term_input,
        term_input_shift,
        term_decay,
    )
    placed = tuple((term for term in small_terms))
    mixer_terms = (
        placed[0],
        term_gate_in,
        term_linear,
        placed[1],
        placed[2],
        placed[3],
        placed[4],
        placed[5],
        placed[6],
        placed[7],
        term_out,
    )
    parts_mixer = (
        lax.psum_scatter(
            mixer_terms[0].astype(jnp.bfloat16), "shard", scatter_dimension=0, tiled=True
        ).astype(jnp.float32),
        lax.psum_scatter(
            mixer_terms[1].astype(jnp.bfloat16), "shard", scatter_dimension=0, tiled=True
        ).astype(jnp.float32),
        lax.psum_scatter(
            mixer_terms[2].astype(jnp.bfloat16), "shard", scatter_dimension=0, tiled=True
        ).astype(jnp.float32),
        lax.psum_scatter(
            mixer_terms[3].astype(jnp.bfloat16), "shard", scatter_dimension=1, tiled=True
        ).astype(jnp.float32),
        lax.psum_scatter(
            mixer_terms[4].astype(jnp.bfloat16), "shard", scatter_dimension=0, tiled=True
        ).astype(jnp.float32),
        lax.psum_scatter(
            mixer_terms[5].astype(jnp.bfloat16), "shard", scatter_dimension=0, tiled=True
        ).astype(jnp.float32),
        lax.psum_scatter(
            mixer_terms[6].astype(jnp.bfloat16), "shard", scatter_dimension=0, tiled=True
        ).astype(jnp.float32),
        lax.psum_scatter(
            mixer_terms[7].astype(jnp.bfloat16), "shard", scatter_dimension=0, tiled=True
        ).astype(jnp.float32),
        lax.psum_scatter(
            mixer_terms[8].astype(jnp.bfloat16), "shard", scatter_dimension=0, tiled=True
        ).astype(jnp.float32),
        lax.psum_scatter(
            mixer_terms[9].astype(jnp.bfloat16), "shard", scatter_dimension=0, tiled=True
        ).astype(jnp.float32),
        lax.psum_scatter(
            mixer_terms[10].astype(jnp.bfloat16), "shard", scatter_dimension=0, tiled=True
        ).astype(jnp.float32),
    )
    shard_parts = tuple(parts_mixer) + (parts_mlp[0], parts_mlp[1], parts_mlp[2], part_down)
    totals = jax.tree.map(
        lambda part: part.astype(jnp.float32), lax.psum(as_sent(shard_parts), "group")
    )
    return (mixed_out, grad_tokens) + tuple(totals)


def solution(mesh):
    placed = (
        P(("group", "shard"), None),
        P(("group", "shard"), None),
        P(("group", "shard"), None),
        P("shard"),
        P("shard", None),
        P("shard", None),
        P(None, "shard"),
        P("shard"),
        P("shard", None),
        P("shard"),
        P("shard", None),
        P("shard"),
        P("shard"),
        P("shard", None),
        P("shard"),
        P("shard", None),
        P("shard", None),
        P("shard", None),
    )
    split_fits = FAST_MESH == tuple(mesh.shape[axis] for axis in ("group", "shard"))
    return jax.shard_map(
        per_device_split if split_fits else per_device_general,
        mesh=mesh,
        in_specs=placed,
        out_specs=(
            P(("group", "shard"), None),
            P(("group", "shard"), None),
            P("shard"),
            P("shard", None),
            P("shard", None),
            P(None, "shard"),
            P("shard"),
            P("shard", None),
            P("shard"),
            P("shard", None),
            P("shard"),
            P("shard"),
            P("shard", None),
            P("shard"),
            P("shard", None),
            P("shard", None),
            P("shard", None),
        ),
        check_vma=False,
    )
```

```python
from functools import partial

import jax
import jax.numpy as jnp
from jax import lax
from jax.experimental import pallas as pl
from jax.experimental.pallas import tpu as pltpu
from jax.sharding import PartitionSpec as P

FAST_MESH = (4, 8)
RATE_SCALE = 8.0
EPSILON = 1e-06
F32 = jnp.float32
BF16 = jnp.bfloat16
GELU_C = 0.7978845608028654
GELU_K = 0.044715
CAP = 128


def positions_in_run(counts, row_count):
    first = counts[0]
    second = first + counts[1]
    third = second + counts[2]
    rows = lax.broadcasted_iota(jnp.int32, (row_count, 1), 0).astype(F32)
    start = jnp.where(rows >= first, first, 0.0)
    start = jnp.where(rows >= second, second, start)
    start = jnp.where(rows >= third, third, start)
    return rows - start, (rows < third).astype(F32)


def gelu_parts(x):
    t = jnp.tanh(GELU_C * (x + GELU_K * x * x * x))
    value = 0.5 * x * (1.0 + t)
    slope = 0.5 * (1.0 + t) + 0.5 * x * (1.0 - t * t) * GELU_C * (1.0 + 3.0 * GELU_K * x * x)
    return value, slope


def gelu_value(x):
    return 0.5 * x * (1.0 + jnp.tanh(GELU_C * (x + GELU_K * x * x * x)))


def sigmoid(x):
    return 0.5 * (1.0 + jnp.tanh(0.5 * x))


def one_less_exp(z):
    series = 1.0 - z * (1.0 / 7.0)
    for k in (6.0, 5.0, 4.0, 3.0, 2.0):
        series = 1.0 - z * (1.0 / k) * series
    return jnp.where(z < 0.35, z * series, 1.0 - jnp.exp(-z))


def softplus_neg(x):
    return jnp.maximum(-x, 0.0) + jnp.log1p(jnp.exp(-jnp.abs(x)))


def mm(a, b):
    return jnp.dot(a, b, preferred_element_type=F32)


def mm_nt(a, b):
    return lax.dot_general(a, b, (((1,), (1,)), ((), ())), preferred_element_type=F32)


def mm_tn(a, b):
    return lax.dot_general(a, b, (((0,), (0,)), ((), ())), preferred_element_type=F32)


def roll_rows(x, n):
    return pltpu.roll(x, n % x.shape[0], 0)


def conv_rows(linear, kernel, bias, masks):
    out = linear * kernel[0:1] + bias
    for k in range(1, 4):
        out = out + kernel[k : k + 1] * (roll_rows(linear, k) * masks[k - 1])
    return out


def decay_terms(rate_pre, decay):
    rate = sigmoid(rate_pre)
    keep = RATE_SCALE * rate * softplus_neg(decay)
    return rate, jnp.exp(-keep), jnp.sqrt(one_less_exp(2.0 * keep))


MESH_ID = pl.DeviceIdType.MESH
VMEM_LIMIT = 62 * 2**20
N_Z, N_X = 4, 2


def place():
    shard = lax.axis_index("shard")
    return lax.axis_index("group"), shard, shard // N_X, shard % N_X


def greet(peers):
    bar = pltpu.get_barrier_semaphore()
    count = 0
    for device, there in peers:
        if there is True:
            pl.semaphore_signal(bar, inc=1, device_id=device, device_id_type=MESH_ID)
            count = count + 1
        else:
            @pl.when(there)
            def _(device=device):
                pl.semaphore_signal(bar, inc=1, device_id=device, device_id_type=MESH_ID)
            count = count + there.astype(jnp.int32)
    pl.semaphore_wait(bar, count)


def line_peers():
    group, shard, z, x = place()
    return [
        ((group, shard + N_X), z < N_Z - 1),
        ((group, shard - N_X), z > 0),
        ((group, z * N_X + 1 - x), True),
    ]


class Gather:
    CHUNKS = 2

    @classmethod
    def scratch(cls):
        return [pltpu.SemaphoreType.DMA((3, N_Z, cls.CHUNKS)), pltpu.SemaphoreType.DMA((N_Z * N_X, cls.CHUNKS))]

    def __init__(self, buf, sems):
        self.buf, (self.send, self.recv) = buf, sems
        self.group, self.shard, self.z, self.x = place()
        self.rows = buf.shape[1] // self.CHUNKS

    def copy(self, origin, column, c, way):
        slot = origin * N_X + column
        z = (self.z + 1, self.z - 1, self.z)[way]
        x = 1 - self.x if way == 2 else self.x
        piece = self.buf.at[slot, pl.ds(c * self.rows, self.rows)]
        return pltpu.make_async_remote_copy(
            src_ref=piece, dst_ref=piece, send_sem=self.send.at[way, origin, c],
            recv_sem=self.recv.at[slot, c], device_id=(self.group, z * N_X + x), device_id_type=MESH_ID,
        )

    def start(self):
        for c in range(self.CHUNKS):
            self.forward(self.z, c, True, True)

    def forward(self, origin, c, up, down):
        if up:
            @pl.when(self.z < N_Z - 1)
            def _():
                self.copy(origin, self.x, c, 0).start()
        if down:
            @pl.when(self.z > 0)
            def _():
                self.copy(origin, self.x, c, 1).start()
        self.copy(origin, self.x, c, 2).start()

    def step(self, k):
        for c in range(self.CHUNKS):
            @pl.when(self.z >= k)
            def _(c=c):
                self.copy(self.z - k, self.x, c, 2).wait_recv()
                self.forward(self.z - k, c, True, False)

            @pl.when(self.z + k < N_Z)
            def _(c=c):
                self.copy(self.z + k, self.x, c, 2).wait_recv()
                self.forward(self.z + k, c, False, True)

    def wait_across(self, origin):
        for c in range(self.CHUNKS):
            self.copy(origin, 1 - self.x, c, 2).wait_recv()

    def finish(self):
        for c in range(self.CHUNKS):
            for origin in range(N_Z):
                @pl.when((self.z < N_Z - 1) & (origin <= self.z))
                def _():
                    self.copy(origin, self.x, c, 0).wait_send()

                @pl.when((self.z > 0) & (origin >= self.z))
                def _():
                    self.copy(origin, self.x, c, 1).wait_send()
                self.copy(origin, self.x, c, 2).wait_send()


class Scatter:
    CHUNKS = 2

    @classmethod
    def scratch(cls, rows, width):
        dma = pltpu.SemaphoreType.DMA
        return [
            pltpu.VMEM((N_Z, rows, width), BF16),
            pltpu.VMEM((N_Z + 1, rows, width), BF16),
            dma((2, N_Z, cls.CHUNKS)), dma((N_Z, cls.CHUNKS)), dma((N_Z + 1, cls.CHUNKS)),
        ]

    def __init__(self, away, own, scratch):
        self.away, self.own = away, own
        self.across, self.along, self.send, self.recv_x, self.recv_z = scratch
        self.group, self.shard, self.z, self.x = place()
        self.rows = self.across.shape[1] // self.CHUNKS

    @classmethod
    def of(cls, parts, scratch):
        _, _, _, x = place()
        return cls(lambda k: parts.at[k * N_X + 1 - x], lambda k: parts.at[k * N_X + x], scratch)

    def dest(self, i):
        low = jnp.minimum(self.z, N_Z - 1 - self.z)
        value = (N_Z - 1, N_Z - 2, jnp.where(low == 0, 1, 0), low)[i]
        return jnp.where(self.z >= N_Z // 2, N_Z - 1 - value, value)

    def span(self, c):
        return pl.ds(c * self.rows, self.rows)

    def copy_x(self, dest, c):
        return pltpu.make_async_remote_copy(
            src_ref=self.away(dest).at[self.span(c)], dst_ref=self.across.at[dest, self.span(c)],
            send_sem=self.send.at[0, dest, c], recv_sem=self.recv_x.at[dest, c],
            device_id=(self.group, self.z * N_X + 1 - self.x), device_id_type=MESH_ID,
        )

    def copy_z(self, dest, slot, c, step):
        return pltpu.make_async_remote_copy(
            src_ref=self.own(dest).at[self.span(c)], dst_ref=self.along.at[slot, self.span(c)],
            send_sem=self.send.at[1, dest, c], recv_sem=self.recv_z.at[slot, c],
            device_id=(self.group, (self.z + step) * N_X + self.x), device_id_type=MESH_ID,
        )

    def start(self, i):
        for c in range(self.CHUNKS):
            self.copy_x(self.dest(i), c).start()

    def arrived(self, slot, c):
        self.copy_z(0, slot, c, 0).wait_recv()
        return self.along[slot, self.span(c)].astype(F32)

    def half(self, dest, c):
        return self.own(dest)[self.span(c)].astype(F32) + self.across[dest, self.span(c)].astype(F32)

    def step(self, i):
        dest = self.dest(i)
        own = self.own(dest)
        for c in range(self.CHUNKS):
            self.copy_x(dest, c).wait_recv()
            inner = ((dest > self.z) & (self.z > 0)) | ((dest < self.z) & (self.z < N_Z - 1))

            @pl.when(inner)
            def _(c=c):
                own[self.span(c)] = (self.half(dest, c) + self.arrived(dest, c)).astype(BF16)

            @pl.when(jnp.logical_not(inner))
            def _(c=c):
                own[self.span(c)] = self.half(dest, c).astype(BF16)

            @pl.when(dest > self.z)
            def _(c=c):
                self.copy_z(dest, dest, c, 1).start()

            @pl.when(dest < self.z)
            def _(c=c):
                self.copy_z(dest, jnp.where(dest == self.z - 1, N_Z, dest), c, -1).start()

    def last(self, out):
        for c in range(self.CHUNKS):
            self.copy_x(self.z, c).wait_recv()
            out[self.span(c)] = self.half(self.z, c)

            @pl.when(self.z > 0)
            def _(c=c):
                out[self.span(c)] += self.arrived(self.z, c)

            @pl.when(self.z < N_Z - 1)
            def _(c=c):
                out[self.span(c)] += self.arrived(N_Z, c)

    def finish(self):
        for c in range(self.CHUNKS):
            for dest in range(N_Z):
                self.copy_x(dest, c).wait_send()

                @pl.when(dest != self.z)
                def _():
                    self.copy_z(dest, 0, c, 0).wait_send()


class Exchange:
    @classmethod
    def scratch(cls, blocks, count):
        dma = pltpu.SemaphoreType.DMA
        return [dma((count, blocks)), dma((count, blocks)), dma((3, count, blocks)), dma((3, count, blocks))]

    def __init__(self, sources, views, blocks, sems):
        self.sources, self.views, self.blocks = sources, views, blocks
        self.send_first, self.recv_first, self.send, self.recv = sems
        self.group, self.shard, _, _ = place()
        self.home = self.shard if blocks > 1 else 0
        self.core_mate, self.y_mate = mates()
        self.count = len(sources)

    def first(self, j, to, origin):
        return pltpu.make_async_remote_copy(
            src_ref=self.sources[j](to), dst_ref=self.views[j](origin, self.group),
            send_sem=self.send_first.at[j, to], recv_sem=self.recv_first.at[j, origin],
            device_id=(self.group, to), device_id_type=MESH_ID,
        )

    def own(self, j):
        return pltpu.make_async_copy(
            self.sources[j](self.home), self.views[j](self.home, self.group), self.recv_first.at[j, self.home]
        )

    def pass_on(self, j, origin, quarter, mate, way, source=None):
        piece = self.views[j](origin, quarter)
        return pltpu.make_async_remote_copy(
            src_ref=piece if source is None else source, dst_ref=piece, send_sem=self.send.at[way, j, origin], recv_sem=self.recv.at[way, j, origin],
            device_id=(mate, self.shard), device_id_type=MESH_ID,
        )

    def others(self, body):
        if self.blocks > 1:
            pl.loop(1, self.blocks)(lambda i: body((self.home + i) % self.blocks))

    def start(self):
        for j in range(self.count):
            self.own(j).start()

        def send(to):
            for j in range(self.count):
                self.first(j, to, self.home).start()

        self.others(send)

    def both(self, j, origin, source=None):
        self.pass_on(j, origin, self.group, self.y_mate, 1, source).start()
        self.pass_on(j, origin, self.group, self.core_mate, 0, source).start()

    def spread(self):
        for j in range(self.count):
            self.both(j, self.home, self.sources[j](self.home))

        def forward(origin):
            for j in range(self.count):
                self.first(j, origin, origin).wait_recv()
                self.both(j, origin)

        self.others(forward)

    def each(self, body):
        for j in range(self.count):
            body(j, self.home)

        def rest(origin):
            for j in range(self.count):
                body(j, origin)

        self.others(rest)

    def relay(self):
        def forward(j, origin):
            self.pass_on(j, origin, self.y_mate, self.core_mate, 1).wait_recv()
            self.pass_on(j, origin, self.y_mate, self.core_mate, 2).start()

        self.each(forward)

    def arrive(self):
        def wait(j, origin):
            self.pass_on(j, origin, self.group, self.core_mate, 0).wait_recv()
            self.pass_on(j, origin, self.group, self.core_mate, 2).wait_recv()

        for j in range(self.count):
            self.own(j).wait()
        self.each(wait)

    def finish(self):
        def sent(to):
            for j in range(self.count):
                self.first(j, to, self.home).wait_send()

        def passed(j, origin):
            for way in range(3):
                self.pass_on(j, origin, self.group, self.core_mate, way).wait_send()

        self.others(sent)
        self.each(passed)


def mates():
    group = lax.axis_index("group")
    return group + 1 - 2 * (group % 2), group + 2 - 4 * (group // 2)


def all_peers():
    group, shard, _, _ = place()
    core_mate, y_mate = mates()
    others = [((group, (shard + i) % (N_Z * N_X)), True) for i in range(1, N_Z * N_X)]
    return others + [((core_mate, shard), True), ((y_mate, shard), True)]


def mixer_forward(linear, gate, pos, vec, gates):
    masks = [(pos >= k).astype(F32) for k in (1, 2, 3)]
    conv = conv_rows(linear, vec[0:4], vec[4:5], masks)
    width = linear.shape[1]
    both = mm_nt(conv.astype(BF16), gates)
    rate_pre = both[:, :width] + vec[5:6]
    input_pre = both[:, width:] + vec[6:7]
    _, a, weight_in = decay_terms(rate_pre, vec[7:8])
    mult = a * masks[0]
    total = weight_in * sigmoid(input_pre) * conv
    step = 1
    while step < CAP:
        total = total + mult * roll_rows(total, step)
        if 2 * step < CAP:
            mult = mult * roll_rows(mult, step)
        step *= 2
    return rate_pre, input_pre, total, (gelu_value(gate) * total).astype(BF16)


def pair_positions(gains, origin, rows):
    places = []
    for column in range(N_X):
        lengths = gains[origin * N_X + column, 2:3]
        places.append(positions_in_run([lengths[:, i : i + 1] for i in range(3)], rows)[0])
    return jnp.concatenate(places, axis=0)


def rms_scale(values):
    return lax.rsqrt(jnp.mean(values * values, axis=1, keepdims=True) + EPSILON)


def forward_kernel(
    lengths_ref, tokens_ref, cotangent_ref, gain1_ref, gain2_ref, kernel_ref, bias_ref, rate_bias_ref, input_bias_ref, decay_ref, rate_weight_ref,
    input_weight_ref, out_proj_ref, gate_in_ref, linear_in_ref, mlp_gate_ref, mlp_up_ref,
    gather_out, weights_out, mlp_out, gains_out, saved_out, merged_out, middle_ref, normed_two_ref, vec_ref, gates_ref, g_low_out,
    gains_ref, g_low, buf, weights, quarter, raw, masked, saved, merged, parts,
    gather_a, gather_b, ex_a, ex_b, ex_c, ex_d, mx_a, mx_b, mx_c, mx_d, *rest,
):
    scatter_scratch, rest = rest[:-8], rest[-8:]
    gain_send, gain_recv, raw_sem, out_sem, pair_sem, g_sem, g_send, g_recv = rest
    group, shard, z, x = place()
    shards = N_Z * N_X
    rows, width = tokens_ref.shape
    quarter_rows = raw.shape[1]
    chans = linear_in_ref.shape[1] // shards
    padded = vec_ref.shape[1]
    fetch = [
        pltpu.make_async_copy(ref.at[pl.ds(group * quarter_rows, quarter_rows)], raw.at[i], raw_sem.at[i])
        for i, ref in enumerate((gate_in_ref, linear_in_ref))
    ]
    for copy in fetch:
        copy.start()
    gains_ref[...] = jnp.zeros_like(gains_ref)
    gains_ref[0:1] = gain1_ref[...].astype(F32).reshape(1, -1)
    gains_ref[1:2] = gain2_ref[...].astype(F32).reshape(1, -1)
    lane = lax.broadcasted_iota(jnp.int32, (1, gains_ref.shape[1]), 1)
    for i in range(3):
        gains_ref[2:3] += jnp.where(lane == i, lengths_ref[0, i].astype(F32), 0.0)
    greet(all_peers())

    def gain_copy(to, origin):
        return pltpu.make_async_remote_copy(
            src_ref=gains_ref, dst_ref=gains_out.at[origin], send_sem=gain_send.at[to], recv_sem=gain_recv.at[origin],
            device_id=(group, to), device_id_type=MESH_ID,
        )

    for i in range(1, shards):
        gain_copy((shard + i) % shards, shard).start()
    gains_out[shard] = gains_ref[...]
    for copy in fetch:
        copy.wait()
    for to in range(shards):
        part = slice(to * chans, (to + 1) * chans)
        quarter[to] = jnp.concatenate([raw[0, :, part].astype(F32), raw[1, :, part].astype(F32)], axis=1).astype(BF16)
    exchange = Exchange(
        [lambda to: quarter.at[to]], [lambda origin, q: weights.at[origin, q]], shards, (ex_a, ex_b, ex_c, ex_d)
    )
    exchange.start()
    hidden = mlp_up_ref.shape[1] // shards

    def part_of(ref):
        return lambda to: ref.at[pl.ds(group * quarter_rows, quarter_rows), pl.ds(to * hidden, hidden)]

    mlp_exchange = Exchange(
        [part_of(mlp_gate_ref), part_of(mlp_up_ref)],
        [lambda origin, q: mlp_out.at[origin, q, :, 0:hidden], lambda origin, q: mlp_out.at[origin, q, :, hidden : 2 * hidden]],
        shards, (mx_a, mx_b, mx_c, mx_d),
    )
    _, live = positions_in_run([lengths_ref[0, i].astype(F32) for i in range(3)], rows)
    masked[...] = tokens_ref[...].astype(F32) * live
    g_low[...] = (cotangent_ref[...].astype(F32) * live).astype(BF16)
    g_copy = pltpu.make_async_copy(g_low, g_low_out.at[shard], g_sem)
    g_copy.start()
    g_gather = Gather(g_low_out, (g_send, g_recv))
    for i in range(1, shards):
        gain_copy(shard, (shard + i) % shards).wait_recv()
    gains = jnp.concatenate([gains_out[i] for i in range(shards)], axis=1)
    gather = Gather(buf, (gather_a, gather_b))
    buf[shard] = (masked[...] * rms_scale(masked[...]) * gains[0:1]).astype(BF16)
    gather.start()
    vec_ref[...] = jnp.zeros_like(vec_ref)
    vec_ref[0:4, :chans] = kernel_ref[...].astype(F32)
    for i, ref in enumerate((bias_ref, rate_bias_ref, input_bias_ref, decay_ref)):
        vec_ref[4 + i : 5 + i, :chans] = ref[...].astype(F32).reshape(1, -1)
    gates_ref[...] = jnp.zeros_like(gates_ref)
    size = rate_weight_ref.shape[0]
    for i, ref in enumerate((rate_weight_ref, input_weight_ref)):
        for h in range(chans // size):
            part = slice(h * size, (h + 1) * size)
            gates_ref[i * padded + h * size : i * padded + (h + 1) * size, part] = ref[:, part]
    gather.step(1)
    exchange.spread()
    gather.step(2)
    exchange.relay()
    mlp_exchange.start()
    exchange.arrive()
    scatter = Scatter.of(parts, scatter_scratch)

    def pair_copies(origin):
        return [
            pltpu.make_async_copy(saved.at[origin], saved_out.at[origin], pair_sem.at[0, origin]),
            pltpu.make_async_copy(merged.at[origin], merged_out.at[origin], pair_sem.at[1, origin]),
        ]

    @pl.loop(0, N_Z)
    def _(i):
        @pl.when(i == 1)
        def _():
            gather.step(3)
            g_copy.wait()
            g_gather.start()

        origin = nearest(z, i)
        gather.wait_across(origin)
        pair = pl.ds(origin * N_X, N_X)
        pre = mm(buf[pair].reshape(N_X * rows, width), weights[...].reshape(width, 2 * chans))
        blank = jnp.zeros((N_X * rows, padded - chans), F32)
        gate = jnp.concatenate([pre[:, :chans], blank], axis=1)
        linear = jnp.concatenate([pre[:, chans:], blank], axis=1)
        where = pair_positions(gains_out, origin, rows)
        rate_pre, input_pre, state, merge = mixer_forward(linear, gate, where, vec_ref[...], gates_ref[...])
        for j, value in enumerate((gate, linear, rate_pre, input_pre, state)):
            saved[origin, j] = value
        merged[origin] = merge
        for copy in pair_copies(origin):
            copy.start()
        parts[pair] = mm(merge[:, :chans], out_proj_ref[...]).astype(BF16).reshape(N_X, rows, width)

    outs = [
        pltpu.make_async_copy(buf, gather_out, out_sem.at[0]),
        pltpu.make_async_copy(weights, weights_out, out_sem.at[1]),
    ]
    for copy in outs:
        copy.start()
    for i in range(N_Z):
        scatter.start(i)
    mlp_exchange.spread()
    scatter.step(0)
    g_gather.step(1)
    mlp_exchange.relay()
    scatter.step(1)
    g_gather.step(2)
    scatter.step(2)
    g_gather.step(3)
    scatter.last(middle_ref)
    middle_ref[...] += masked[...]
    normed_two_ref[...] = (middle_ref[...] * rms_scale(middle_ref[...]) * gains[1:2]).astype(BF16)
    for i in range(1, shards):
        gain_copy((shard + i) % shards, shard).wait_send()
    gather.finish()
    exchange.finish()
    for origin in range(N_Z):
        g_gather.wait_across(origin)
    g_gather.finish()
    mlp_exchange.arrive()
    mlp_exchange.finish()
    scatter.finish()
    for copy in outs:
        copy.wait()

    @pl.loop(0, N_Z)
    def _(origin):
        for copy in pair_copies(origin):
            copy.wait()


def nearest(z, i):
    low = jnp.minimum(z, N_Z - 1 - z)
    value = jnp.where(low == 0, i, jnp.where(i == 0, 1, jnp.where(i == 1, 0, i)))
    return jnp.where(z >= N_Z // 2, N_Z - 1 - value, value)


def any_spec():
    return pl.BlockSpec(memory_space=pl.ANY)


def vmem_spec():
    return pl.BlockSpec(memory_space=pltpu.VMEM)


def forward_call(lengths, tokens, cotangent, small, out_proj, gate_in, linear_in, mlp_gate, mlp_up):
    rows, width = tokens.shape
    shards, groups = lax.axis_size("shard"), lax.axis_size("group")
    chans = out_proj.shape[0]
    padded = -(-chans // 128) * 128
    gains = (8, width // shards)
    quarter_rows = gate_in.shape[0] // groups
    hidden = mlp_up.shape[1] // shards
    dma = pltpu.SemaphoreType.DMA
    shape = jax.ShapeDtypeStruct
    out_shape = [
        shape((shards, rows, width), BF16),
        shape((shards, groups, quarter_rows, 2 * chans), BF16),
        shape((shards, groups, quarter_rows, 2 * hidden), BF16),
        shape((shards,) + gains, F32),
        shape((N_Z, 5, N_X * rows, padded), F32),
        shape((N_Z, N_X * rows, padded), BF16),
        shape((rows, width), F32),
        shape((rows, width), BF16),
        shape((8, padded), F32),
        shape((2 * padded, padded), BF16),
        shape((shards, rows, width), BF16),
    ]
    return pl.pallas_call(
        forward_kernel,
        out_shape=out_shape,
        in_specs=[pl.BlockSpec(memory_space=pltpu.SMEM)] + [vmem_spec()] * 12 + [any_spec()] * 4,
        out_specs=[any_spec()] * 3 + [vmem_spec()] + [any_spec()] * 2 + [vmem_spec()] * 4 + [any_spec()],
        scratch_shapes=[
            pltpu.VMEM(gains, F32),
            pltpu.VMEM((rows, width), BF16),
            pltpu.VMEM((shards, rows, width), BF16),
            pltpu.VMEM((shards, groups, quarter_rows, 2 * chans), BF16),
            pltpu.VMEM((shards, quarter_rows, 2 * chans), BF16),
            pltpu.VMEM((2, quarter_rows, gate_in.shape[1]), BF16),
            pltpu.VMEM((rows, width), F32),
            pltpu.VMEM((N_Z, 5, N_X * rows, padded), F32),
            pltpu.VMEM((N_Z, N_X * rows, padded), BF16),
            pltpu.VMEM((shards, rows, width), BF16),
        ]
        + Gather.scratch()
        + Exchange.scratch(shards, 1)
        + Exchange.scratch(shards, 2)
        + Scatter.scratch(rows, width)
        + [dma((shards,)), dma((shards,)), dma((2,)), dma((2,)), dma((2, N_Z)), dma]
        + Gather.scratch(),
        compiler_params=pltpu.CompilerParams(collective_id=1, has_side_effects=True, vmem_limit_bytes=VMEM_LIMIT),
        name="mixer_forward",
    )(lengths, tokens, cotangent, *small, out_proj, gate_in, linear_in, mlp_gate, mlp_up)


class CoreSum:
    @classmethod
    def scratch(cls, count):
        return [pltpu.SemaphoreType.DMA((count, 2))] * 2

    def __init__(self, terms, arrived, sems):
        self.terms, self.arrived = terms, arrived
        self.send, self.recv = sems
        group, self.shard, _, _ = place()
        self.core, self.y = group % 2, group // 2
        self.core_mate, _ = mates()

    def copy(self, j, half):
        return pltpu.make_async_remote_copy(
            src_ref=self.terms[j](2 * half + 1 - self.core), dst_ref=self.arrived[j].at[half],
            send_sem=self.send.at[j, half], recv_sem=self.recv.at[j, half],
            device_id=(self.core_mate, self.shard), device_id_type=MESH_ID,
        )

    def mine(self, j, half):
        return self.terms[j](2 * half + self.core)

    def start(self, j):
        for half in (1 - self.y, self.y):
            self.copy(j, half).start()

    def add(self, j, half):
        self.copy(j, half).wait_recv()
        own = self.mine(j, half)

        @pl.loop(0, self.arrived[j].shape[1])
        def _(i):
            own[i] = (own[i].astype(F32) + self.arrived[j][half, i].astype(F32)).astype(BF16)

    def finish(self):
        for half in (0, 1):
            for j in range(len(self.terms)):
                self.copy(j, half).wait_send()


class LineSum:
    @classmethod
    def scratch(cls, count):
        return [pltpu.SemaphoreType.DMA((count,))] * 2

    def __init__(self, core_sum, arrived, sems):
        self.core_sum, self.arrived = core_sum, arrived
        self.send, self.recv = sems
        self.shard, self.y = core_sum.shard, core_sum.y
        _, self.y_mate = mates()

    def copy(self, j):
        return pltpu.make_async_remote_copy(
            src_ref=self.core_sum.mine(j, 1 - self.y), dst_ref=self.arrived[j],
            send_sem=self.send.at[j], recv_sem=self.recv.at[j],
            device_id=(self.y_mate, self.shard), device_id_type=MESH_ID,
        )

    def start(self, j):
        self.core_sum.add(j, 1 - self.y)
        self.copy(j).start()
        self.core_sum.add(j, self.y)

    def add(self, j):
        self.copy(j).wait_recv()
        own = self.core_sum.mine(j, self.y)

        @pl.loop(0, self.arrived[j].shape[0])
        def _(i):
            own[i] = (own[i].astype(F32) + self.arrived[j][i].astype(F32)).astype(BF16)

    def finish(self):
        self.core_sum.finish()
        for j in range(len(self.arrived)):
            self.copy(j).wait_send()


def split_gains(ref, row, values):
    size = ref.shape[2]
    for i in range(ref.shape[0]):
        ref[i, row : row + 1] = values[:, i * size : (i + 1) * size]


def norm_backward(values, gain, grad):
    scale = rms_scale(values)
    e = grad * gain
    back = scale * e - values * (scale * scale * scale) * jnp.mean(values * e, axis=1, keepdims=True)
    return back, jnp.sum(grad * values * scale, axis=0, keepdims=True)


def mlp_kernel(
    lengths_ref, normed_ref, middle_ref, gains_ref, g_low_ref, weights_ref, down_ref,
    quarter_gu_out, quarter_down_out, mixed_ref, g_middle_ref, gain_ref,
    normed, g_low, weights, down, hidden, grads, parts, mixed_parts, term_down,
    core_down, core_first, core_second, line_down, line_first, line_second, *sems,
):
    sems = list(sems)

    def take(n):
        taken = tuple(sems[:n])
        del sems[:n]
        return taken

    group, shard, z, x = place()
    core_mate, y_mate = mates()
    rows, width = normed_ref.shape
    size = hidden.shape[2]
    load_sem, out_sem = take(2)
    loads = [
        pltpu.make_async_copy(source, target, load_sem.at[i])
        for i, (source, target) in enumerate(((weights_ref, weights), (down_ref, down), (g_low_ref, g_low)))
    ]
    for copy in loads:
        copy.start()
    gather = Gather(normed, take(2))
    scatter = Scatter.of(parts, take(5))
    mixed_scatter = Scatter.of(mixed_parts, take(5))
    middle_tile = N_Z * N_X // 2
    core_sum = CoreSum(
        [lambda q: term_down.at[q], lambda q: weights.at[0:middle_tile, q], lambda q: weights.at[middle_tile : 2 * middle_tile, q]],
        [core_down, core_first, core_second], take(2),
    )
    line_sum = LineSum(core_sum, [line_down, line_first, line_second], take(2))
    greet(line_peers() + [((core_mate, shard), True), ((y_mate, shard), True)])
    normed[shard] = normed_ref[...]
    gather.start()
    gather.step(1)
    gather.step(2)
    for copy in loads:
        copy.wait()

    @pl.loop(0, N_Z)
    def _(i):
        @pl.when(i == 1)
        def _():
            gather.step(3)

        @pl.when(i == N_Z - 1)
        def _():
            for k in range(1, N_Z):
                mixed_scatter.start(k)

        origin = nearest(z, i)
        gather.wait_across(origin)
        pair = pl.ds(origin * N_X, N_X)
        left = normed[pair].reshape(N_X * rows, width)
        g_left = g_low[pair].reshape(N_X * rows, width)
        for first in range(0, size, size // 2):
            part, up_part = slice(first, first + size // 2), slice(size + first, size + first + size // 2)
            act, slope = gelu_parts(mm(left, weights[:, :, :, part].reshape(width, size // 2)))
            up = mm(left, weights[:, :, :, up_part].reshape(width, size // 2))
            g_hidden = mm_nt(g_left, down[part])
            hidden[origin, :, part] = (act * up).astype(BF16)
            grads[origin, :, part] = (g_hidden * up * slope).astype(BF16)
            grads[origin, :, up_part] = (g_hidden * act).astype(BF16)
        back = mm_nt(grads[origin], weights[...].reshape(width, 2 * size))
        parts[pair] = back.astype(BF16).reshape(N_X, rows, width)
        mixed_parts[pair] = mm(hidden[origin], down[...]).astype(BF16).reshape(N_X, rows, width)

    mixed_scatter.start(0)
    for i in range(N_Z):
        scatter.start(i)
    tile = normed.shape[2] // (N_Z * N_X)
    total = N_Z * N_X * rows

    @pl.loop(0, size // tile)
    def _(i):
        left = hidden[:, :, pl.ds(i * tile, tile)].reshape(total, tile)
        term = mm_tn(left, g_low[...].reshape(total, width)).astype(BF16)
        step = term_down.shape[2]
        for j in range(tile // step):
            chunk = i * (tile // step) + j
            term_down[chunk // term_down.shape[1], chunk % term_down.shape[1]] = term[j * step : (j + 1) * step]

    core_sum.start(0)

    def gu_terms(first, last):
        @pl.loop(first, last)
        def _(i):
            left = normed[:, :, pl.ds(i * tile, tile)].reshape(total, tile)
            term = mm_tn(left, grads[...].reshape(total, 2 * size)).astype(BF16)
            weights[i] = term.reshape(weights.shape[1:])

    gu_terms(0, middle_tile)
    core_sum.start(1)
    line_sum.start(0)
    gu_terms(middle_tile, 2 * middle_tile)
    core_sum.start(2)
    line_sum.start(1)
    mixed_scatter.step(0)
    line_sum.start(2)
    mixed_scatter.step(1)
    mixed_scatter.step(2)
    scatter.step(0)
    mixed_scatter.last(g_middle_ref)
    _, live = positions_in_run([lengths_ref[0, i].astype(F32) for i in range(3)], rows)
    mixed_ref[...] = ((middle_ref[...] + g_middle_ref[...]) * live).astype(BF16)
    scatter.step(1)
    scatter.step(2)
    outs = []
    for j, out in enumerate((quarter_down_out, quarter_gu_out.at[0:middle_tile], quarter_gu_out.at[middle_tile : 2 * middle_tile])):
        line_sum.add(j)
        outs.append(pltpu.make_async_copy(core_sum.mine(j, group // 2), out, out_sem.at[j]))
        outs[-1].start()
    scatter.last(g_middle_ref)
    gain = jnp.concatenate([gains_ref[i] for i in range(N_Z * N_X)], axis=1)[1:2]
    back, gain_term = norm_backward(middle_ref[...], gain, g_middle_ref[...])
    g_middle_ref[...] = g_low[shard].astype(F32) + back
    gain_ref[...] = jnp.zeros_like(gain_ref)
    split_gains(gain_ref, 1, gain_term)
    gather.finish()
    line_sum.finish()
    mixed_scatter.finish()
    scatter.finish()
    for copy in outs:
        copy.wait()


def mlp_call(lengths, normed, middle, gains, g_low, weights, down):
    rows, width = normed.shape
    shards, groups, quarter_rows, both = weights.shape
    size = down.shape[0]
    dma = pltpu.SemaphoreType.DMA
    shape = jax.ShapeDtypeStruct
    down_term = (size // groups // 64, 64, width)
    gu_term = (shards, quarter_rows, both)
    terms = [down_term] + [(shards // 2, quarter_rows, both)] * 2
    pairs = (N_Z, N_X * rows)
    scratch = [
        (shards, rows, width), (shards, rows, width), weights.shape, down.shape, pairs + (size,), pairs + (both,),
        (shards, rows, width), (shards, rows, width), (groups,) + down_term,
        *[(2,) + term for term in terms], *terms,
    ]
    return pl.pallas_call(
        mlp_kernel,
        out_shape=[
            shape(gu_term, BF16),
            shape(down_term, BF16),
            shape((rows, width), BF16),
            shape((rows, width), F32),
            shape(gains.shape, F32),
        ],
        in_specs=[pl.BlockSpec(memory_space=pltpu.SMEM)] + [vmem_spec()] * 3 + [any_spec()] * 3,
        out_specs=[any_spec()] * 2 + [vmem_spec()] * 3,
        scratch_shapes=[pltpu.VMEM(dims, BF16) for dims in scratch]
        + [dma((3,)), dma((3,))]
        + Gather.scratch()
        + Scatter.scratch(rows, width)
        + Scatter.scratch(rows, width)
        + CoreSum.scratch(3)
        + LineSum.scratch(3),
        compiler_params=pltpu.CompilerParams(collective_id=2, has_side_effects=True, vmem_limit_bytes=VMEM_LIMIT),
        name="mlp",
    )(lengths, normed, middle, gains, g_low, weights, down)


def mixer_backward(g_merged, saved, pos, vec, gates):
    gate, linear, rate_pre, input_pre, state = saved
    width = linear.shape[1]
    masks = [(pos >= k).astype(F32) for k in (1, 2, 3)]
    later = [roll_rows(jnp.broadcast_to(masks[k - 1], linear.shape), -k) for k in (1, 2, 3)]
    conv = conv_rows(linear, vec[0:4], vec[4:5], masks)
    input_gate = sigmoid(input_pre)
    decay = vec[7:8]
    rate, a, weight_in = decay_terms(rate_pre, decay)
    act, slope = gelu_parts(gate)
    g_gate = g_merged * state * slope
    lam = g_merged * act
    mult = roll_rows(a, -1) * later[0]
    step = 1
    while step < CAP:
        lam = lam + mult * roll_rows(lam, -step)
        if 2 * step < CAP:
            mult = mult * roll_rows(mult, -step)
        step *= 2
    g_a = lam * (roll_rows(state, 1) * masks[0])
    g_keep = g_a * a - lam * (input_gate * conv) * (a * a) / weight_in
    g_rate = (g_keep * (-RATE_SCALE * softplus_neg(decay)) * (rate * (1.0 - rate))).astype(BF16)
    g_decay = g_keep * (RATE_SCALE * rate) * sigmoid(-decay)
    flow = lam * weight_in
    g_inp = (flow * conv * (input_gate * (1.0 - input_gate))).astype(BF16)
    g_conv = flow * input_gate + mm(jnp.concatenate([g_rate, g_inp], axis=1), gates)
    g_linear = g_conv * vec[0:1]
    sums = [jnp.sum(g_conv * linear, axis=0, keepdims=True)]
    for k in (1, 2, 3):
        g_linear = g_linear + vec[k : k + 1] * (roll_rows(g_conv, -k) * later[k - 1])
        sums.append(jnp.sum(g_conv * (roll_rows(linear, k) * masks[k - 1]), axis=0, keepdims=True))
    for value in (g_conv, g_rate.astype(F32), g_inp.astype(F32), g_decay):
        sums.append(jnp.sum(value, axis=0, keepdims=True))
    return g_gate, g_linear, jnp.concatenate(sums, axis=0), conv.astype(BF16), g_rate, g_inp


def backward_kernel(
    lengths_ref, tokens_ref, g_middle_ref, gains_ref, gain_in_ref, vec_ref, gates_ref, out_proj_ref,
    quarter_gu_ref, quarter_down_ref, weights_ref, saved_ref, merged_ref, gathered_ref,
    grad_gate_out, grad_up_out, grad_down_out, gl_out, out_out, bd_out, grad_tokens_ref, small_out_ref,
    g_mix, normed, weights, saved, merged, grads, parts, term_gl, term_out, term_bd, total_bd, total_small, result,
    core_gl, core_out, core_bd, line_gl, line_out, line_bd,
    gain_terms, gains_got, packed, packs, *sems,
):
    sems = list(sems)

    def take(n):
        taken = tuple(sems[:n])
        del sems[:n]
        return taken

    group, shard, z, x = place()
    core_mate, y_mate = mates()
    shards = N_Z * N_X
    rows, width = tokens_ref.shape
    padded = vec_ref.shape[1]
    total = shards * rows
    chans = out_proj_ref.shape[0]
    half = quarter_gu_ref.shape[2] // 2
    quarter_rows = quarter_gu_ref.shape[1]
    load_sem, saved_sem, gain_send, gain_recv, pack_send, pack_recv = take(6)
    gather = Gather(g_mix, take(2))
    scatter = Scatter.of(parts, take(5))
    core_sum = CoreSum(
        [lambda q: term_gl.at[q], lambda q: term_out.at[q], lambda q: term_bd.at[q]], [core_gl, core_out, core_bd], take(2)
    )
    line_sum = LineSum(core_sum, [line_gl, line_out, line_bd], take(2))

    def columns(ref):
        return lambda origin, quarter: ref.at[pl.ds(quarter * quarter_rows, quarter_rows), pl.ds(origin * half, half)]

    gate_exchange = Exchange([lambda to: quarter_gu_ref.at[to, :, 0:half]], [columns(grad_gate_out)], shards, take(4))
    up_exchange = Exchange([lambda to: quarter_gu_ref.at[to, :, half : 2 * half]], [columns(grad_up_out)], shards, take(4))
    down_exchange = Exchange([lambda to: quarter_down_ref], [lambda origin, quarter: grad_down_out.at[quarter]], 1, take(4))
    gl_exchange = Exchange(
        [lambda to: term_gl.at[group, to]], [lambda origin, quarter: gl_out.at[origin, quarter]], shards, take(4)
    )
    out_exchange = Exchange([lambda to: term_out.at[group]], [lambda origin, quarter: out_out.at[quarter]], 1, take(4))
    bd_exchange = Exchange([lambda to: term_bd.at[group]], [lambda origin, quarter: bd_out.at[quarter]], 1, take(4))

    def gain_copy(to, origin):
        return pltpu.make_async_remote_copy(
            src_ref=gain_terms.at[to], dst_ref=gains_got.at[origin], send_sem=gain_send.at[to], recv_sem=gain_recv.at[origin],
            device_id=(group, to), device_id_type=MESH_ID,
        )

    def pack_copy(i):
        return pltpu.make_async_remote_copy(
            src_ref=packed, dst_ref=packs.at[i], send_sem=pack_send.at[i], recv_sem=pack_recv.at[i],
            device_id=((core_mate, y_mate, 3 - group)[i], shard), device_id_type=MESH_ID,
        )

    def saved_copy(i):
        return pltpu.make_async_copy(saved_ref.at[nearest(z, i)], saved.at[i % 2], saved_sem.at[i % 2])

    loads = [
        pltpu.make_async_copy(source, target, load_sem.at[i])
        for i, (source, target) in enumerate((
            (weights_ref, weights), (gathered_ref, normed), (merged_ref, merged),
        ))
    ]
    for copy in loads:
        copy.start()
    saved_copy(0).start()
    greet(all_peers() + [((3 - group, shard), True)])
    g_mix[shard] = g_middle_ref[...].astype(BF16)
    gather.start()
    gate_exchange.start()
    down_exchange.start()
    down_exchange.spread()
    total_small[...] = jnp.zeros_like(total_small)
    total_bd[...] = jnp.zeros_like(total_bd)
    gather.step(1)
    gather.step(2)
    for copy in loads:
        copy.wait()

    @pl.loop(0, N_Z)
    def _(i):
        @pl.when(i == 1)
        def _():
            gather.step(3)
            up_exchange.start()

        @pl.when(i == 2)
        def _():
            gate_exchange.spread()

        origin = nearest(z, i)
        gather.wait_across(origin)
        saved_copy(i).wait()

        @pl.when(i < N_Z - 1)
        def _():
            saved_copy(i + 1).start()

        pair = pl.ds(origin * N_X, N_X)
        g_merged = mm_nt(g_mix[pair].reshape(N_X * rows, width), out_proj_ref[...])
        g_merged = jnp.concatenate([g_merged, jnp.zeros((N_X * rows, padded - chans), F32)], axis=1)
        where = pair_positions(gains_ref, origin, rows)
        g_gate, g_linear, sums, low, g_rate, g_inp = mixer_backward(
            g_merged, [saved[i % 2, j] for j in range(5)], where, vec_ref[...], gates_ref[...]
        )
        grads[origin] = jnp.concatenate([g_gate[:, :chans], g_linear[:, :chans]], axis=1).astype(BF16)
        total_small[...] += sums
        total_bd[0] += mm_tn(g_rate, low)
        total_bd[1] += mm_tn(g_inp, low)
        back = mm_nt(grads[origin], weights[...].reshape(width, 2 * chans))
        parts[pair] = back.astype(BF16).reshape(N_X, rows, width)

    for i in range(N_Z):
        scatter.start(i)
    tile = width // shards

    @pl.loop(0, shards)
    def _(i):
        left = normed[:, :, pl.ds(i * tile, tile)].reshape(total, tile)
        term = mm_tn(left, grads[...].reshape(total, 2 * chans)).astype(BF16)
        term_gl[:, i] = term.reshape(term_gl.shape[0], term_gl.shape[2], 2 * chans)

    core_sum.start(0)
    up_exchange.spread()
    scatter.step(0)
    term = mm_tn(merged[...].reshape(total, padded), g_mix[...].reshape(total, width))
    term_out[...] = term[:chans].astype(BF16).reshape(term_out.shape)
    size = term_bd.shape[0] * term_bd.shape[1] * term_bd.shape[2] // 2
    both = []
    for i in range(2):
        heads = [slice(h * size, (h + 1) * size) for h in range(chans // size)]
        both.append(jnp.concatenate([total_bd[i, part, part] for part in heads], axis=1))
    term_bd[...] = jnp.concatenate(both, axis=0).astype(BF16).reshape(term_bd.shape)
    core_sum.start(1)
    core_sum.start(2)
    for j in range(3):
        line_sum.start(j)
    scatter.step(1)
    scatter.step(2)
    scatter.last(result)
    _, live = positions_in_run([lengths_ref[0, i].astype(F32) for i in range(3)], rows)
    masked = tokens_ref[...].astype(F32) * live
    gain = jnp.concatenate([gains_ref[i] for i in range(shards)], axis=1)[0:1]
    back, gain_term = norm_backward(masked, gain, result[...])
    grad_tokens_ref[...] = ((g_middle_ref[...] + back) * live).astype(BF16)
    gain_terms[...] = gain_in_ref[...]
    split_gains(gain_terms, 0, gain_term)
    for i in range(1, shards):
        gain_copy((shard + i) % shards, shard).start()
    line_sum.add(0)
    gl_exchange.start()
    for j, one in ((1, out_exchange), (2, bd_exchange)):
        line_sum.add(j)
        one.start()
        one.spread()
    gl_exchange.spread()
    down_exchange.relay()
    gate_exchange.relay()
    up_exchange.relay()
    gain_sum = gain_terms[shard]
    for i in range(1, shards):
        origin = (shard + i) % shards
        gain_copy(origin, origin).wait_recv()
        gain_sum = gain_sum + gains_got[origin]
    packed[0:8] = total_small[...]
    packed[8:16] = jnp.concatenate([gain_sum, jnp.zeros((8, padded - gain_sum.shape[1]), F32)], axis=1)
    for i in range(3):
        pack_copy(i).start()
    packs_sum = packed[...]
    for i in range(3):
        pack_copy(i).wait_recv()
        packs_sum = packs_sum + packs[i]
    small_out_ref[...] = packs_sum
    for one in (out_exchange, bd_exchange, gl_exchange):
        one.relay()
    for i in range(1, shards):
        gain_copy((shard + i) % shards, shard).wait_send()
    for i in range(3):
        pack_copy(i).wait_send()
    for one in (gather, scatter, line_sum):
        one.finish()
    for one in (down_exchange, gate_exchange, up_exchange, out_exchange, bd_exchange, gl_exchange):
        one.arrive()
        one.finish()


def backward_call(
    head, lengths, tokens, g_middle, gains, gain_terms, vec, gates, out_proj, quarter_gu, quarter_down, weights, saved, merged,
    gathered,
):
    rows, width = tokens.shape
    shards, groups = N_Z * N_X, weights.shape[1]
    quarter_rows, both = quarter_gu.shape[1:]
    padded = vec.shape[1]
    chans = out_proj.shape[0]
    dma = pltpu.SemaphoreType.DMA
    shape = jax.ShapeDtypeStruct
    terms = [
        (groups, shards, quarter_rows, 2 * chans),
        (groups, chans // groups // 16, 16, width),
        (groups, 2 * head // groups // 16, 16, chans),
    ]
    packed = (16, padded)
    scratch = [
        ((shards, rows, width), BF16), (gathered.shape, BF16), (weights.shape, BF16), ((2,) + saved.shape[1:], F32),
        (merged.shape, BF16), ((N_Z, N_X * rows, 2 * chans), BF16), ((shards, rows, width), BF16),
        *[(term, BF16) for term in terms], ((2, padded, padded), F32), (vec.shape, F32), ((rows, width), F32),
        *[((2,) + term[1:], BF16) for term in terms], *[(term[1:], BF16) for term in terms],
        (gains.shape, F32), (gains.shape, F32), (packed, F32), ((3,) + packed, F32),
    ]
    return pl.pallas_call(
        backward_kernel,
        out_shape=[
            shape((groups * quarter_rows, shards * both // 2), BF16),
            shape((groups * quarter_rows, shards * both // 2), BF16),
            shape((groups,) + quarter_down.shape, BF16),
            shape((shards, groups) + terms[0][2:], BF16),
            shape(terms[1], BF16),
            shape(terms[2], BF16),
            shape((rows, width), BF16),
            shape(packed, F32),
        ],
        in_specs=[pl.BlockSpec(memory_space=pltpu.SMEM)] + [vmem_spec()] * 7 + [any_spec()] * 6,
        out_specs=[any_spec()] * 6 + [vmem_spec()] * 2,
        scratch_shapes=[pltpu.VMEM(dims, kind) for dims, kind in scratch]
        + [dma((3,)), dma((2,)), dma((shards,)), dma((shards,)), dma((3,)), dma((3,))]
        + Gather.scratch()
        + Scatter.scratch(rows, width)
        + CoreSum.scratch(3)
        + LineSum.scratch(3)
        + Exchange.scratch(shards, 1)
        + Exchange.scratch(shards, 1)
        + Exchange.scratch(1, 1)
        + Exchange.scratch(shards, 1)
        + Exchange.scratch(1, 1) * 2,
        compiler_params=pltpu.CompilerParams(collective_id=3, has_side_effects=True, vmem_limit_bytes=VMEM_LIMIT),
        name="mixer_backward",
    )(
        lengths, tokens, g_middle, gains, gain_terms, vec, gates, out_proj, quarter_gu, quarter_down, weights, saved, merged,
        gathered,
    )


def widen_kernel(
    mixed_ref, tokens_ref, small_ref, gate_ref, up_ref, down_ref, gl_ref, out_ref, bd_ref,
    mixed_out, tokens_out, gain1_out, gate_in_out, linear_in_out, kernel_out, bias_out, rate_out, rate_bias_out, input_out,
    input_bias_out, decay_out, out_out, gain2_out, gate_out, up_out, down_out,
):
    mixed_out[...] = mixed_ref[...]
    tokens_out[...] = tokens_ref[...]
    for out, ref in ((gate_out, gate_ref), (up_out, up_ref), (down_out, down_ref), (out_out, out_ref)):
        out[...] = ref[...].astype(F32)
    shards = gl_ref.shape[0]
    chans = gl_ref.shape[3] // 2
    for out, first in ((gate_in_out, 0), (linear_in_out, chans)):
        for s in range(shards):
            out[:, s * chans : (s + 1) * chans] = gl_ref[s, 0, :, first : first + chans].astype(F32)

    @pl.when(pl.program_id(0) == 0)
    def _():
        size = rate_out.shape[0]
        rate_out[...] = bd_ref[:size].astype(F32)
        input_out[...] = bd_ref[size:].astype(F32)
        kernel_out[...] = small_ref[0:4, :chans]
        for i, out in ((4, bias_out), (5, rate_bias_out), (6, input_bias_out), (7, decay_out), (8, gain1_out), (9, gain2_out)):
            out[...] = small_ref[i, : out.shape[0]]


def widen_call(mixed, grad_tokens, small, gate, up, down, gl, out, bd, gain_size):
    shards, groups, quarter_rows, both = gl.shape
    chans = out.shape[0]

    def rows_of(dims):
        return pl.BlockSpec((dims[0] // groups, dims[1]), lambda i: (i, 0))

    def whole(dims):
        return pl.BlockSpec(dims, lambda i: (0,) * len(dims))

    wide = (groups * quarter_rows, shards * chans)
    block = (bd.shape[0] // 2, bd.shape[1])
    shapes = [
        mixed.shape, grad_tokens.shape, (gain_size,), wide, wide, (4, chans), (chans,), block, (chans,), block, (chans,), (chans,),
        out.shape, (gain_size,), gate.shape, up.shape, down.shape,
    ]
    specs = [whole(dims) if len(dims) == 1 or dims in ((4, chans), block) else rows_of(dims) for dims in shapes]
    return pl.pallas_call(
        widen_kernel,
        grid=(groups,),
        in_specs=[rows_of(mixed.shape), rows_of(grad_tokens.shape), whole(small.shape)]
        + [rows_of(a.shape) for a in (gate, up, down)]
        + [pl.BlockSpec((shards, 1, quarter_rows, both), lambda i: (0, i, 0, 0)), rows_of(out.shape), whole(bd.shape)],
        out_specs=specs,
        out_shape=[jax.ShapeDtypeStruct(dims, BF16 if i < 2 else F32) for i, dims in enumerate(shapes)],
        compiler_params=pltpu.CompilerParams(vmem_limit_bytes=VMEM_LIMIT),
        name="widen",
    )(mixed, grad_tokens, small, gate, up, down, gl, out, bd)


def per_device_split(
    tokens, lengths, cotangent, norm1_gain, gate_in, linear_in, conv_kernel, conv_bias, rate_weight,
    rate_bias, input_weight, input_bias, decay_param, out_proj, norm2_gain, mlp_gate, mlp_up, mlp_down,
):
    chans, size = rate_weight.shape
    gathered, weights, mlp_weights, gains, saved, merged, middle, normed_two, vec, gates, g_low = forward_call(
        lengths, tokens, cotangent,
        (norm1_gain, norm2_gain, conv_kernel, conv_bias, rate_bias, input_bias, decay_param, rate_weight.T, input_weight.T),
        out_proj, gate_in, linear_in, mlp_gate, mlp_up,
    )
    quarter_gu, quarter_down, mixed, g_middle, gain_terms = mlp_call(
        lengths, normed_two, middle, gains, g_low, mlp_weights, mlp_down
    )
    grad_gate, grad_up, grad_down, gl, grad_out, bd, grad_tokens, small = backward_call(
        size, lengths, tokens, g_middle, gains, gain_terms, vec, gates, out_proj, quarter_gu, quarter_down, weights, saved, merged,
        gathered,
    )
    outs = list(widen_call(
        mixed, grad_tokens, small, grad_gate, grad_up, grad_down.reshape(mlp_down.shape), gl, grad_out.reshape(out_proj.shape),
        bd.reshape(2 * size, chans), norm1_gain.shape[0],
    ))
    for i in (7, 9):
        outs[i] = outs[i].T
    return tuple(outs)


def as_sent(shard):
    return jax.tree.map(lambda a: a.astype(jnp.bfloat16) if a.dtype == jnp.float32 else a, shard)


def layout(counts, row_count):
    first = counts[0]
    second = first + counts[1]
    run_ends = jnp.stack([first, second, second + counts[2], second + counts[2] + counts[3]])
    positions = jnp.arange(row_count, dtype=jnp.int32)
    segment_ids = jnp.sum((positions[:, None] >= run_ends[None, :-1]).astype(jnp.int32), axis=1)
    live_rows = (positions < run_ends[-2]).astype(jnp.float32)
    return (segment_ids, live_rows)


def earlier_ids(segment_ids, offset):
    filler = jnp.full((offset,), -1, dtype=jnp.int32)
    return jnp.concatenate([filler, segment_ids[:-offset]])


def normalize(values, gain_vec):
    scale = lax.rsqrt(jnp.mean(values * values, axis=1, keepdims=True) + EPSILON)
    return values * scale * gain_vec


def convolve(linear_out, kernel, shift_vec, segment_ids):
    summed = linear_out * kernel[0] + shift_vec
    for offset in range(1, kernel.shape[0]):
        shifted = jnp.concatenate(
            [jnp.zeros((offset, linear_out.shape[1]), linear_out.dtype), linear_out[:-offset]],
            axis=0,
        )
        same_seq = (earlier_ids(segment_ids, offset) == segment_ids).astype(linear_out.dtype)
        summed = summed + kernel[offset] * shifted * same_seq[:, None]
    return summed


def combine_pairs(earlier_pair, later_pair):
    return (earlier_pair[0] * later_pair[0], later_pair[0] * earlier_pair[1] + later_pair[1])


def recurrence(rate_pre, input_pre, inflow, decay_vec, segment_ids):
    rate_gate = jax.nn.sigmoid(rate_pre)
    opened = jax.nn.sigmoid(input_pre)
    log_keep = -RATE_SCALE * rate_gate * jax.nn.softplus(-decay_vec)
    factor = jnp.exp(log_keep)
    weight_in = jnp.sqrt(-jnp.expm1(2.0 * log_keep))
    same_run = (earlier_ids(segment_ids, 1) == segment_ids).astype(factor.dtype)
    carried, states = lax.associative_scan(
        combine_pairs, (factor * same_run[:, None], weight_in * opened * inflow), axis=0
    )
    return states


def gated_gelu(gate_vals, up_vals):
    return jax.nn.gelu(gate_vals) * up_vals


def product(left, right):
    return jnp.dot(left, right, preferred_element_type=jnp.float32)


def contract(left, right):
    return jnp.einsum("ti,tj->ij", left, right, preferred_element_type=jnp.float32)


def back_dot(grad_vals, weight):
    return jnp.einsum("tj,ij->ti", grad_vals, weight, preferred_element_type=jnp.float32)


def blocked(values, weight):
    row_count = values.shape[0]
    size = weight.shape[1]
    heads = weight.shape[0] // size
    return jnp.einsum(
        "thj,hjk->thk",
        values.reshape(row_count, heads, size),
        weight.reshape(heads, size, size),
        preferred_element_type=jnp.float32,
    ).reshape(row_count, heads * size)


def block_terms(values, grad_vals, size):
    row_count = values.shape[0]
    heads = values.shape[1] // size
    terms = jnp.einsum(
        "thj,thk->hjk",
        values.reshape(row_count, heads, size),
        grad_vals.reshape(row_count, heads, size),
        preferred_element_type=jnp.float32,
    )
    return terms.reshape(heads * size, size)


def block_back(grad_vals, weight):
    row_count = grad_vals.shape[0]
    size = weight.shape[1]
    heads = weight.shape[0] // size
    return jnp.einsum(
        "thk,hjk->thj",
        grad_vals.reshape(row_count, heads, size),
        weight.reshape(heads, size, size),
        preferred_element_type=jnp.float32,
    ).reshape(row_count, heads * size)


def per_device_general(
    tokens,
    lengths,
    cotangent,
    norm1_gain,
    gate_in,
    linear_in,
    conv_kernel,
    conv_bias,
    rate_weight,
    rate_bias,
    input_weight,
    input_bias,
    decay_param,
    out_proj,
    norm2_gain,
    mlp_gate,
    mlp_up,
    mlp_down,
):
    row_count = tokens.shape[0]
    segment_ids, live_rows = layout(lengths[0], row_count)
    live_col = live_rows[:, None]
    mixer_full = (
        lax.all_gather(norm1_gain, "shard", axis=0, tiled=True),
        lax.all_gather(gate_in, "shard", axis=0, tiled=True),
        lax.all_gather(linear_in, "shard", axis=0, tiled=True),
        lax.all_gather(conv_kernel, "shard", axis=1, tiled=True),
        lax.all_gather(conv_bias, "shard", axis=0, tiled=True),
        lax.all_gather(rate_weight, "shard", axis=0, tiled=True),
        lax.all_gather(rate_bias, "shard", axis=0, tiled=True),
        lax.all_gather(input_weight, "shard", axis=0, tiled=True),
        lax.all_gather(input_bias, "shard", axis=0, tiled=True),
        lax.all_gather(decay_param, "shard", axis=0, tiled=True),
        lax.all_gather(out_proj, "shard", axis=0, tiled=True),
    )
    gain_first = mixer_full[0].astype(jnp.float32)
    kernel_full = mixer_full[3].astype(jnp.float32)
    kernel_shift = mixer_full[4].astype(jnp.float32)
    rate_shift = mixer_full[6].astype(jnp.float32)
    input_shift = mixer_full[8].astype(jnp.float32)
    decay_full = mixer_full[9].astype(jnp.float32)
    block_size = mixer_full[5].shape[1]
    masked_in = tokens.astype(jnp.float32) * live_col
    normed_low = normalize(masked_in, gain_first).astype(jnp.bfloat16)
    gate_pre = product(normed_low, mixer_full[1])
    linear_out = product(normed_low, mixer_full[2])
    gate_act = jax.nn.gelu(gate_pre)
    conv_out = convolve(linear_out, kernel_full, kernel_shift, segment_ids)
    conv_low = conv_out.astype(jnp.bfloat16)
    rate_pre = blocked(conv_low, mixer_full[5]) + rate_shift
    input_pre = blocked(conv_low, mixer_full[7]) + input_shift
    states = recurrence(rate_pre, input_pre, conv_out, decay_full, segment_ids)
    merged_low = (gate_act * states).astype(jnp.bfloat16)
    middle = masked_in + product(merged_low, mixer_full[10])
    mlp_full = (
        lax.all_gather(norm2_gain, "shard", axis=0, tiled=True),
        lax.all_gather(mlp_gate, "shard", axis=0, tiled=True),
        lax.all_gather(mlp_up, "shard", axis=0, tiled=True),
        lax.all_gather(mlp_down, "shard", axis=0, tiled=True),
    )
    gain_second = mlp_full[0].astype(jnp.float32)
    normed_two = normalize(middle, gain_second).astype(jnp.bfloat16)
    gate_mlp = product(normed_two, mlp_full[1])
    up_mlp = product(normed_two, mlp_full[2])
    hidden_low = gated_gelu(gate_mlp, up_mlp).astype(jnp.bfloat16)
    mixed_out = ((middle + product(hidden_low, mlp_full[3])) * live_col).astype(jnp.bfloat16)
    grad_out = cotangent.astype(jnp.float32) * live_col
    grad_down = grad_out.astype(jnp.bfloat16)
    again_mlp = (
        lax.all_gather(mlp_gate, "shard", axis=0, tiled=True),
        lax.all_gather(mlp_up, "shard", axis=0, tiled=True),
        lax.all_gather(mlp_down, "shard", axis=0, tiled=True),
    )
    term_down = contract(hidden_low, grad_down)
    part_down = lax.psum_scatter(
        term_down.astype(jnp.bfloat16), "shard", scatter_dimension=0, tiled=True
    ).astype(jnp.float32)
    grad_hidden = back_dot(grad_down, again_mlp[2])
    unused_val, hidden_back = jax.vjp(gated_gelu, gate_mlp, up_mlp)
    grad_gate_mlp, grad_up_mlp = hidden_back(grad_hidden)
    gate_mlp_low = grad_gate_mlp.astype(jnp.bfloat16)
    up_mlp_low = grad_up_mlp.astype(jnp.bfloat16)
    term_gate_mlp = contract(normed_two, gate_mlp_low)
    term_up_mlp = contract(normed_two, up_mlp_low)
    grad_normed_two = back_dot(gate_mlp_low, again_mlp[0]) + back_dot(up_mlp_low, again_mlp[1])
    unused_two, second_back = jax.vjp(normalize, middle, gain_second)
    grad_middle_norm, term_gain_two = second_back(grad_normed_two)
    parts_mlp = (
        lax.psum_scatter(
            term_gain_two.astype(jnp.bfloat16), "shard", scatter_dimension=0, tiled=True
        ).astype(jnp.float32),
        lax.psum_scatter(
            term_gate_mlp.astype(jnp.bfloat16), "shard", scatter_dimension=0, tiled=True
        ).astype(jnp.float32),
        lax.psum_scatter(
            term_up_mlp.astype(jnp.bfloat16), "shard", scatter_dimension=0, tiled=True
        ).astype(jnp.float32),
    )
    grad_middle = grad_out + grad_middle_norm
    grad_mix_low = grad_middle.astype(jnp.bfloat16)
    again_mixer = (
        lax.all_gather(gate_in, "shard", axis=0, tiled=True),
        lax.all_gather(linear_in, "shard", axis=0, tiled=True),
        lax.all_gather(rate_weight, "shard", axis=0, tiled=True),
        lax.all_gather(input_weight, "shard", axis=0, tiled=True),
        lax.all_gather(out_proj, "shard", axis=0, tiled=True),
    )
    term_out = contract(merged_low, grad_mix_low)
    grad_merged = back_dot(grad_mix_low, again_mixer[4])
    grad_states = grad_merged * gate_act
    unused_three, gelu_back = jax.vjp(jax.nn.gelu, gate_pre)
    gate_low = gelu_back(grad_merged * states)[0].astype(jnp.bfloat16)
    unused_four, scan_back = jax.vjp(
        partial(recurrence, segment_ids=segment_ids), rate_pre, input_pre, conv_out, decay_full
    )
    grad_rate, grad_input, grad_flow, term_decay = scan_back(grad_states)
    rate_low = grad_rate.astype(jnp.bfloat16)
    input_low = grad_input.astype(jnp.bfloat16)
    term_rate = block_terms(conv_low, rate_low, block_size)
    term_input = block_terms(conv_low, input_low, block_size)
    term_rate_shift = jnp.sum(rate_low.astype(jnp.float32), axis=0)
    term_input_shift = jnp.sum(input_low.astype(jnp.float32), axis=0)
    grad_conv = (
        grad_flow + block_back(rate_low, again_mixer[2]) + block_back(input_low, again_mixer[3])
    )
    unused_five, conv_back = jax.vjp(
        partial(convolve, segment_ids=segment_ids), linear_out, kernel_full, kernel_shift
    )
    grad_linear, term_kernel, term_kernel_shift = conv_back(grad_conv)
    linear_low = grad_linear.astype(jnp.bfloat16)
    term_gate_in = contract(normed_low, gate_low)
    term_linear = contract(normed_low, linear_low)
    grad_normed = back_dot(gate_low, again_mixer[0]) + back_dot(linear_low, again_mixer[1])
    unused_six, first_back = jax.vjp(normalize, masked_in, gain_first)
    grad_masked, term_gain_one = first_back(grad_normed)
    grad_tokens = ((grad_middle + grad_masked) * live_col).astype(jnp.bfloat16)
    small_terms = (
        term_gain_one,
        term_kernel,
        term_kernel_shift,
        term_rate,
        term_rate_shift,
        term_input,
        term_input_shift,
        term_decay,
    )
    placed = tuple((term for term in small_terms))
    mixer_terms = (
        placed[0],
        term_gate_in,
        term_linear,
        placed[1],
        placed[2],
        placed[3],
        placed[4],
        placed[5],
        placed[6],
        placed[7],
        term_out,
    )
    parts_mixer = (
        lax.psum_scatter(
            mixer_terms[0].astype(jnp.bfloat16), "shard", scatter_dimension=0, tiled=True
        ).astype(jnp.float32),
        lax.psum_scatter(
            mixer_terms[1].astype(jnp.bfloat16), "shard", scatter_dimension=0, tiled=True
        ).astype(jnp.float32),
        lax.psum_scatter(
            mixer_terms[2].astype(jnp.bfloat16), "shard", scatter_dimension=0, tiled=True
        ).astype(jnp.float32),
        lax.psum_scatter(
            mixer_terms[3].astype(jnp.bfloat16), "shard", scatter_dimension=1, tiled=True
        ).astype(jnp.float32),
        lax.psum_scatter(
            mixer_terms[4].astype(jnp.bfloat16), "shard", scatter_dimension=0, tiled=True
        ).astype(jnp.float32),
        lax.psum_scatter(
            mixer_terms[5].astype(jnp.bfloat16), "shard", scatter_dimension=0, tiled=True
        ).astype(jnp.float32),
        lax.psum_scatter(
            mixer_terms[6].astype(jnp.bfloat16), "shard", scatter_dimension=0, tiled=True
        ).astype(jnp.float32),
        lax.psum_scatter(
            mixer_terms[7].astype(jnp.bfloat16), "shard", scatter_dimension=0, tiled=True
        ).astype(jnp.float32),
        lax.psum_scatter(
            mixer_terms[8].astype(jnp.bfloat16), "shard", scatter_dimension=0, tiled=True
        ).astype(jnp.float32),
        lax.psum_scatter(
            mixer_terms[9].astype(jnp.bfloat16), "shard", scatter_dimension=0, tiled=True
        ).astype(jnp.float32),
        lax.psum_scatter(
            mixer_terms[10].astype(jnp.bfloat16), "shard", scatter_dimension=0, tiled=True
        ).astype(jnp.float32),
    )
    shard_parts = tuple(parts_mixer) + (parts_mlp[0], parts_mlp[1], parts_mlp[2], part_down)
    totals = jax.tree.map(
        lambda part: part.astype(jnp.float32), lax.psum(as_sent(shard_parts), "group")
    )
    return (mixed_out, grad_tokens) + tuple(totals)


def solution(mesh):
    placed = (
        P(("group", "shard"), None),
        P(("group", "shard"), None),
        P(("group", "shard"), None),
        P("shard"),
        P("shard", None),
        P("shard", None),
        P(None, "shard"),
        P("shard"),
        P("shard", None),
        P("shard"),
        P("shard", None),
        P("shard"),
        P("shard"),
        P("shard", None),
        P("shard"),
        P("shard", None),
        P("shard", None),
        P("shard", None),
    )
    split_fits = FAST_MESH == tuple(mesh.shape[axis] for axis in ("group", "shard"))
    return jax.shard_map(
        per_device_split if split_fits else per_device_general,
        mesh=mesh,
        in_specs=placed,
        out_specs=(
            P(("group", "shard"), None),
            P(("group", "shard"), None),
            P("shard"),
            P("shard", None),
            P("shard", None),
            P(None, "shard"),
            P("shard"),
            P("shard", None),
            P("shard"),
            P("shard", None),
            P("shard"),
            P("shard"),
            P("shard", None),
            P("shard"),
            P("shard", None),
            P("shard", None),
            P("shard", None),
        ),
        check_vma=False,
    )
```

```python
from functools import partial

import jax
import jax.numpy as jnp
from jax import lax
from jax.experimental import pallas as pl
from jax.experimental.pallas import tpu as pltpu
from jax.sharding import PartitionSpec as P

FAST_MESH = (4, 8)
RATE_SCALE = 8.0
EPSILON = 1e-06
F32 = jnp.float32
BF16 = jnp.bfloat16
GELU_C = 0.7978845608028654
GELU_K = 0.044715
CAP = 128


def positions_in_run(counts, row_count):
    first = counts[0]
    second = first + counts[1]
    third = second + counts[2]
    rows = lax.broadcasted_iota(jnp.int32, (row_count, 1), 0).astype(F32)
    start = jnp.where(rows >= first, first, 0.0)
    start = jnp.where(rows >= second, second, start)
    start = jnp.where(rows >= third, third, start)
    return rows - start, (rows < third).astype(F32)


def gelu_parts(x):
    t = jnp.tanh(GELU_C * (x + GELU_K * x * x * x))
    value = 0.5 * x * (1.0 + t)
    slope = 0.5 * (1.0 + t) + 0.5 * x * (1.0 - t * t) * GELU_C * (1.0 + 3.0 * GELU_K * x * x)
    return value, slope


def gelu_value(x):
    return 0.5 * x * (1.0 + jnp.tanh(GELU_C * (x + GELU_K * x * x * x)))


def sigmoid(x):
    return 0.5 * (1.0 + jnp.tanh(0.5 * x))


def one_less_exp(z):
    series = 1.0 - z * (1.0 / 7.0)
    for k in (6.0, 5.0, 4.0, 3.0, 2.0):
        series = 1.0 - z * (1.0 / k) * series
    return jnp.where(z < 0.35, z * series, 1.0 - jnp.exp(-z))


def softplus_neg(x):
    return jnp.maximum(-x, 0.0) + jnp.log1p(jnp.exp(-jnp.abs(x)))


def mm(a, b):
    return jnp.dot(a, b, preferred_element_type=F32)


def mm_nt(a, b):
    return lax.dot_general(a, b, (((1,), (1,)), ((), ())), preferred_element_type=F32)


def mm_tn(a, b):
    return lax.dot_general(a, b, (((0,), (0,)), ((), ())), preferred_element_type=F32)


def roll_rows(x, n):
    return pltpu.roll(x, n % x.shape[0], 0)


def conv_rows(linear, kernel, bias, masks):
    out = linear * kernel[0:1] + bias
    for k in range(1, 4):
        out = out + kernel[k : k + 1] * (roll_rows(linear, k) * masks[k - 1])
    return out


def decay_terms(rate_pre, decay):
    rate = sigmoid(rate_pre)
    keep = RATE_SCALE * rate * softplus_neg(decay)
    return rate, jnp.exp(-keep), jnp.sqrt(one_less_exp(2.0 * keep))


MESH_ID = pl.DeviceIdType.MESH
VMEM_LIMIT = 62 * 2**20
N_Z, N_X = 4, 2


def place():
    shard = lax.axis_index("shard")
    return lax.axis_index("group"), shard, shard // N_X, shard % N_X


def greet(peers):
    bar = pltpu.get_barrier_semaphore()
    count = 0
    for device, there in peers:
        if there is True:
            pl.semaphore_signal(bar, inc=1, device_id=device, device_id_type=MESH_ID)
            count = count + 1
        else:
            @pl.when(there)
            def _(device=device):
                pl.semaphore_signal(bar, inc=1, device_id=device, device_id_type=MESH_ID)
            count = count + there.astype(jnp.int32)
    pl.semaphore_wait(bar, count)


def line_peers():
    group, shard, z, x = place()
    return [
        ((group, shard + N_X), z < N_Z - 1),
        ((group, shard - N_X), z > 0),
        ((group, z * N_X + 1 - x), True),
    ]


class Gather:
    CHUNKS = 2

    @classmethod
    def scratch(cls):
        return [pltpu.SemaphoreType.DMA((3, N_Z, cls.CHUNKS)), pltpu.SemaphoreType.DMA((N_Z * N_X, cls.CHUNKS))]

    def __init__(self, buf, sems):
        self.buf, (self.send, self.recv) = buf, sems
        self.group, self.shard, self.z, self.x = place()
        self.rows = buf.shape[1] // self.CHUNKS

    def copy(self, origin, column, c, way):
        slot = origin * N_X + column
        z = (self.z + 1, self.z - 1, self.z)[way]
        x = 1 - self.x if way == 2 else self.x
        piece = self.buf.at[slot, pl.ds(c * self.rows, self.rows)]
        return pltpu.make_async_remote_copy(
            src_ref=piece, dst_ref=piece, send_sem=self.send.at[way, origin, c],
            recv_sem=self.recv.at[slot, c], device_id=(self.group, z * N_X + x), device_id_type=MESH_ID,
        )

    def start(self):
        for c in range(self.CHUNKS):
            self.forward(self.z, c, True, True)

    def forward(self, origin, c, up, down):
        if up:
            @pl.when(self.z < N_Z - 1)
            def _():
                self.copy(origin, self.x, c, 0).start()
        if down:
            @pl.when(self.z > 0)
            def _():
                self.copy(origin, self.x, c, 1).start()
        self.copy(origin, self.x, c, 2).start()

    def step(self, k):
        for c in range(self.CHUNKS):
            @pl.when(self.z >= k)
            def _(c=c):
                self.copy(self.z - k, self.x, c, 2).wait_recv()
                self.forward(self.z - k, c, True, False)

            @pl.when(self.z + k < N_Z)
            def _(c=c):
                self.copy(self.z + k, self.x, c, 2).wait_recv()
                self.forward(self.z + k, c, False, True)

    def wait_across(self, origin):
        for c in range(self.CHUNKS):
            self.copy(origin, 1 - self.x, c, 2).wait_recv()

    def finish(self):
        for c in range(self.CHUNKS):
            for origin in range(N_Z):
                @pl.when((self.z < N_Z - 1) & (origin <= self.z))
                def _():
                    self.copy(origin, self.x, c, 0).wait_send()

                @pl.when((self.z > 0) & (origin >= self.z))
                def _():
                    self.copy(origin, self.x, c, 1).wait_send()
                self.copy(origin, self.x, c, 2).wait_send()


class Scatter:
    CHUNKS = 2

    @classmethod
    def scratch(cls, rows, width):
        dma = pltpu.SemaphoreType.DMA
        return [
            pltpu.VMEM((N_Z, rows, width), BF16),
            pltpu.VMEM((N_Z + 1, rows, width), BF16),
            dma((2, N_Z, cls.CHUNKS)), dma((N_Z, cls.CHUNKS)), dma((N_Z + 1, cls.CHUNKS)),
        ]

    def __init__(self, away, own, scratch):
        self.away, self.own = away, own
        self.across, self.along, self.send, self.recv_x, self.recv_z = scratch
        self.group, self.shard, self.z, self.x = place()
        self.rows = self.across.shape[1] // self.CHUNKS

    @classmethod
    def of(cls, parts, scratch):
        _, _, _, x = place()
        return cls(lambda k: parts.at[k * N_X + 1 - x], lambda k: parts.at[k * N_X + x], scratch)

    def dest(self, i):
        low = jnp.minimum(self.z, N_Z - 1 - self.z)
        value = (N_Z - 1, N_Z - 2, jnp.where(low == 0, 1, 0), low)[i]
        return jnp.where(self.z >= N_Z // 2, N_Z - 1 - value, value)

    def span(self, c):
        return pl.ds(c * self.rows, self.rows)

    def copy_x(self, dest, c):
        return pltpu.make_async_remote_copy(
            src_ref=self.away(dest).at[self.span(c)], dst_ref=self.across.at[dest, self.span(c)],
            send_sem=self.send.at[0, dest, c], recv_sem=self.recv_x.at[dest, c],
            device_id=(self.group, self.z * N_X + 1 - self.x), device_id_type=MESH_ID,
        )

    def copy_z(self, dest, slot, c, step):
        return pltpu.make_async_remote_copy(
            src_ref=self.own(dest).at[self.span(c)], dst_ref=self.along.at[slot, self.span(c)],
            send_sem=self.send.at[1, dest, c], recv_sem=self.recv_z.at[slot, c],
            device_id=(self.group, (self.z + step) * N_X + self.x), device_id_type=MESH_ID,
        )

    def start(self, i):
        for c in range(self.CHUNKS):
            self.copy_x(self.dest(i), c).start()

    def arrived(self, slot, c):
        self.copy_z(0, slot, c, 0).wait_recv()
        return self.along[slot, self.span(c)].astype(F32)

    def half(self, dest, c):
        return self.own(dest)[self.span(c)].astype(F32) + self.across[dest, self.span(c)].astype(F32)

    def step(self, i):
        dest = self.dest(i)
        own = self.own(dest)
        for c in range(self.CHUNKS):
            self.copy_x(dest, c).wait_recv()
            inner = ((dest > self.z) & (self.z > 0)) | ((dest < self.z) & (self.z < N_Z - 1))

            @pl.when(inner)
            def _(c=c):
                own[self.span(c)] = (self.half(dest, c) + self.arrived(dest, c)).astype(BF16)

            @pl.when(jnp.logical_not(inner))
            def _(c=c):
                own[self.span(c)] = self.half(dest, c).astype(BF16)

            @pl.when(dest > self.z)
            def _(c=c):
                self.copy_z(dest, dest, c, 1).start()

            @pl.when(dest < self.z)
            def _(c=c):
                self.copy_z(dest, jnp.where(dest == self.z - 1, N_Z, dest), c, -1).start()

    def last(self, out):
        for c in range(self.CHUNKS):
            self.copy_x(self.z, c).wait_recv()
            out[self.span(c)] = self.half(self.z, c)

            @pl.when(self.z > 0)
            def _(c=c):
                out[self.span(c)] += self.arrived(self.z, c)

            @pl.when(self.z < N_Z - 1)
            def _(c=c):
                out[self.span(c)] += self.arrived(N_Z, c)

    def finish(self):
        for c in range(self.CHUNKS):
            for dest in range(N_Z):
                self.copy_x(dest, c).wait_send()

                @pl.when(dest != self.z)
                def _():
                    self.copy_z(dest, 0, c, 0).wait_send()


class FineScatter(Scatter):
    CHUNKS = 4


class Exchange:
    @classmethod
    def scratch(cls, blocks, count):
        dma = pltpu.SemaphoreType.DMA
        return [dma((count, blocks)), dma((count, blocks)), dma((3, count, blocks)), dma((3, count, blocks))]

    def __init__(self, sources, views, blocks, sems):
        self.sources, self.views, self.blocks = sources, views, blocks
        self.send_first, self.recv_first, self.send, self.recv = sems
        self.group, self.shard, _, _ = place()
        self.home = self.shard if blocks > 1 else 0
        self.core_mate, self.y_mate = mates()
        self.count = len(sources)

    def first(self, j, to, origin):
        return pltpu.make_async_remote_copy(
            src_ref=self.sources[j](to), dst_ref=self.views[j](origin, self.group),
            send_sem=self.send_first.at[j, to], recv_sem=self.recv_first.at[j, origin],
            device_id=(self.group, to), device_id_type=MESH_ID,
        )

    def own(self, j):
        return pltpu.make_async_copy(
            self.sources[j](self.home), self.views[j](self.home, self.group), self.recv_first.at[j, self.home]
        )

    def pass_on(self, j, origin, quarter, mate, way, source=None):
        piece = self.views[j](origin, quarter)
        return pltpu.make_async_remote_copy(
            src_ref=piece if source is None else source, dst_ref=piece, send_sem=self.send.at[way, j, origin], recv_sem=self.recv.at[way, j, origin],
            device_id=(mate, self.shard), device_id_type=MESH_ID,
        )

    def others(self, body):
        if self.blocks > 1:
            pl.loop(1, self.blocks)(lambda i: body((self.home + i) % self.blocks))

    def start(self):
        for j in range(self.count):
            self.own(j).start()

        def send(to):
            for j in range(self.count):
                self.first(j, to, self.home).start()

        self.others(send)

    def both(self, j, origin, source=None):
        self.pass_on(j, origin, self.group, self.y_mate, 1, source).start()
        self.pass_on(j, origin, self.group, self.core_mate, 0, source).start()

    def spread(self):
        for j in range(self.count):
            self.both(j, self.home, self.sources[j](self.home))

        def forward(origin):
            for j in range(self.count):
                self.first(j, origin, origin).wait_recv()
                self.both(j, origin)

        self.others(forward)

    def each(self, body):
        for j in range(self.count):
            body(j, self.home)

        def rest(origin):
            for j in range(self.count):
                body(j, origin)

        self.others(rest)

    def relay(self):
        def forward(j, origin):
            self.pass_on(j, origin, self.y_mate, self.core_mate, 1).wait_recv()
            self.pass_on(j, origin, self.y_mate, self.core_mate, 2).start()

        self.each(forward)

    def arrive(self):
        def wait(j, origin):
            self.pass_on(j, origin, self.group, self.core_mate, 0).wait_recv()
            self.pass_on(j, origin, self.group, self.core_mate, 2).wait_recv()

        for j in range(self.count):
            self.own(j).wait()
        self.each(wait)

    def finish(self):
        def sent(to):
            for j in range(self.count):
                self.first(j, to, self.home).wait_send()

        def passed(j, origin):
            for way in range(3):
                self.pass_on(j, origin, self.group, self.core_mate, way).wait_send()

        self.others(sent)
        self.each(passed)


def mates():
    group = lax.axis_index("group")
    return group + 1 - 2 * (group % 2), group + 2 - 4 * (group // 2)


def all_peers():
    group, shard, _, _ = place()
    core_mate, y_mate = mates()
    others = [((group, (shard + i) % (N_Z * N_X)), True) for i in range(1, N_Z * N_X)]
    return others + [((core_mate, shard), True), ((y_mate, shard), True)]


def mixer_forward(linear, gate, pos, vec, gates):
    masks = [(pos >= k).astype(F32) for k in (1, 2, 3)]
    conv = conv_rows(linear, vec[0:4], vec[4:5], masks)
    width = linear.shape[1]
    both = mm_nt(conv.astype(BF16), gates)
    rate_pre = both[:, :width] + vec[5:6]
    input_pre = both[:, width:] + vec[6:7]
    _, a, weight_in = decay_terms(rate_pre, vec[7:8])
    mult = a * masks[0]
    total = weight_in * sigmoid(input_pre) * conv
    step = 1
    while step < CAP:
        total = total + mult * roll_rows(total, step)
        if 2 * step < CAP:
            mult = mult * roll_rows(mult, step)
        step *= 2
    return rate_pre, input_pre, total, (gelu_value(gate) * total).astype(BF16)


def pair_positions(gains, origin, rows):
    places = []
    for column in range(N_X):
        lengths = gains[origin * N_X + column, 2:3]
        places.append(positions_in_run([lengths[:, i : i + 1] for i in range(3)], rows)[0])
    return jnp.concatenate(places, axis=0)


def rms_scale(values):
    return lax.rsqrt(jnp.mean(values * values, axis=1, keepdims=True) + EPSILON)


def forward_kernel(
    lengths_ref, tokens_ref, cotangent_ref, gain1_ref, gain2_ref, kernel_ref, bias_ref, rate_bias_ref, input_bias_ref, decay_ref, rate_weight_ref,
    input_weight_ref, out_proj_ref, gate_in_ref, linear_in_ref, mlp_gate_ref, mlp_up_ref,
    gather_out, weights_out, mlp_out, gains_out, saved_out, merged_out, middle_ref, normed_two_ref, vec_ref, gates_ref, g_low_out,
    gains_ref, g_low, buf, weights, quarter, raw, masked, saved, merged, parts,
    gather_a, gather_b, ex_a, ex_b, ex_c, ex_d, mx_a, mx_b, mx_c, mx_d, *rest,
):
    scatter_scratch, rest = rest[:-8], rest[-8:]
    gain_send, gain_recv, raw_sem, out_sem, pair_sem, g_sem, g_send, g_recv = rest
    group, shard, z, x = place()
    shards = N_Z * N_X
    rows, width = tokens_ref.shape
    quarter_rows = raw.shape[1]
    chans = linear_in_ref.shape[1] // shards
    padded = vec_ref.shape[1]
    fetch = [
        pltpu.make_async_copy(ref.at[pl.ds(group * quarter_rows, quarter_rows)], raw.at[i], raw_sem.at[i])
        for i, ref in enumerate((gate_in_ref, linear_in_ref))
    ]
    for copy in fetch:
        copy.start()
    gains_ref[...] = jnp.zeros_like(gains_ref)
    gains_ref[0:1] = gain1_ref[...].astype(F32).reshape(1, -1)
    gains_ref[1:2] = gain2_ref[...].astype(F32).reshape(1, -1)
    lane = lax.broadcasted_iota(jnp.int32, (1, gains_ref.shape[1]), 1)
    for i in range(3):
        gains_ref[2:3] += jnp.where(lane == i, lengths_ref[0, i].astype(F32), 0.0)
    greet(all_peers())

    def gain_copy(to, origin):
        return pltpu.make_async_remote_copy(
            src_ref=gains_ref, dst_ref=gains_out.at[origin], send_sem=gain_send.at[to], recv_sem=gain_recv.at[origin],
            device_id=(group, to), device_id_type=MESH_ID,
        )

    for i in range(1, shards):
        gain_copy((shard + i) % shards, shard).start()
    gains_out[shard] = gains_ref[...]
    for copy in fetch:
        copy.wait()
    for to in range(shards):
        part = slice(to * chans, (to + 1) * chans)
        quarter[to] = jnp.concatenate([raw[0, :, part].astype(F32), raw[1, :, part].astype(F32)], axis=1).astype(BF16)
    exchange = Exchange(
        [lambda to: quarter.at[to]], [lambda origin, q: weights.at[origin, q]], shards, (ex_a, ex_b, ex_c, ex_d)
    )
    exchange.start()
    hidden = mlp_up_ref.shape[1] // shards

    def part_of(ref):
        return lambda to: ref.at[pl.ds(group * quarter_rows, quarter_rows), pl.ds(to * hidden, hidden)]

    mlp_exchange = Exchange(
        [part_of(mlp_gate_ref), part_of(mlp_up_ref)],
        [lambda origin, q: mlp_out.at[origin, q, :, 0:hidden], lambda origin, q: mlp_out.at[origin, q, :, hidden : 2 * hidden]],
        shards, (mx_a, mx_b, mx_c, mx_d),
    )
    _, live = positions_in_run([lengths_ref[0, i].astype(F32) for i in range(3)], rows)
    masked[...] = tokens_ref[...].astype(F32) * live
    g_low[...] = (cotangent_ref[...].astype(F32) * live).astype(BF16)
    g_copy = pltpu.make_async_copy(g_low, g_low_out.at[shard], g_sem)
    g_copy.start()
    g_gather = Gather(g_low_out, (g_send, g_recv))
    for i in range(1, shards):
        gain_copy(shard, (shard + i) % shards).wait_recv()
    gains = jnp.concatenate([gains_out[i] for i in range(shards)], axis=1)
    gather = Gather(buf, (gather_a, gather_b))
    buf[shard] = (masked[...] * rms_scale(masked[...]) * gains[0:1]).astype(BF16)
    gather.start()
    vec_ref[...] = jnp.zeros_like(vec_ref)
    vec_ref[0:4, :chans] = kernel_ref[...].astype(F32)
    for i, ref in enumerate((bias_ref, rate_bias_ref, input_bias_ref, decay_ref)):
        vec_ref[4 + i : 5 + i, :chans] = ref[...].astype(F32).reshape(1, -1)
    gates_ref[...] = jnp.zeros_like(gates_ref)
    size = rate_weight_ref.shape[0]
    for i, ref in enumerate((rate_weight_ref, input_weight_ref)):
        for h in range(chans // size):
            part = slice(h * size, (h + 1) * size)
            gates_ref[i * padded + h * size : i * padded + (h + 1) * size, part] = ref[:, part]
    gather.step(1)
    exchange.spread()
    gather.step(2)
    exchange.relay()
    mlp_exchange.start()
    exchange.arrive()
    scatter = Scatter.of(parts, scatter_scratch)

    def pair_copies(origin):
        return [
            pltpu.make_async_copy(saved.at[origin], saved_out.at[origin], pair_sem.at[0, origin]),
            pltpu.make_async_copy(merged.at[origin], merged_out.at[origin], pair_sem.at[1, origin]),
        ]

    @pl.loop(0, N_Z)
    def _(i):
        @pl.when(i == 1)
        def _():
            gather.step(3)
            g_copy.wait()
            g_gather.start()

        origin = nearest(z, i)
        gather.wait_across(origin)
        pair = pl.ds(origin * N_X, N_X)
        pre = mm(buf[pair].reshape(N_X * rows, width), weights[...].reshape(width, 2 * chans))
        blank = jnp.zeros((N_X * rows, padded - chans), F32)
        gate = jnp.concatenate([pre[:, :chans], blank], axis=1)
        linear = jnp.concatenate([pre[:, chans:], blank], axis=1)
        where = pair_positions(gains_out, origin, rows)
        rate_pre, input_pre, state, merge = mixer_forward(linear, gate, where, vec_ref[...], gates_ref[...])
        for j, value in enumerate((gate, linear, rate_pre, input_pre, state)):
            saved[origin, j] = value
        merged[origin] = merge
        for copy in pair_copies(origin):
            copy.start()
        parts[pair] = mm(merge[:, :chans], out_proj_ref[...]).astype(BF16).reshape(N_X, rows, width)

    outs = [
        pltpu.make_async_copy(buf, gather_out, out_sem.at[0]),
        pltpu.make_async_copy(weights, weights_out, out_sem.at[1]),
    ]
    for copy in outs:
        copy.start()
    for i in range(N_Z):
        scatter.start(i)
    mlp_exchange.spread()
    scatter.step(0)
    g_gather.step(1)
    mlp_exchange.relay()
    scatter.step(1)
    g_gather.step(2)
    scatter.step(2)
    g_gather.step(3)
    scatter.last(middle_ref)
    middle_ref[...] += masked[...]
    normed_two_ref[...] = (middle_ref[...] * rms_scale(middle_ref[...]) * gains[1:2]).astype(BF16)
    for i in range(1, shards):
        gain_copy((shard + i) % shards, shard).wait_send()
    gather.finish()
    exchange.finish()
    for origin in range(N_Z):
        g_gather.wait_across(origin)
    g_gather.finish()
    mlp_exchange.arrive()
    mlp_exchange.finish()
    scatter.finish()
    for copy in outs:
        copy.wait()

    @pl.loop(0, N_Z)
    def _(origin):
        for copy in pair_copies(origin):
            copy.wait()


def nearest(z, i):
    low = jnp.minimum(z, N_Z - 1 - z)
    value = jnp.where(low == 0, i, jnp.where(i == 0, 1, jnp.where(i == 1, 0, i)))
    return jnp.where(z >= N_Z // 2, N_Z - 1 - value, value)


def any_spec():
    return pl.BlockSpec(memory_space=pl.ANY)


def vmem_spec():
    return pl.BlockSpec(memory_space=pltpu.VMEM)


def forward_call(lengths, tokens, cotangent, small, out_proj, gate_in, linear_in, mlp_gate, mlp_up):
    rows, width = tokens.shape
    shards, groups = lax.axis_size("shard"), lax.axis_size("group")
    chans = out_proj.shape[0]
    padded = -(-chans // 128) * 128
    gains = (8, width // shards)
    quarter_rows = gate_in.shape[0] // groups
    hidden = mlp_up.shape[1] // shards
    dma = pltpu.SemaphoreType.DMA
    shape = jax.ShapeDtypeStruct
    out_shape = [
        shape((shards, rows, width), BF16),
        shape((shards, groups, quarter_rows, 2 * chans), BF16),
        shape((shards, groups, quarter_rows, 2 * hidden), BF16),
        shape((shards,) + gains, F32),
        shape((N_Z, 5, N_X * rows, padded), F32),
        shape((N_Z, N_X * rows, padded), BF16),
        shape((rows, width), F32),
        shape((rows, width), BF16),
        shape((8, padded), F32),
        shape((2 * padded, padded), BF16),
        shape((shards, rows, width), BF16),
    ]
    return pl.pallas_call(
        forward_kernel,
        out_shape=out_shape,
        in_specs=[pl.BlockSpec(memory_space=pltpu.SMEM)] + [vmem_spec()] * 12 + [any_spec()] * 4,
        out_specs=[any_spec()] * 3 + [vmem_spec()] + [any_spec()] * 2 + [vmem_spec()] * 4 + [any_spec()],
        scratch_shapes=[
            pltpu.VMEM(gains, F32),
            pltpu.VMEM((rows, width), BF16),
            pltpu.VMEM((shards, rows, width), BF16),
            pltpu.VMEM((shards, groups, quarter_rows, 2 * chans), BF16),
            pltpu.VMEM((shards, quarter_rows, 2 * chans), BF16),
            pltpu.VMEM((2, quarter_rows, gate_in.shape[1]), BF16),
            pltpu.VMEM((rows, width), F32),
            pltpu.VMEM((N_Z, 5, N_X * rows, padded), F32),
            pltpu.VMEM((N_Z, N_X * rows, padded), BF16),
            pltpu.VMEM((shards, rows, width), BF16),
        ]
        + Gather.scratch()
        + Exchange.scratch(shards, 1)
        + Exchange.scratch(shards, 2)
        + Scatter.scratch(rows, width)
        + [dma((shards,)), dma((shards,)), dma((2,)), dma((2,)), dma((2, N_Z)), dma]
        + Gather.scratch(),
        compiler_params=pltpu.CompilerParams(collective_id=1, has_side_effects=True, vmem_limit_bytes=VMEM_LIMIT),
        name="mixer_forward",
    )(lengths, tokens, cotangent, *small, out_proj, gate_in, linear_in, mlp_gate, mlp_up)


class CoreSum:
    @classmethod
    def scratch(cls, count):
        return [pltpu.SemaphoreType.DMA((count, 2))] * 2

    def __init__(self, terms, arrived, sems):
        self.terms, self.arrived = terms, arrived
        self.send, self.recv = sems
        group, self.shard, _, _ = place()
        self.core, self.y = group % 2, group // 2
        self.core_mate, _ = mates()

    def copy(self, j, half):
        return pltpu.make_async_remote_copy(
            src_ref=self.terms[j](2 * half + 1 - self.core), dst_ref=self.arrived[j].at[half],
            send_sem=self.send.at[j, half], recv_sem=self.recv.at[j, half],
            device_id=(self.core_mate, self.shard), device_id_type=MESH_ID,
        )

    def mine(self, j, half):
        return self.terms[j](2 * half + self.core)

    def start(self, j):
        for half in (1 - self.y, self.y):
            self.copy(j, half).start()

    def add(self, j, half):
        self.copy(j, half).wait_recv()
        own = self.mine(j, half)

        @pl.loop(0, self.arrived[j].shape[1])
        def _(i):
            own[i] = (own[i].astype(F32) + self.arrived[j][half, i].astype(F32)).astype(BF16)

    def finish(self):
        for half in (0, 1):
            for j in range(len(self.terms)):
                self.copy(j, half).wait_send()


class LineSum:
    @classmethod
    def scratch(cls, count):
        return [pltpu.SemaphoreType.DMA((count,))] * 2

    def __init__(self, core_sum, arrived, sems):
        self.core_sum, self.arrived = core_sum, arrived
        self.send, self.recv = sems
        self.shard, self.y = core_sum.shard, core_sum.y
        _, self.y_mate = mates()

    def copy(self, j):
        return pltpu.make_async_remote_copy(
            src_ref=self.core_sum.mine(j, 1 - self.y), dst_ref=self.arrived[j],
            send_sem=self.send.at[j], recv_sem=self.recv.at[j],
            device_id=(self.y_mate, self.shard), device_id_type=MESH_ID,
        )

    def start(self, j):
        self.core_sum.add(j, 1 - self.y)
        self.copy(j).start()
        self.core_sum.add(j, self.y)

    def add(self, j):
        self.copy(j).wait_recv()
        own = self.core_sum.mine(j, self.y)

        @pl.loop(0, self.arrived[j].shape[0])
        def _(i):
            own[i] = (own[i].astype(F32) + self.arrived[j][i].astype(F32)).astype(BF16)

    def finish(self):
        self.core_sum.finish()
        for j in range(len(self.arrived)):
            self.copy(j).wait_send()


def split_gains(ref, row, values):
    size = ref.shape[2]
    for i in range(ref.shape[0]):
        ref[i, row : row + 1] = values[:, i * size : (i + 1) * size]


def norm_backward(values, gain, grad):
    scale = rms_scale(values)
    e = grad * gain
    back = scale * e - values * (scale * scale * scale) * jnp.mean(values * e, axis=1, keepdims=True)
    return back, jnp.sum(grad * values * scale, axis=0, keepdims=True)


def mlp_kernel(
    lengths_ref, normed_ref, middle_ref, gains_ref, g_low_ref, weights_ref, down_ref,
    quarter_gu_out, quarter_down_out, mixed_ref, g_middle_ref, gain_ref,
    normed, g_low, weights, down, hidden, grads, parts, mixed_parts, term_down,
    core_down, core_first, core_second, line_down, line_first, line_second, result, *sems,
):
    sems = list(sems)

    def take(n):
        taken = tuple(sems[:n])
        del sems[:n]
        return taken

    group, shard, z, x = place()
    core_mate, y_mate = mates()
    rows, width = normed_ref.shape
    size = hidden.shape[2]
    load_sem, out_sem = take(2)
    loads = [
        pltpu.make_async_copy(source, target, load_sem.at[i])
        for i, (source, target) in enumerate(((weights_ref, weights), (down_ref, down), (g_low_ref, g_low)))
    ]
    for copy in loads:
        copy.start()
    gather = Gather(normed, take(2))
    scatter = FineScatter.of(parts, take(5))
    mixed_scatter = FineScatter.of(mixed_parts, take(5))
    middle_tile = N_Z * N_X // 2
    core_sum = CoreSum(
        [lambda q: term_down.at[q], lambda q: weights.at[0:middle_tile, q], lambda q: weights.at[middle_tile : 2 * middle_tile, q]],
        [core_down, core_first, core_second], take(2),
    )
    line_sum = LineSum(core_sum, [line_down, line_first, line_second], take(2))
    greet(line_peers() + [((core_mate, shard), True), ((y_mate, shard), True)])
    normed[shard] = normed_ref[...]
    gather.start()
    gather.step(1)
    gather.step(2)
    for copy in loads:
        copy.wait()

    @pl.loop(0, N_Z)
    def _(i):
        @pl.when(i == 1)
        def _():
            gather.step(3)

        @pl.when(i == N_Z - 1)
        def _():
            for k in range(1, N_Z):
                scatter.start(k)

        origin = nearest(z, i)
        gather.wait_across(origin)
        pair = pl.ds(origin * N_X, N_X)
        left = normed[pair].reshape(N_X * rows, width)
        g_left = g_low[pair].reshape(N_X * rows, width)
        for first in range(0, size, size // 2):
            part, up_part = slice(first, first + size // 2), slice(size + first, size + first + size // 2)
            act, slope = gelu_parts(mm(left, weights[:, :, :, part].reshape(width, size // 2)))
            up = mm(left, weights[:, :, :, up_part].reshape(width, size // 2))
            g_hidden = mm_nt(g_left, down[part])
            hidden[origin, :, part] = (act * up).astype(BF16)
            grads[origin, :, part] = (g_hidden * up * slope).astype(BF16)
            grads[origin, :, up_part] = (g_hidden * act).astype(BF16)
        back = mm_nt(grads[origin], weights[...].reshape(width, 2 * size))
        parts[pair] = back.astype(BF16).reshape(N_X, rows, width)
        mixed_parts[pair] = mm(hidden[origin], down[...]).astype(BF16).reshape(N_X, rows, width)

    scatter.start(0)
    for i in range(N_Z):
        mixed_scatter.start(i)
    tile = normed.shape[2] // (N_Z * N_X)
    total = N_Z * N_X * rows

    @pl.loop(0, size // tile)
    def _(i):
        left = hidden[:, :, pl.ds(i * tile, tile)].reshape(total, tile)
        term = mm_tn(left, g_low[...].reshape(total, width)).astype(BF16)
        step = term_down.shape[2]
        for j in range(tile // step):
            chunk = i * (tile // step) + j
            term_down[chunk // term_down.shape[1], chunk % term_down.shape[1]] = term[j * step : (j + 1) * step]

    core_sum.start(0)

    def gu_terms(first, last):
        @pl.loop(first, last)
        def _(i):
            left = normed[:, :, pl.ds(i * tile, tile)].reshape(total, tile)
            term = mm_tn(left, grads[...].reshape(total, 2 * size)).astype(BF16)
            weights[i] = term.reshape(weights.shape[1:])

    gu_terms(0, middle_tile)
    core_sum.start(1)
    line_sum.start(0)
    gu_terms(middle_tile, 2 * middle_tile)
    core_sum.start(2)
    line_sum.start(1)
    scatter.step(0)
    line_sum.start(2)
    scatter.step(1)
    scatter.step(2)
    mixed_scatter.step(0)
    scatter.last(g_middle_ref)
    gain = jnp.concatenate([gains_ref[i] for i in range(N_Z * N_X)], axis=1)[1:2]
    back, gain_term = norm_backward(middle_ref[...], gain, g_middle_ref[...])
    g_middle_ref[...] = g_low[shard].astype(F32) + back
    gain_ref[...] = jnp.zeros_like(gain_ref)
    split_gains(gain_ref, 1, gain_term)
    mixed_scatter.step(1)
    mixed_scatter.step(2)
    outs = []
    for j, out in enumerate((quarter_down_out, quarter_gu_out.at[0:middle_tile], quarter_gu_out.at[middle_tile : 2 * middle_tile])):
        line_sum.add(j)
        outs.append(pltpu.make_async_copy(core_sum.mine(j, group // 2), out, out_sem.at[j]))
        outs[-1].start()
    mixed_scatter.last(result)
    _, live = positions_in_run([lengths_ref[0, i].astype(F32) for i in range(3)], rows)
    mixed_ref[...] = ((middle_ref[...] + result[...]) * live).astype(BF16)
    gather.finish()
    line_sum.finish()
    mixed_scatter.finish()
    scatter.finish()
    for copy in outs:
        copy.wait()


def mlp_call(lengths, normed, middle, gains, g_low, weights, down):
    rows, width = normed.shape
    shards, groups, quarter_rows, both = weights.shape
    size = down.shape[0]
    dma = pltpu.SemaphoreType.DMA
    shape = jax.ShapeDtypeStruct
    down_term = (size // groups // 64, 64, width)
    gu_term = (shards, quarter_rows, both)
    terms = [down_term] + [(shards // 2, quarter_rows, both)] * 2
    pairs = (N_Z, N_X * rows)
    scratch = [
        (shards, rows, width), (shards, rows, width), weights.shape, down.shape, pairs + (size,), pairs + (both,),
        (shards, rows, width), (shards, rows, width), (groups,) + down_term,
        *[(2,) + term for term in terms], *terms,
    ]
    return pl.pallas_call(
        mlp_kernel,
        out_shape=[
            shape(gu_term, BF16),
            shape(down_term, BF16),
            shape((rows, width), BF16),
            shape((rows, width), F32),
            shape(gains.shape, F32),
        ],
        in_specs=[pl.BlockSpec(memory_space=pltpu.SMEM)] + [vmem_spec()] * 3 + [any_spec()] * 3,
        out_specs=[any_spec()] * 2 + [vmem_spec()] * 3,
        scratch_shapes=[pltpu.VMEM(dims, BF16) for dims in scratch]
        + [pltpu.VMEM((rows, width), F32), dma((3,)), dma((3,))]
        + Gather.scratch()
        + FineScatter.scratch(rows, width)
        + FineScatter.scratch(rows, width)
        + CoreSum.scratch(3)
        + LineSum.scratch(3),
        compiler_params=pltpu.CompilerParams(collective_id=2, has_side_effects=True, vmem_limit_bytes=VMEM_LIMIT),
        name="mlp",
    )(lengths, normed, middle, gains, g_low, weights, down)


def mixer_backward(g_merged, saved, pos, vec, gates):
    gate, linear, rate_pre, input_pre, state = saved
    width = linear.shape[1]
    masks = [(pos >= k).astype(F32) for k in (1, 2, 3)]
    later = [roll_rows(jnp.broadcast_to(masks[k - 1], linear.shape), -k) for k in (1, 2, 3)]
    conv = conv_rows(linear, vec[0:4], vec[4:5], masks)
    input_gate = sigmoid(input_pre)
    decay = vec[7:8]
    rate, a, weight_in = decay_terms(rate_pre, decay)
    act, slope = gelu_parts(gate)
    g_gate = g_merged * state * slope
    lam = g_merged * act
    mult = roll_rows(a, -1) * later[0]
    step = 1
    while step < CAP:
        lam = lam + mult * roll_rows(lam, -step)
        if 2 * step < CAP:
            mult = mult * roll_rows(mult, -step)
        step *= 2
    g_a = lam * (roll_rows(state, 1) * masks[0])
    g_keep = g_a * a - lam * (input_gate * conv) * (a * a) / weight_in
    g_rate = (g_keep * (-RATE_SCALE * softplus_neg(decay)) * (rate * (1.0 - rate))).astype(BF16)
    g_decay = g_keep * (RATE_SCALE * rate) * sigmoid(-decay)
    flow = lam * weight_in
    g_inp = (flow * conv * (input_gate * (1.0 - input_gate))).astype(BF16)
    g_conv = flow * input_gate + mm(jnp.concatenate([g_rate, g_inp], axis=1), gates)
    g_linear = g_conv * vec[0:1]
    sums = [jnp.sum(g_conv * linear, axis=0, keepdims=True)]
    for k in (1, 2, 3):
        g_linear = g_linear + vec[k : k + 1] * (roll_rows(g_conv, -k) * later[k - 1])
        sums.append(jnp.sum(g_conv * (roll_rows(linear, k) * masks[k - 1]), axis=0, keepdims=True))
    for value in (g_conv, g_rate.astype(F32), g_inp.astype(F32), g_decay):
        sums.append(jnp.sum(value, axis=0, keepdims=True))
    return g_gate, g_linear, jnp.concatenate(sums, axis=0), conv.astype(BF16), g_rate, g_inp


def backward_kernel(
    lengths_ref, tokens_ref, g_middle_ref, gains_ref, gain_in_ref, vec_ref, gates_ref, out_proj_ref,
    quarter_gu_ref, quarter_down_ref, weights_ref, saved_ref, merged_ref, gathered_ref,
    grad_gate_out, grad_up_out, grad_down_out, gl_out, out_out, bd_out, grad_tokens_ref, small_out_ref,
    g_mix, normed, weights, saved, merged, grads, parts, term_gl, term_out, term_bd, total_bd, total_small, result,
    core_gl, core_out, core_bd, line_gl, line_out, line_bd,
    gain_terms, gains_got, packed, packs, *sems,
):
    sems = list(sems)

    def take(n):
        taken = tuple(sems[:n])
        del sems[:n]
        return taken

    group, shard, z, x = place()
    core_mate, y_mate = mates()
    shards = N_Z * N_X
    rows, width = tokens_ref.shape
    padded = vec_ref.shape[1]
    total = shards * rows
    chans = out_proj_ref.shape[0]
    half = quarter_gu_ref.shape[2] // 2
    quarter_rows = quarter_gu_ref.shape[1]
    load_sem, saved_sem, gain_send, gain_recv, pack_send, pack_recv = take(6)
    gather = Gather(g_mix, take(2))
    scatter = Scatter.of(parts, take(5))
    core_sum = CoreSum(
        [lambda q: term_gl.at[q], lambda q: term_out.at[q], lambda q: term_bd.at[q]], [core_gl, core_out, core_bd], take(2)
    )
    line_sum = LineSum(core_sum, [line_gl, line_out, line_bd], take(2))

    def columns(ref):
        return lambda origin, quarter: ref.at[pl.ds(quarter * quarter_rows, quarter_rows), pl.ds(origin * half, half)]

    gate_exchange = Exchange([lambda to: quarter_gu_ref.at[to, :, 0:half]], [columns(grad_gate_out)], shards, take(4))
    up_exchange = Exchange([lambda to: quarter_gu_ref.at[to, :, half : 2 * half]], [columns(grad_up_out)], shards, take(4))
    down_exchange = Exchange([lambda to: quarter_down_ref], [lambda origin, quarter: grad_down_out.at[quarter]], 1, take(4))
    gl_exchange = Exchange(
        [lambda to: term_gl.at[group, to]], [lambda origin, quarter: gl_out.at[origin, quarter]], shards, take(4)
    )
    out_exchange = Exchange([lambda to: term_out.at[group]], [lambda origin, quarter: out_out.at[quarter]], 1, take(4))
    bd_exchange = Exchange([lambda to: term_bd.at[group]], [lambda origin, quarter: bd_out.at[quarter]], 1, take(4))

    def gain_copy(to, origin):
        return pltpu.make_async_remote_copy(
            src_ref=gain_terms.at[to], dst_ref=gains_got.at[origin], send_sem=gain_send.at[to], recv_sem=gain_recv.at[origin],
            device_id=(group, to), device_id_type=MESH_ID,
        )

    def pack_copy(i):
        return pltpu.make_async_remote_copy(
            src_ref=packed, dst_ref=packs.at[i], send_sem=pack_send.at[i], recv_sem=pack_recv.at[i],
            device_id=((core_mate, y_mate, 3 - group)[i], shard), device_id_type=MESH_ID,
        )

    def saved_copy(i):
        return pltpu.make_async_copy(saved_ref.at[nearest(z, i)], saved.at[i % 2], saved_sem.at[i % 2])

    loads = [
        pltpu.make_async_copy(source, target, load_sem.at[i])
        for i, (source, target) in enumerate((
            (weights_ref, weights), (gathered_ref, normed), (merged_ref, merged),
        ))
    ]
    for copy in loads:
        copy.start()
    saved_copy(0).start()
    greet(all_peers() + [((3 - group, shard), True)])
    g_mix[shard] = g_middle_ref[...].astype(BF16)
    gather.start()
    down_exchange.start()
    down_exchange.spread()
    total_small[...] = jnp.zeros_like(total_small)
    total_bd[...] = jnp.zeros_like(total_bd)
    gather.step(1)
    gather.step(2)
    for copy in loads:
        copy.wait()

    @pl.loop(0, N_Z)
    def _(i):
        @pl.when(i == 1)
        def _():
            gather.step(3)
            gate_exchange.start()
            up_exchange.start()

        @pl.when(i == 3)
        def _():
            gate_exchange.spread()

        origin = nearest(z, i)
        gather.wait_across(origin)
        saved_copy(i).wait()

        @pl.when(i < N_Z - 1)
        def _():
            saved_copy(i + 1).start()

        pair = pl.ds(origin * N_X, N_X)
        g_merged = mm_nt(g_mix[pair].reshape(N_X * rows, width), out_proj_ref[...])
        g_merged = jnp.concatenate([g_merged, jnp.zeros((N_X * rows, padded - chans), F32)], axis=1)
        where = pair_positions(gains_ref, origin, rows)
        g_gate, g_linear, sums, low, g_rate, g_inp = mixer_backward(
            g_merged, [saved[i % 2, j] for j in range(5)], where, vec_ref[...], gates_ref[...]
        )
        grads[origin] = jnp.concatenate([g_gate[:, :chans], g_linear[:, :chans]], axis=1).astype(BF16)
        total_small[...] += sums
        total_bd[0] += mm_tn(g_rate, low)
        total_bd[1] += mm_tn(g_inp, low)
        back = mm_nt(grads[origin], weights[...].reshape(width, 2 * chans))
        parts[pair] = back.astype(BF16).reshape(N_X, rows, width)

    for i in range(N_Z):
        scatter.start(i)
    tile = width // shards

    @pl.loop(0, shards)
    def _(i):
        left = normed[:, :, pl.ds(i * tile, tile)].reshape(total, tile)
        term = mm_tn(left, grads[...].reshape(total, 2 * chans)).astype(BF16)
        term_gl[:, i] = term.reshape(term_gl.shape[0], term_gl.shape[2], 2 * chans)

    core_sum.start(0)
    up_exchange.spread()
    scatter.step(0)
    term = mm_tn(merged[...].reshape(total, padded), g_mix[...].reshape(total, width))
    term_out[...] = term[:chans].astype(BF16).reshape(term_out.shape)
    size = term_bd.shape[0] * term_bd.shape[1] * term_bd.shape[2] // 2
    both = []
    for i in range(2):
        heads = [slice(h * size, (h + 1) * size) for h in range(chans // size)]
        both.append(jnp.concatenate([total_bd[i, part, part] for part in heads], axis=1))
    term_bd[...] = jnp.concatenate(both, axis=0).astype(BF16).reshape(term_bd.shape)
    core_sum.start(1)
    core_sum.start(2)
    for j in range(3):
        line_sum.start(j)
    scatter.step(1)
    scatter.step(2)
    scatter.last(result)
    _, live = positions_in_run([lengths_ref[0, i].astype(F32) for i in range(3)], rows)
    masked = tokens_ref[...].astype(F32) * live
    gain = jnp.concatenate([gains_ref[i] for i in range(shards)], axis=1)[0:1]
    back, gain_term = norm_backward(masked, gain, result[...])
    grad_tokens_ref[...] = ((g_middle_ref[...] + back) * live).astype(BF16)
    gain_terms[...] = gain_in_ref[...]
    split_gains(gain_terms, 0, gain_term)
    for i in range(1, shards):
        gain_copy((shard + i) % shards, shard).start()
    line_sum.add(0)
    gl_exchange.start()
    for j, one in ((1, out_exchange), (2, bd_exchange)):
        line_sum.add(j)
        one.start()
        one.spread()
    gl_exchange.spread()
    down_exchange.relay()
    gate_exchange.relay()
    up_exchange.relay()
    gain_sum = gain_terms[shard]
    for i in range(1, shards):
        origin = (shard + i) % shards
        gain_copy(origin, origin).wait_recv()
        gain_sum = gain_sum + gains_got[origin]
    packed[0:8] = total_small[...]
    packed[8:16] = jnp.concatenate([gain_sum, jnp.zeros((8, padded - gain_sum.shape[1]), F32)], axis=1)
    for i in range(3):
        pack_copy(i).start()
    packs_sum = packed[...]
    for i in range(3):
        pack_copy(i).wait_recv()
        packs_sum = packs_sum + packs[i]
    small_out_ref[...] = packs_sum
    for one in (out_exchange, bd_exchange, gl_exchange):
        one.relay()
    for i in range(1, shards):
        gain_copy((shard + i) % shards, shard).wait_send()
    for i in range(3):
        pack_copy(i).wait_send()
    for one in (gather, scatter, line_sum):
        one.finish()
    for one in (down_exchange, gate_exchange, up_exchange, out_exchange, bd_exchange, gl_exchange):
        one.arrive()
        one.finish()


def backward_call(
    head, lengths, tokens, g_middle, gains, gain_terms, vec, gates, out_proj, quarter_gu, quarter_down, weights, saved, merged,
    gathered,
):
    rows, width = tokens.shape
    shards, groups = N_Z * N_X, weights.shape[1]
    quarter_rows, both = quarter_gu.shape[1:]
    padded = vec.shape[1]
    chans = out_proj.shape[0]
    dma = pltpu.SemaphoreType.DMA
    shape = jax.ShapeDtypeStruct
    terms = [
        (groups, shards, quarter_rows, 2 * chans),
        (groups, chans // groups // 16, 16, width),
        (groups, 2 * head // groups // 16, 16, chans),
    ]
    packed = (16, padded)
    scratch = [
        ((shards, rows, width), BF16), (gathered.shape, BF16), (weights.shape, BF16), ((2,) + saved.shape[1:], F32),
        (merged.shape, BF16), ((N_Z, N_X * rows, 2 * chans), BF16), ((shards, rows, width), BF16),
        *[(term, BF16) for term in terms], ((2, padded, padded), F32), (vec.shape, F32), ((rows, width), F32),
        *[((2,) + term[1:], BF16) for term in terms], *[(term[1:], BF16) for term in terms],
        (gains.shape, F32), (gains.shape, F32), (packed, F32), ((3,) + packed, F32),
    ]
    return pl.pallas_call(
        backward_kernel,
        out_shape=[
            shape((groups * quarter_rows, shards * both // 2), BF16),
            shape((groups * quarter_rows, shards * both // 2), BF16),
            shape((groups,) + quarter_down.shape, BF16),
            shape((shards, groups) + terms[0][2:], BF16),
            shape(terms[1], BF16),
            shape(terms[2], BF16),
            shape((rows, width), BF16),
            shape(packed, F32),
        ],
        in_specs=[pl.BlockSpec(memory_space=pltpu.SMEM)] + [vmem_spec()] * 7 + [any_spec()] * 6,
        out_specs=[any_spec()] * 6 + [vmem_spec()] * 2,
        scratch_shapes=[pltpu.VMEM(dims, kind) for dims, kind in scratch]
        + [dma((3,)), dma((2,)), dma((shards,)), dma((shards,)), dma((3,)), dma((3,))]
        + Gather.scratch()
        + Scatter.scratch(rows, width)
        + CoreSum.scratch(3)
        + LineSum.scratch(3)
        + Exchange.scratch(shards, 1)
        + Exchange.scratch(shards, 1)
        + Exchange.scratch(1, 1)
        + Exchange.scratch(shards, 1)
        + Exchange.scratch(1, 1) * 2,
        compiler_params=pltpu.CompilerParams(collective_id=3, has_side_effects=True, vmem_limit_bytes=VMEM_LIMIT),
        name="mixer_backward",
    )(
        lengths, tokens, g_middle, gains, gain_terms, vec, gates, out_proj, quarter_gu, quarter_down, weights, saved, merged,
        gathered,
    )


def widen_kernel(
    mixed_ref, tokens_ref, small_ref, gate_ref, up_ref, down_ref, gl_ref, out_ref, bd_ref,
    mixed_out, tokens_out, gain1_out, gate_in_out, linear_in_out, kernel_out, bias_out, rate_out, rate_bias_out, input_out,
    input_bias_out, decay_out, out_out, gain2_out, gate_out, up_out, down_out,
):
    mixed_out[...] = mixed_ref[...]
    tokens_out[...] = tokens_ref[...]
    for out, ref in ((gate_out, gate_ref), (up_out, up_ref), (down_out, down_ref), (out_out, out_ref)):
        out[...] = ref[...].astype(F32)
    shards = gl_ref.shape[0]
    chans = gl_ref.shape[3] // 2
    for out, first in ((gate_in_out, 0), (linear_in_out, chans)):
        for s in range(shards):
            out[:, s * chans : (s + 1) * chans] = gl_ref[s, 0, :, first : first + chans].astype(F32)

    @pl.when(pl.program_id(0) == 0)
    def _():
        size = rate_out.shape[0]
        rate_out[...] = bd_ref[:size].astype(F32)
        input_out[...] = bd_ref[size:].astype(F32)
        kernel_out[...] = small_ref[0:4, :chans]
        for i, out in ((4, bias_out), (5, rate_bias_out), (6, input_bias_out), (7, decay_out), (8, gain1_out), (9, gain2_out)):
            out[...] = small_ref[i, : out.shape[0]]


def widen_call(mixed, grad_tokens, small, gate, up, down, gl, out, bd, gain_size):
    shards, groups, quarter_rows, both = gl.shape
    chans = out.shape[0]

    def rows_of(dims):
        return pl.BlockSpec((dims[0] // groups, dims[1]), lambda i: (i, 0))

    def whole(dims):
        return pl.BlockSpec(dims, lambda i: (0,) * len(dims))

    wide = (groups * quarter_rows, shards * chans)
    block = (bd.shape[0] // 2, bd.shape[1])
    shapes = [
        mixed.shape, grad_tokens.shape, (gain_size,), wide, wide, (4, chans), (chans,), block, (chans,), block, (chans,), (chans,),
        out.shape, (gain_size,), gate.shape, up.shape, down.shape,
    ]
    specs = [whole(dims) if len(dims) == 1 or dims in ((4, chans), block) else rows_of(dims) for dims in shapes]
    return pl.pallas_call(
        widen_kernel,
        grid=(groups,),
        in_specs=[rows_of(mixed.shape), rows_of(grad_tokens.shape), whole(small.shape)]
        + [rows_of(a.shape) for a in (gate, up, down)]
        + [pl.BlockSpec((shards, 1, quarter_rows, both), lambda i: (0, i, 0, 0)), rows_of(out.shape), whole(bd.shape)],
        out_specs=specs,
        out_shape=[jax.ShapeDtypeStruct(dims, BF16 if i < 2 else F32) for i, dims in enumerate(shapes)],
        compiler_params=pltpu.CompilerParams(vmem_limit_bytes=VMEM_LIMIT),
        name="widen",
    )(mixed, grad_tokens, small, gate, up, down, gl, out, bd)


def per_device_split(
    tokens, lengths, cotangent, norm1_gain, gate_in, linear_in, conv_kernel, conv_bias, rate_weight,
    rate_bias, input_weight, input_bias, decay_param, out_proj, norm2_gain, mlp_gate, mlp_up, mlp_down,
):
    chans, size = rate_weight.shape
    gathered, weights, mlp_weights, gains, saved, merged, middle, normed_two, vec, gates, g_low = forward_call(
        lengths, tokens, cotangent,
        (norm1_gain, norm2_gain, conv_kernel, conv_bias, rate_bias, input_bias, decay_param, rate_weight.T, input_weight.T),
        out_proj, gate_in, linear_in, mlp_gate, mlp_up,
    )
    quarter_gu, quarter_down, mixed, g_middle, gain_terms = mlp_call(
        lengths, normed_two, middle, gains, g_low, mlp_weights, mlp_down
    )
    grad_gate, grad_up, grad_down, gl, grad_out, bd, grad_tokens, small = backward_call(
        size, lengths, tokens, g_middle, gains, gain_terms, vec, gates, out_proj, quarter_gu, quarter_down, weights, saved, merged,
        gathered,
    )
    outs = list(widen_call(
        mixed, grad_tokens, small, grad_gate, grad_up, grad_down.reshape(mlp_down.shape), gl, grad_out.reshape(out_proj.shape),
        bd.reshape(2 * size, chans), norm1_gain.shape[0],
    ))
    for i in (7, 9):
        outs[i] = outs[i].T
    return tuple(outs)


def as_sent(shard):
    return jax.tree.map(lambda a: a.astype(jnp.bfloat16) if a.dtype == jnp.float32 else a, shard)


def layout(counts, row_count):
    first = counts[0]
    second = first + counts[1]
    run_ends = jnp.stack([first, second, second + counts[2], second + counts[2] + counts[3]])
    positions = jnp.arange(row_count, dtype=jnp.int32)
    segment_ids = jnp.sum((positions[:, None] >= run_ends[None, :-1]).astype(jnp.int32), axis=1)
    live_rows = (positions < run_ends[-2]).astype(jnp.float32)
    return (segment_ids, live_rows)


def earlier_ids(segment_ids, offset):
    filler = jnp.full((offset,), -1, dtype=jnp.int32)
    return jnp.concatenate([filler, segment_ids[:-offset]])


def normalize(values, gain_vec):
    scale = lax.rsqrt(jnp.mean(values * values, axis=1, keepdims=True) + EPSILON)
    return values * scale * gain_vec


def convolve(linear_out, kernel, shift_vec, segment_ids):
    summed = linear_out * kernel[0] + shift_vec
    for offset in range(1, kernel.shape[0]):
        shifted = jnp.concatenate(
            [jnp.zeros((offset, linear_out.shape[1]), linear_out.dtype), linear_out[:-offset]],
            axis=0,
        )
        same_seq = (earlier_ids(segment_ids, offset) == segment_ids).astype(linear_out.dtype)
        summed = summed + kernel[offset] * shifted * same_seq[:, None]
    return summed


def combine_pairs(earlier_pair, later_pair):
    return (earlier_pair[0] * later_pair[0], later_pair[0] * earlier_pair[1] + later_pair[1])


def recurrence(rate_pre, input_pre, inflow, decay_vec, segment_ids):
    rate_gate = jax.nn.sigmoid(rate_pre)
    opened = jax.nn.sigmoid(input_pre)
    log_keep = -RATE_SCALE * rate_gate * jax.nn.softplus(-decay_vec)
    factor = jnp.exp(log_keep)
    weight_in = jnp.sqrt(-jnp.expm1(2.0 * log_keep))
    same_run = (earlier_ids(segment_ids, 1) == segment_ids).astype(factor.dtype)
    carried, states = lax.associative_scan(
        combine_pairs, (factor * same_run[:, None], weight_in * opened * inflow), axis=0
    )
    return states


def gated_gelu(gate_vals, up_vals):
    return jax.nn.gelu(gate_vals) * up_vals


def product(left, right):
    return jnp.dot(left, right, preferred_element_type=jnp.float32)


def contract(left, right):
    return jnp.einsum("ti,tj->ij", left, right, preferred_element_type=jnp.float32)


def back_dot(grad_vals, weight):
    return jnp.einsum("tj,ij->ti", grad_vals, weight, preferred_element_type=jnp.float32)


def blocked(values, weight):
    row_count = values.shape[0]
    size = weight.shape[1]
    heads = weight.shape[0] // size
    return jnp.einsum(
        "thj,hjk->thk",
        values.reshape(row_count, heads, size),
        weight.reshape(heads, size, size),
        preferred_element_type=jnp.float32,
    ).reshape(row_count, heads * size)


def block_terms(values, grad_vals, size):
    row_count = values.shape[0]
    heads = values.shape[1] // size
    terms = jnp.einsum(
        "thj,thk->hjk",
        values.reshape(row_count, heads, size),
        grad_vals.reshape(row_count, heads, size),
        preferred_element_type=jnp.float32,
    )
    return terms.reshape(heads * size, size)


def block_back(grad_vals, weight):
    row_count = grad_vals.shape[0]
    size = weight.shape[1]
    heads = weight.shape[0] // size
    return jnp.einsum(
        "thk,hjk->thj",
        grad_vals.reshape(row_count, heads, size),
        weight.reshape(heads, size, size),
        preferred_element_type=jnp.float32,
    ).reshape(row_count, heads * size)


def per_device_general(
    tokens,
    lengths,
    cotangent,
    norm1_gain,
    gate_in,
    linear_in,
    conv_kernel,
    conv_bias,
    rate_weight,
    rate_bias,
    input_weight,
    input_bias,
    decay_param,
    out_proj,
    norm2_gain,
    mlp_gate,
    mlp_up,
    mlp_down,
):
    row_count = tokens.shape[0]
    segment_ids, live_rows = layout(lengths[0], row_count)
    live_col = live_rows[:, None]
    mixer_full = (
        lax.all_gather(norm1_gain, "shard", axis=0, tiled=True),
        lax.all_gather(gate_in, "shard", axis=0, tiled=True),
        lax.all_gather(linear_in, "shard", axis=0, tiled=True),
        lax.all_gather(conv_kernel, "shard", axis=1, tiled=True),
        lax.all_gather(conv_bias, "shard", axis=0, tiled=True),
        lax.all_gather(rate_weight, "shard", axis=0, tiled=True),
        lax.all_gather(rate_bias, "shard", axis=0, tiled=True),
        lax.all_gather(input_weight, "shard", axis=0, tiled=True),
        lax.all_gather(input_bias, "shard", axis=0, tiled=True),
        lax.all_gather(decay_param, "shard", axis=0, tiled=True),
        lax.all_gather(out_proj, "shard", axis=0, tiled=True),
    )
    gain_first = mixer_full[0].astype(jnp.float32)
    kernel_full = mixer_full[3].astype(jnp.float32)
    kernel_shift = mixer_full[4].astype(jnp.float32)
    rate_shift = mixer_full[6].astype(jnp.float32)
    input_shift = mixer_full[8].astype(jnp.float32)
    decay_full = mixer_full[9].astype(jnp.float32)
    block_size = mixer_full[5].shape[1]
    masked_in = tokens.astype(jnp.float32) * live_col
    normed_low = normalize(masked_in, gain_first).astype(jnp.bfloat16)
    gate_pre = product(normed_low, mixer_full[1])
    linear_out = product(normed_low, mixer_full[2])
    gate_act = jax.nn.gelu(gate_pre)
    conv_out = convolve(linear_out, kernel_full, kernel_shift, segment_ids)
    conv_low = conv_out.astype(jnp.bfloat16)
    rate_pre = blocked(conv_low, mixer_full[5]) + rate_shift
    input_pre = blocked(conv_low, mixer_full[7]) + input_shift
    states = recurrence(rate_pre, input_pre, conv_out, decay_full, segment_ids)
    merged_low = (gate_act * states).astype(jnp.bfloat16)
    middle = masked_in + product(merged_low, mixer_full[10])
    mlp_full = (
        lax.all_gather(norm2_gain, "shard", axis=0, tiled=True),
        lax.all_gather(mlp_gate, "shard", axis=0, tiled=True),
        lax.all_gather(mlp_up, "shard", axis=0, tiled=True),
        lax.all_gather(mlp_down, "shard", axis=0, tiled=True),
    )
    gain_second = mlp_full[0].astype(jnp.float32)
    normed_two = normalize(middle, gain_second).astype(jnp.bfloat16)
    gate_mlp = product(normed_two, mlp_full[1])
    up_mlp = product(normed_two, mlp_full[2])
    hidden_low = gated_gelu(gate_mlp, up_mlp).astype(jnp.bfloat16)
    mixed_out = ((middle + product(hidden_low, mlp_full[3])) * live_col).astype(jnp.bfloat16)
    grad_out = cotangent.astype(jnp.float32) * live_col
    grad_down = grad_out.astype(jnp.bfloat16)
    again_mlp = (
        lax.all_gather(mlp_gate, "shard", axis=0, tiled=True),
        lax.all_gather(mlp_up, "shard", axis=0, tiled=True),
        lax.all_gather(mlp_down, "shard", axis=0, tiled=True),
    )
    term_down = contract(hidden_low, grad_down)
    part_down = lax.psum_scatter(
        term_down.astype(jnp.bfloat16), "shard", scatter_dimension=0, tiled=True
    ).astype(jnp.float32)
    grad_hidden = back_dot(grad_down, again_mlp[2])
    unused_val, hidden_back = jax.vjp(gated_gelu, gate_mlp, up_mlp)
    grad_gate_mlp, grad_up_mlp = hidden_back(grad_hidden)
    gate_mlp_low = grad_gate_mlp.astype(jnp.bfloat16)
    up_mlp_low = grad_up_mlp.astype(jnp.bfloat16)
    term_gate_mlp = contract(normed_two, gate_mlp_low)
    term_up_mlp = contract(normed_two, up_mlp_low)
    grad_normed_two = back_dot(gate_mlp_low, again_mlp[0]) + back_dot(up_mlp_low, again_mlp[1])
    unused_two, second_back = jax.vjp(normalize, middle, gain_second)
    grad_middle_norm, term_gain_two = second_back(grad_normed_two)
    parts_mlp = (
        lax.psum_scatter(
            term_gain_two.astype(jnp.bfloat16), "shard", scatter_dimension=0, tiled=True
        ).astype(jnp.float32),
        lax.psum_scatter(
            term_gate_mlp.astype(jnp.bfloat16), "shard", scatter_dimension=0, tiled=True
        ).astype(jnp.float32),
        lax.psum_scatter(
            term_up_mlp.astype(jnp.bfloat16), "shard", scatter_dimension=0, tiled=True
        ).astype(jnp.float32),
    )
    grad_middle = grad_out + grad_middle_norm
    grad_mix_low = grad_middle.astype(jnp.bfloat16)
    again_mixer = (
        lax.all_gather(gate_in, "shard", axis=0, tiled=True),
        lax.all_gather(linear_in, "shard", axis=0, tiled=True),
        lax.all_gather(rate_weight, "shard", axis=0, tiled=True),
        lax.all_gather(input_weight, "shard", axis=0, tiled=True),
        lax.all_gather(out_proj, "shard", axis=0, tiled=True),
    )
    term_out = contract(merged_low, grad_mix_low)
    grad_merged = back_dot(grad_mix_low, again_mixer[4])
    grad_states = grad_merged * gate_act
    unused_three, gelu_back = jax.vjp(jax.nn.gelu, gate_pre)
    gate_low = gelu_back(grad_merged * states)[0].astype(jnp.bfloat16)
    unused_four, scan_back = jax.vjp(
        partial(recurrence, segment_ids=segment_ids), rate_pre, input_pre, conv_out, decay_full
    )
    grad_rate, grad_input, grad_flow, term_decay = scan_back(grad_states)
    rate_low = grad_rate.astype(jnp.bfloat16)
    input_low = grad_input.astype(jnp.bfloat16)
    term_rate = block_terms(conv_low, rate_low, block_size)
    term_input = block_terms(conv_low, input_low, block_size)
    term_rate_shift = jnp.sum(rate_low.astype(jnp.float32), axis=0)
    term_input_shift = jnp.sum(input_low.astype(jnp.float32), axis=0)
    grad_conv = (
        grad_flow + block_back(rate_low, again_mixer[2]) + block_back(input_low, again_mixer[3])
    )
    unused_five, conv_back = jax.vjp(
        partial(convolve, segment_ids=segment_ids), linear_out, kernel_full, kernel_shift
    )
    grad_linear, term_kernel, term_kernel_shift = conv_back(grad_conv)
    linear_low = grad_linear.astype(jnp.bfloat16)
    term_gate_in = contract(normed_low, gate_low)
    term_linear = contract(normed_low, linear_low)
    grad_normed = back_dot(gate_low, again_mixer[0]) + back_dot(linear_low, again_mixer[1])
    unused_six, first_back = jax.vjp(normalize, masked_in, gain_first)
    grad_masked, term_gain_one = first_back(grad_normed)
    grad_tokens = ((grad_middle + grad_masked) * live_col).astype(jnp.bfloat16)
    small_terms = (
        term_gain_one,
        term_kernel,
        term_kernel_shift,
        term_rate,
        term_rate_shift,
        term_input,
        term_input_shift,
        term_decay,
    )
    placed = tuple((term for term in small_terms))
    mixer_terms = (
        placed[0],
        term_gate_in,
        term_linear,
        placed[1],
        placed[2],
        placed[3],
        placed[4],
        placed[5],
        placed[6],
        placed[7],
        term_out,
    )
    parts_mixer = (
        lax.psum_scatter(
            mixer_terms[0].astype(jnp.bfloat16), "shard", scatter_dimension=0, tiled=True
        ).astype(jnp.float32),
        lax.psum_scatter(
            mixer_terms[1].astype(jnp.bfloat16), "shard", scatter_dimension=0, tiled=True
        ).astype(jnp.float32),
        lax.psum_scatter(
            mixer_terms[2].astype(jnp.bfloat16), "shard", scatter_dimension=0, tiled=True
        ).astype(jnp.float32),
        lax.psum_scatter(
            mixer_terms[3].astype(jnp.bfloat16), "shard", scatter_dimension=1, tiled=True
        ).astype(jnp.float32),
        lax.psum_scatter(
            mixer_terms[4].astype(jnp.bfloat16), "shard", scatter_dimension=0, tiled=True
        ).astype(jnp.float32),
        lax.psum_scatter(
            mixer_terms[5].astype(jnp.bfloat16), "shard", scatter_dimension=0, tiled=True
        ).astype(jnp.float32),
        lax.psum_scatter(
            mixer_terms[6].astype(jnp.bfloat16), "shard", scatter_dimension=0, tiled=True
        ).astype(jnp.float32),
        lax.psum_scatter(
            mixer_terms[7].astype(jnp.bfloat16), "shard", scatter_dimension=0, tiled=True
        ).astype(jnp.float32),
        lax.psum_scatter(
            mixer_terms[8].astype(jnp.bfloat16), "shard", scatter_dimension=0, tiled=True
        ).astype(jnp.float32),
        lax.psum_scatter(
            mixer_terms[9].astype(jnp.bfloat16), "shard", scatter_dimension=0, tiled=True
        ).astype(jnp.float32),
        lax.psum_scatter(
            mixer_terms[10].astype(jnp.bfloat16), "shard", scatter_dimension=0, tiled=True
        ).astype(jnp.float32),
    )
    shard_parts = tuple(parts_mixer) + (parts_mlp[0], parts_mlp[1], parts_mlp[2], part_down)
    totals = jax.tree.map(
        lambda part: part.astype(jnp.float32), lax.psum(as_sent(shard_parts), "group")
    )
    return (mixed_out, grad_tokens) + tuple(totals)


def solution(mesh):
    placed = (
        P(("group", "shard"), None),
        P(("group", "shard"), None),
        P(("group", "shard"), None),
        P("shard"),
        P("shard", None),
        P("shard", None),
        P(None, "shard"),
        P("shard"),
        P("shard", None),
        P("shard"),
        P("shard", None),
        P("shard"),
        P("shard"),
        P("shard", None),
        P("shard"),
        P("shard", None),
        P("shard", None),
        P("shard", None),
    )
    split_fits = FAST_MESH == tuple(mesh.shape[axis] for axis in ("group", "shard"))
    return jax.shard_map(
        per_device_split if split_fits else per_device_general,
        mesh=mesh,
        in_specs=placed,
        out_specs=(
            P(("group", "shard"), None),
            P(("group", "shard"), None),
            P("shard"),
            P("shard", None),
            P("shard", None),
            P(None, "shard"),
            P("shard"),
            P("shard", None),
            P("shard"),
            P("shard", None),
            P("shard"),
            P("shard"),
            P("shard", None),
            P("shard"),
            P("shard", None),
            P("shard", None),
            P("shard", None),
        ),
        check_vma=False,
    )
```
